32 devices in a mesh: bx: 8 (over z, y), by: 4 (over x, core).
Axes of the slice: x: 2, y: 2, z: 4, core: 2. Of those that a mesh axis runs over, the one named last changes fastest.
Arguments:
- normals: float32 [3, 131072], P(None, ('bx', 'by')), may hold values from -60 to 60
- owners: int32 [131072, 1], P(('bx', 'by')), may hold values from 0 to 31; in each aligned block of 4096 rows (0 to 4095, 4096 to 8191, ...) at most 256 rows name the same one
- cells: int32 [131072], P(('bx', 'by')), may hold values from 0 to 262143
- levels: int32 [8, 4], P('bx', 'by'), may hold values from 0 to 3
- rows_inverse: float32 [128, 128], replicated, may hold values from 0 to 0.25
- columns_inverse: float32 [256, 256], replicated, may hold values from 0 to 0.25
- depth_inverse: float32 [256, 256], replicated, may hold values from 0 to 0.25
Outputs:
- iterate: float32 [128, 256, 256], P('bx', 'by')
- implicit: float32 [131072], P(('bx', 'by'))
The draws below stay inside these ranges and needn't reach their ends.
Inputs may be any that keep to these rules, and one draw needn't show every extreme that they name: `owners`: A brick's number is its index along bx times the number of devices along by plus its index along by. Among the 4096 points of one device at most 256 name one brick, and in every draw some brick is named by exactly 256 of them.
All inputs are finite; a program needn't handle non-finite values.
Results may differ from the reference program's by a relative error of at most 0.0001.
Values sent between devices are 32-bit elements; how exact they have to be, the bound alone decides.
No kernel may reach another device: no remote copies, remote signals or barrier semaphores. Data moves between devices by JAX's collectives and lax.ppermute only.
A program may use at most 320 MiB of HBM per device.

```python
import math
import jax
import jax.numpy as jnp
import numpy as np
from jax import lax

CX = 16
CY = 64
NZ = 256
P_DEV = 4096
ITERS = 4
CAP = 256
NX = 128
NY = 256
POINTS = 131072
N_BX = 8
N_BY = 4


def line_matrix(key, order):
    index = jnp.arange(order)
    distance = jnp.abs(index[:, None] - index[None, :]).astype(jnp.float32)
    strength = jax.random.uniform(jax.random.fold_in(key, 3), (), jnp.float32, 2.0, 3.5)
    spread = order * jax.random.uniform(jax.random.fold_in(key, 4), (), jnp.float32, 0.125, 0.5)
    factors = jnp.exp(jax.random.uniform(jax.random.fold_in(key, 1), (order, order), jnp.float32, math.log(0.1), math.log(3.0)))
    kernel = 0.25 * strength / spread * jnp.exp(-distance / spread) * factors
    diagonal = jax.random.uniform(jax.random.fold_in(key, 2), (order,), jnp.float32, 0.4, 0.8)
    return 0.1 * (jnp.diag(diagonal) + kernel)


def draw_rows_inverse(key, part):
    return line_matrix(jax.random.fold_in(key, 11), NX)


def draw_columns_inverse(key, part):
    return line_matrix(jax.random.fold_in(key, 12), NY)


def draw_depth_inverse(key, part):
    return line_matrix(jax.random.fold_in(key, 13), NZ)


def set_ends(drawn, rng, smallest, top_value):
    index_at = [jax.random.randint(jax.random.fold_in(rng, axis), (), 0, length) for axis, length in enumerate(drawn.shape)]
    longest = drawn.shape.index(max(drawn.shape))
    neighbour = index_at[:longest] + [(index_at[longest] + 1) % drawn.shape[longest]] + index_at[longest + 1:]
    return drawn.at[tuple(index_at)].set(smallest).at[tuple(neighbour)].set(top_value)


def block_scale(stream_key, shape, cuts, smallest, top_value):
    loudness, own = 1.0, jax.random.fold_in(stream_key, 6)
    for axis_at, shards_of in cuts:
        steps = jnp.exp(jax.random.uniform(jax.random.fold_in(own, axis_at), (shards_of,), jnp.float32, smallest / len(cuts), top_value / len(cuts)))
        loudness = loudness * jnp.repeat(steps, shape[axis_at] // shards_of).reshape([-1 if axis == axis_at else 1 for axis in range(len(shape))])
    return loudness


def shared_out(key, own, number, rows, count, top, limit, slope):
    order = jax.random.permutation(key, count)
    crowded, common = shares(count, rows * top, limit, slope, True), shares(count, rows * top, limit, slope, False)
    places = jnp.arange(count)

    def named(tallies, rotation):
        used = int((tallies > 0).sum())
        fixed = max(1, used // 4)
        shifted = fixed + (places - fixed + rotation * (used - fixed)) % max(1, count - fixed)
        return jnp.zeros((count,), jnp.int32).at[order[jnp.where(places < fixed, places, shifted)]].set(jnp.asarray(tallies, jnp.int32))

    tallies = jnp.where(number % 4 == 0, named(crowded, number // 4), named(common, number - number // 4 - 1))
    mixed = jax.random.permutation(jax.random.fold_in(own, 3), count)
    giver, sink = mixed[0:count // 2 * 2:2], mixed[1:count // 2 * 2:2]
    room = jnp.minimum(tallies[giver] - 1, limit - tallies[sink]) // 2
    room = jnp.where((giver == order[0]) | (sink == order[0]) | (tallies[sink] == 0), 0, jnp.maximum(room, 0))
    shifted = jax.random.randint(jax.random.fold_in(own, 4), (count // 2,), 0, 1 << 20) % (room + 1)
    tallies = tallies.at[giver].add(-shifted).at[sink].add(shifted)
    items = jnp.searchsorted(jnp.cumsum(tallies), jnp.arange(rows * top), side="right").astype(jnp.int32)
    listing = items.reshape(top, rows).T
    listing = listing[jax.random.permutation(jax.random.fold_in(own, 1), rows)]
    rotation = jax.random.randint(jax.random.fold_in(own, 2), (rows, 1), 0, top)
    return jnp.take_along_axis(listing, (jnp.arange(top)[None, :] + rotation) % top, axis=1)


def shares(amount, total, bound, slope, full):
    loads = [(1 << 20) // math.isqrt(grade ** slope) + 1 for grade in range(1, amount + 1)]
    largest = bound if full else min(bound, max(-(-total // amount), total * loads[0] // sum(loads)))
    least = 1 if total - largest >= amount - 1 else 0
    given, spare = [largest] + [least] * (amount - 1), total - largest - least * (amount - 1)
    while spare > 0:
        movable = [i for i in range(1, amount) if given[i] < largest] or [i for i in range(1, amount) if given[i] < bound]
        whole, left = sum([loads[i] for i in movable]), spare
        for i in movable:
            addition = min(bound - given[i], max(1, left * loads[i] // whole), spare)
            given[i] = given[i] + addition
            spare = spare - addition
    return np.array(given)


def scatter_about(own_key, dims, scale, most, split=(), held_as=jnp.bfloat16):
    level = block_scale(own_key, dims, split, -0.22, 0.18) if split else 1.0
    entries = jax.random.normal(own_key, dims, jnp.float32) * scale * level
    return jnp.minimum(jnp.maximum(entries, -most), most).astype(held_as)


def setup_inputs(seed: int = 0) -> dict:
    key_list = jax.random.split(jax.random.key(seed), 8)
    normals = scatter_about(key_list[0], (3, POINTS), 10.0, 60.0, ((1, 32),), jnp.float32)
    owners_keys = jax.random.split(jax.random.fold_in(key_list[1], 1), POINTS // P_DEV)
    owners_turns = jax.random.permutation(jax.random.fold_in(key_list[1], 3), POINTS // P_DEV)
    owners = jax.vmap(lambda own, number: shared_out(jax.random.fold_in(key_list[1], 2), own, number, P_DEV, N_BX * N_BY, 1, CAP, 2))(owners_keys, owners_turns).reshape((POINTS, 1))
    cells = set_ends(jax.random.randint(key_list[2], (POINTS,), 0, CX * CY * NZ), jax.random.fold_in(key_list[2], 1), 0, (CX * CY * NZ) - 1).astype(jnp.int32)
    levels = set_ends(jax.random.randint(key_list[3], (N_BX, N_BY), 0, 4), jax.random.fold_in(key_list[3], 1), 0, 3).astype(jnp.int32)
    rows_inverse = draw_rows_inverse(jax.random.fold_in(key_list[7], 71), 0)
    columns_inverse = draw_columns_inverse(jax.random.fold_in(key_list[7], 71), 0)
    depth_inverse = draw_depth_inverse(jax.random.fold_in(key_list[7], 71), 0)
    return {"normals": normals, "owners": owners, "cells": cells, "levels": levels, "rows_inverse": rows_inverse, "columns_inverse": columns_inverse, "depth_inverse": depth_inverse}


screen_base = 1.0


def stencil(field, screening):
    padded = jnp.pad(field, 1)
    beside = padded[2:, 1:-1, 1:-1] + padded[:-2, 1:-1, 1:-1]
    beside = beside + padded[1:-1, 2:, 1:-1] + padded[1:-1, :-2, 1:-1]
    beside = beside + padded[1:-1, 1:-1, 2:] + padded[1:-1, 1:-1, :-2]
    return (6.0 + screening) * field - beside


def reference(normals, owners, cells, levels, rows_inverse, columns_inverse, depth_inverse):
    target = owners[:, 0]
    first_index = (target // N_BY) * CX + cells // (CY * NZ)
    second_index = (target % N_BY) * CY + (cells // NZ) % CY
    third_index = cells % NZ
    vector_field = jnp.zeros((3, NX, NY, NZ), jnp.float32).at[:, first_index, second_index, third_index].add(normals)
    padded = jnp.pad(vector_field, ((0, 0), (1, 1), (1, 1), (1, 1)))
    source = -0.5 * ((padded[0, 2:, 1:-1, 1:-1] - padded[0, :-2, 1:-1, 1:-1])
                     + (padded[1, 1:-1, 2:, 1:-1] - padded[1, 1:-1, :-2, 1:-1])
                     + (padded[2, 1:-1, 1:-1, 2:] - padded[2, 1:-1, 1:-1, :-2]))
    screening = screen_base * (1.0 + levels.astype(jnp.float32))
    screening = jnp.repeat(jnp.repeat(screening, CX, 0), CY, 1)[:, :, None]
    highest = lax.Precision.HIGHEST
    iterate = jnp.zeros((NX, NY, NZ), jnp.float32)
    for iteration in range(ITERS):
        remainder = source - stencil(iterate, screening)
        iterate = iterate + jnp.einsum("ab,bjk->ajk", rows_inverse, remainder, precision=highest)
        remainder = source - stencil(iterate, screening)
        iterate = iterate + jnp.einsum("ab,ibk->iak", columns_inverse, remainder, precision=highest)
        remainder = source - stencil(iterate, screening)
        iterate = iterate + jnp.einsum("ab,ijb->ija", depth_inverse, remainder, precision=highest)
    implicit = iterate[first_index, second_index, third_index]
    return iterate, implicit
```

```python
import jax
import jax.numpy as jnp
from jax import lax
from jax.sharding import PartitionSpec as P

CX = 16
CY = 64
NZ = 256
ITERS = 4
EVERY = ("bx", "by")


screen_base = 1.0


def padded(shard, sides, width):
    for axis, dim in sides:
        peers, length = (lax.axis_size(axis), shard.shape[dim])
        up = [(i, (i + 1) % peers) for i in range(peers - 1)]
        down = [(j, i) for i, j in up]
        last = lax.slice_in_dim(shard, length - width, length, axis=dim)
        initial = lax.slice_in_dim(shard, 0, width, axis=dim)
        before = lax.ppermute(last, axis, up)
        after = lax.ppermute(initial, axis, down)
        shard = jnp.concatenate([before, shard, after], axis=dim)
    return shard


def slab_halo(slab, width):
    devices = lax.axis_size(EVERY)
    count = slab.shape[0]
    before, after = [], []
    reach = 1
    while width > 0:
        part = min(width, count)
        up = [(i, i + reach) for i in range(devices - reach)]
        down = [(j, i) for i, j in up]
        before.insert(0, lax.ppermute(slab[count - part :], EVERY, up))
        after.append(lax.ppermute(slab[:part], EVERY, down))
        width, reach = width - part, reach + 1
    return jnp.concatenate(before + [slab] + after, axis=0)


def turn(slab):
    devices = lax.axis_size(EVERY)
    n, first, second = slab.shape
    sent = slab.transpose(2, 0, 1)
    held = lax.all_to_all(sent, EVERY, split_axis=0, concat_axis=0, tiled=True)
    held = held.reshape(devices, second // devices, n, first)
    return held.transpose(1, 0, 2, 3).reshape(second // devices, devices * n, first)


def stencil(field, diagonal):
    middle = field[1:-1]
    beside = field[2:] + field[:-2]
    wide = jnp.pad(middle, ((0, 0), (1, 1), (1, 1)))
    beside = beside + wide[:, 2:, 1:-1] + wide[:, :-2, 1:-1]
    beside = beside + wide[:, 1:-1, 2:] + wide[:, 1:-1, :-2]
    return diagonal * middle - beside


def phase(iterate, source, diagonal, inside, first_matrix, second_matrix):
    highest = lax.Precision.HIGHEST
    remainder = source - stencil(iterate, diagonal)
    step = jnp.einsum("ab,nbk->nak", first_matrix, remainder, precision=highest)
    iterate = iterate[1:-1] + step * inside
    remainder = source[1:-1] - stencil(iterate, diagonal[1:-1] if diagonal.shape[0] > 1 else diagonal)
    step = jnp.einsum("ab,nkb->nka", second_matrix, remainder, precision=highest)
    return iterate[1:-1] + step


def relax(source, level, rows_inverse, columns_inverse, depth_inverse):
    first_count, second_count = lax.axis_size("bx"), lax.axis_size("by")
    devices = first_count * second_count
    me = lax.axis_index(EVERY)
    nx, ny = first_count * CX, second_count * CY
    thick = (NZ // devices, ny // devices, nx // devices)
    levels = lax.all_gather(level[0], EVERY, tiled=False).reshape(first_count, second_count)
    diagonal = 6.0 + screen_base * (1.0 + levels.astype(jnp.float32))
    diagonal = jnp.repeat(jnp.repeat(diagonal, CX, 0), CY, 1)
    own = lambda n: me * n - 1 + jnp.arange(n + 2)
    inside = []
    for n in thick:
        place = own(n)
        inside.append(((place >= 0) & (place < n * devices)).astype(jnp.float32)[:, None, None])
    wide = jnp.pad(diagonal, ((1, 1), (1, 1)), constant_values=1.0)
    diagonals = (
        diagonal[None],
        lax.dynamic_slice_in_dim(wide, me * thick[1], thick[1] + 2, 1).T[:, None, 1:-1],
        lax.dynamic_slice_in_dim(wide, me * thick[2], thick[2] + 2, 0)[:, 1:-1, None],
    )
    sent = source.reshape(CX, CY, devices, NZ // devices).transpose(2, 3, 0, 1)
    held = lax.all_to_all(sent, EVERY, split_axis=0, concat_axis=0, tiled=True)
    held = held.reshape(first_count, second_count, thick[0], CX, CY).transpose(2, 0, 3, 1, 4)
    z_source = held.reshape(thick[0], nx, ny)
    held = lax.all_to_all(source, "by", split_axis=0, concat_axis=1, tiled=True)
    sources = [slab_halo(z_source, 1), slab_halo(turn(z_source), 1), slab_halo(held, 1)]
    matrices = (rows_inverse, columns_inverse, depth_inverse)
    iterate = jnp.zeros((thick[0], nx, ny), jnp.float32)
    for step in range(3 * ITERS // 2):
        at = step % 3
        iterate = phase(
            slab_halo(iterate, 2),
            sources[at],
            diagonals[at],
            inside[at],
            matrices[2 * step % 3],
            matrices[(2 * step + 1) % 3],
        )
        if step + 1 < 3 * ITERS // 2:
            iterate = turn(iterate)
    return lax.all_to_all(iterate, "by", split_axis=1, concat_axis=0, tiled=True)


def local(normals, owners, cells, levels, rows_inverse, columns_inverse, depth_inverse):
    first_count = lax.axis_size("bx")
    second_count = lax.axis_size("by")
    bricks = first_count * second_count
    point_count = cells.shape[0]
    capacity = 2 * point_count // bricks
    brick_cells = CX * CY * NZ
    target = owners[:, 0]
    onehot = (target[:, None] == jnp.arange(bricks, dtype=jnp.int32)[None, :]).astype(jnp.int32)
    ranking = jnp.sum(onehot * (jnp.cumsum(onehot, axis=0) - 1), axis=1)
    slot_index = target * capacity + ranking
    send_normals = jnp.zeros((3, bricks * capacity), jnp.float32).at[:, slot_index].set(normals)
    send_cells = jnp.zeros((bricks * capacity,), jnp.int32).at[slot_index].set(cells)
    arrived_normals, arrived_cells = (
        lax.all_to_all(
            send_normals.reshape(3, bricks, capacity),
            ("bx", "by"),
            split_axis=1,
            concat_axis=1,
            tiled=True,
        ),
        lax.all_to_all(
            send_cells.reshape(1, bricks, capacity),
            ("bx", "by"),
            split_axis=1,
            concat_axis=1,
            tiled=True,
        ),
    )
    flat_cells = arrived_cells.reshape(-1)
    vector_field = (
        jnp.zeros((3, brick_cells), jnp.float32)
        .at[:, flat_cells]
        .add(arrived_normals.reshape(3, -1))
    )
    vector_field = vector_field.reshape(3, CX, CY, NZ)
    stretched = padded(vector_field, (("bx", 1), ("by", 2)), 1)
    z_padded = jnp.pad(vector_field[2], ((0, 0), (0, 0), (1, 1)))
    source = -0.5 * (
        stretched[0, 2:, 1:-1]
        - stretched[0, :-2, 1:-1]
        + (stretched[1, 1:-1, 2:] - stretched[1, 1:-1, :-2])
        + (z_padded[:, :, 2:] - z_padded[:, :, :-2])
    )
    iterate = relax(source, levels[0], rows_inverse, columns_inverse, depth_inverse)
    sampled = iterate.reshape(-1)[flat_cells]
    returned = lax.all_to_all(
        sampled.reshape(1, bricks, capacity), ("bx", "by"), split_axis=1, concat_axis=1, tiled=True
    )
    implicit = returned.reshape(-1)[slot_index]
    return (iterate, implicit)


def solution(mesh):
    placed = (
        P(None, ("bx", "by")),
        P(("bx", "by"), None),
        P(("bx", "by")),
        P("bx", "by"),
        P(),
        P(),
        P(),
    )
    return jax.shard_map(
        local,
        mesh=mesh,
        in_specs=placed,
        out_specs=(P("bx", "by", None), P(("bx", "by"))),
        check_vma=False,
    )
```

```python
import jax
import jax.numpy as jnp
from jax import lax
from jax.experimental import pallas as pl
from jax.experimental.pallas import tpu as pltpu
from jax.sharding import PartitionSpec as P

CX = 16
CY = 64
NZ = 256
ITERS = 4
EVERY = ("bx", "by")


screen_base = 1.0


def parts_of(value, count):
    parts = []
    for _ in range(count):
        part = value.astype(jnp.bfloat16)
        parts.append(part)
        value = value - part.astype(jnp.float32)
    return parts


def rows_iota(rows, columns):
    return lax.broadcasted_iota(jnp.int32, (rows, columns), 0)


def flags(condition):
    return jnp.where(condition, 1.0, 0.0)


def whole_arrays(count):
    return [pl.BlockSpec(memory_space=pltpu.VMEM)] * count


def pack_kernel(owner_ref, cell_ref, normal_ref, send_ref, rank_ref, total_ref):
    bricks, capacity = send_ref.shape[0], total_ref.shape[1]
    points = owner_ref.shape[1]
    block = 256
    before = flags(rows_iota(block, block) < lax.broadcasted_iota(jnp.int32, (block, block), 1)).astype(jnp.bfloat16)
    total_ref[...] = jnp.zeros_like(total_ref)

    def step(at, seen):
        here = pl.ds(pl.multiple_of(at * block, block), block)
        named = flags(rows_iota(bricks, block) == owner_ref[:, here])
        inside = jnp.dot(named.astype(jnp.bfloat16), before, preferred_element_type=jnp.float32)
        rank = jnp.sum(named * (inside + seen), axis=0, keepdims=True)
        rank_ref[:, here] = rank
        slot = flags(rows_iota(capacity, block).astype(jnp.float32) == rank).astype(jnp.bfloat16)
        values = []
        for k in range(3):
            values += [part.astype(jnp.float32) for part in parts_of(normal_ref[k : k + 1, here], 3)]
        cell = cell_ref[:, here] + 1
        for shift in (16, 8, 0):
            values.append(((cell >> shift) & 255).astype(jnp.float32))
        rows = jnp.concatenate([(named * value).astype(jnp.bfloat16) for value in values], axis=0)
        total_ref[...] += lax.dot_general(
            rows, slot, (((1,), (1,)), ((), ())), preferred_element_type=jnp.float32
        )
        return seen + jnp.sum(named, axis=1, keepdims=True)

    lax.fori_loop(0, points // block, step, jnp.zeros((bricks, 1), jnp.float32))
    part = lambda i: total_ref[i * bricks : (i + 1) * bricks, :]
    fields = [part(3 * k) + part(3 * k + 1) + part(3 * k + 2) for k in range(3)]
    fields.append(part(9) * 65536.0 + part(10) * 256.0 + part(11))
    row = jnp.concatenate(fields, axis=1)
    for j in range(send_ref.shape[1]):
        send_ref[:, j, :] = row[:, 128 * j : 128 * (j + 1)]


def pack(owners, cells, normals, bricks, capacity):
    points = cells.shape[0]
    return pl.pallas_call(
        pack_kernel,
        out_shape=(
            jax.ShapeDtypeStruct((bricks, 4 * capacity // 128, 128), jnp.float32),
            jax.ShapeDtypeStruct((1, points), jnp.float32),
        ),
        in_specs=whole_arrays(3),
        out_specs=tuple(whole_arrays(2)),
        scratch_shapes=[pltpu.VMEM((12 * bricks, capacity), jnp.float32)],
        compiler_params=pltpu.CompilerParams(vmem_limit_bytes=32 << 20),
        name="pack",
    )(owners.reshape(1, points), cells.reshape(1, points), normals)


def unpack_kernel(owner_ref, rank_ref, held_ref, out_ref):
    bricks, capacity = held_ref.shape
    points = owner_ref.shape[1]
    block = 512
    held = jnp.concatenate([part.astype(jnp.float32).T for part in parts_of(held_ref[...], 3)], axis=1)
    held = held.astype(jnp.bfloat16)
    for at in range(points // block):
        here = slice(at * block, (at + 1) * block)
        named = flags(rows_iota(bricks, block) == owner_ref[:, here]).astype(jnp.bfloat16)
        named = jnp.concatenate([named] * 3, axis=0)
        found = jnp.dot(held, named, preferred_element_type=jnp.float32)
        slot = rows_iota(capacity, block).astype(jnp.float32) == rank_ref[:, here]
        out_ref[:, here] = jnp.sum(jnp.where(slot, found, 0.0), axis=0, keepdims=True)


def unpack(owners, rank, held):
    points = owners.shape[0]
    out = pl.pallas_call(
        unpack_kernel,
        out_shape=jax.ShapeDtypeStruct((1, points), jnp.float32),
        in_specs=whole_arrays(3),
        out_specs=pl.BlockSpec(memory_space=pltpu.VMEM),
        compiler_params=pltpu.CompilerParams(vmem_limit_bytes=32 << 20),
        name="unpack",
    )(owners.reshape(1, points), rank, held)
    return out.reshape(points)


def spread(row):
    return jnp.broadcast_to(row, (16, 128)).astype(jnp.bfloat16)


def times_row(table, row16):
    rows = table.shape[0]
    return (table.reshape(rows // 16, 16, 128) * row16[None]).reshape(rows, 128)


def places(cell_row):
    cell = cell_row.astype(jnp.int32) - 1
    return cell >> 14, (cell >> 8) & (CY - 1), cell & (NZ - 1)


def differenced(rows, first, at):
    index = rows_iota(rows, 128) + first
    return jnp.where(index == at + 1, 0.5, 0.0) - jnp.where(index == at - 1, 0.5, 0.0)


def splat_kernel(used_ref, field_ref, source_ref, x_face_ref, y_face_ref):
    chunks = field_ref.shape[0] // 4
    source_ref[...] = jnp.zeros_like(source_ref)
    x_face_ref[...] = jnp.zeros_like(x_face_ref)
    y_face_ref[...] = jnp.zeros_like(y_face_ref)

    def product(rows, columns):
        return lax.dot_general(rows, columns, (((1,), (1,)), ((), ())), preferred_element_type=jnp.float32)

    def step(at, carry):
        @pl.when(used_ref[at] > 0)
        def _():
            x, y, z = places(field_ref[pl.ds(3 * chunks + at, 1), :])
            y_hot = flags(rows_iota(CY, 128) == y).astype(jnp.bfloat16)
            y_step = differenced(CY, 0, y).astype(jnp.bfloat16)
            z_hot = flags(rows_iota(NZ, 128) == z).astype(jnp.bfloat16)
            z_step = differenced(NZ, 0, z).astype(jnp.bfloat16)
            columns = []
            for k in range(3):
                for part in parts_of(field_ref[pl.ds(k * chunks + at, 1), :], 2):
                    columns.append(times_row(z_step if k == 2 else z_hot, spread(part.astype(jnp.float32))))
            columns = jnp.concatenate(columns, axis=1)
            steps = [spread(jnp.where(x == i - 1, 0.5, 0.0) - jnp.where(x == i + 1, 0.5, 0.0)) for i in range(-1, CX + 1)]
            hots = [spread(flags(x == i)) for i in range(CX)]
            along_x = jnp.concatenate([times_row(y_hot, steps[i + 1]) for i in range(CX)], axis=0)
            along_y = jnp.concatenate([times_row(y_step, hots[i]) for i in range(CX)], axis=0)
            along_z = jnp.concatenate([times_row(y_hot, hots[i]) for i in range(CX)], axis=0)
            rows = jnp.concatenate([along_x, along_x, along_y, along_y, along_z, along_z], axis=1)
            source_ref[...] += product(rows, columns)
            ends = jnp.concatenate([times_row(y_hot, steps[0]), times_row(y_hot, steps[CX + 1])], axis=0)
            x_face_ref[...] += product(jnp.concatenate([ends, ends], axis=1), columns[:, :256])
            x_hot = flags(rows_iota(CX, 128) == x).astype(jnp.bfloat16)
            ends = jnp.concatenate(
                [x_hot * spread(jnp.where(y == 0, -0.5, 0.0)), x_hot * spread(jnp.where(y == CY - 1, 0.5, 0.0))], axis=0
            )
            y_face_ref[...] += product(jnp.concatenate([ends, ends], axis=1), columns[:, 256:512])

        return carry

    lax.fori_loop(0, chunks, step, 0)


def splat(field, used):
    shapes = ((CX * CY, NZ), (2 * CY, NZ), (2 * CX, NZ))
    return pl.pallas_call(
        splat_kernel,
        out_shape=tuple(jax.ShapeDtypeStruct(shape, jnp.float32) for shape in shapes),
        in_specs=[pl.BlockSpec(memory_space=pltpu.SMEM), pl.BlockSpec(memory_space=pltpu.VMEM)],
        out_specs=tuple(whole_arrays(3)),
        compiler_params=pltpu.CompilerParams(vmem_limit_bytes=32 << 20),
        name="splat",
    )(used, field)


def sample_kernel(field_ref, iterate_ref, out_ref, turned_ref):
    chunks = out_ref.shape[0]
    for i in range(CX * CY // 128):
        here = slice(128 * i, 128 * (i + 1))
        block = iterate_ref[here, :].T
        high, low = parts_of(block, 2)
        turned_ref[:NZ, here] = high
        turned_ref[NZ:, here] = low

    def step(at, carry):
        tables, heights = [], []
        for half in range(2):
            x, y, z = places(field_ref[pl.ds(2 * at + half, 1), :])
            y_hot = flags(rows_iota(CY, 128) == y).astype(jnp.bfloat16)
            hots = [spread(flags(x == i)) for i in range(CX)]
            tables.append(jnp.concatenate([times_row(y_hot, hots[i]) for i in range(CX)], axis=0))
            heights.append(z)
        found = jnp.dot(turned_ref[...], jnp.concatenate(tables, axis=1), preferred_element_type=jnp.float32)
        found = found[:NZ] + found[NZ:]
        level = rows_iota(NZ, 256) == jnp.concatenate(heights, axis=1)
        row = jnp.sum(jnp.where(level, found, 0.0), axis=0, keepdims=True)
        out_ref[pl.ds(2 * at, 1), :] = row[:, :128]
        out_ref[pl.ds(2 * at + 1, 1), :] = row[:, 128:]
        return carry

    lax.fori_loop(0, chunks // 2, step, 0)


def sample(cell_rows, iterate):
    return pl.pallas_call(
        sample_kernel,
        out_shape=jax.ShapeDtypeStruct(cell_rows.shape, jnp.float32),
        in_specs=whole_arrays(2),
        out_specs=pl.BlockSpec(memory_space=pltpu.VMEM),
        scratch_shapes=[pltpu.VMEM((2 * NZ, CX * CY), jnp.bfloat16)],
        compiler_params=pltpu.CompilerParams(vmem_limit_bytes=32 << 20),
        name="sample",
    )(cell_rows, iterate)


def neighbours(face, axis, count):
    peers = lax.axis_size(axis)
    up = [(i, i + 1) for i in range(peers - 1)]
    down = [(j, i) for i, j in up]
    return lax.ppermute(face[count:], axis, up), lax.ppermute(face[:count], axis, down)


def slab_halo(slab, width):
    devices = lax.axis_size(EVERY)
    count = slab.shape[0]
    before, after = [], []
    reach = 1
    while width > 0:
        part = min(width, count)
        up = [(i, i + reach) for i in range(devices - reach)]
        down = [(j, i) for i, j in up]
        before.insert(0, lax.ppermute(slab[count - part :], EVERY, up))
        after.append(lax.ppermute(slab[:part], EVERY, down))
        width, reach = width - part, reach + 1
    return jnp.concatenate(before + [slab] + after, axis=0)


def turn(slab):
    devices = lax.axis_size(EVERY)
    n, first, second = slab.shape
    sent = slab.transpose(2, 0, 1)
    held = lax.all_to_all(sent, EVERY, split_axis=0, concat_axis=0, tiled=True)
    held = held.reshape(devices, second // devices, n, first)
    return held.transpose(1, 0, 2, 3).reshape(second // devices, devices * n, first)


def stencil(field, diagonal):
    middle = field[1:-1]
    beside = field[2:] + field[:-2]
    wide = jnp.pad(middle, ((0, 0), (1, 1), (1, 1)))
    beside = beside + wide[:, 2:, 1:-1] + wide[:, :-2, 1:-1]
    beside = beside + wide[:, 1:-1, 2:] + wide[:, 1:-1, :-2]
    return diagonal * middle - beside


def phase(iterate, source, diagonal, inside, first_matrix, second_matrix):
    highest = lax.Precision.HIGHEST
    remainder = source - stencil(iterate, diagonal)
    step = jnp.einsum("ab,nbk->nak", first_matrix, remainder, precision=highest)
    iterate = iterate[1:-1] + step * inside
    remainder = source[1:-1] - stencil(iterate, diagonal[1:-1] if diagonal.shape[0] > 1 else diagonal)
    step = jnp.einsum("ab,nkb->nka", second_matrix, remainder, precision=highest)
    return iterate[1:-1] + step


def relax(source, levels, rows_inverse, columns_inverse, depth_inverse):
    first_count, second_count = lax.axis_size("bx"), lax.axis_size("by")
    devices = first_count * second_count
    me = lax.axis_index(EVERY)
    nx, ny = first_count * CX, second_count * CY
    thick = (NZ // devices, ny // devices, nx // devices)
    diagonal = 6.0 + screen_base * (1.0 + levels.reshape(first_count, second_count))
    diagonal = jnp.repeat(jnp.repeat(diagonal, CX, 0), CY, 1)
    own = lambda n: me * n - 1 + jnp.arange(n + 2)
    inside = []
    for n in thick:
        place = own(n)
        inside.append(((place >= 0) & (place < n * devices)).astype(jnp.float32)[:, None, None])
    wide = jnp.pad(diagonal, ((1, 1), (1, 1)), constant_values=1.0)
    diagonals = (
        diagonal[None],
        lax.dynamic_slice_in_dim(wide, me * thick[1], thick[1] + 2, 1).T[:, None, 1:-1],
        lax.dynamic_slice_in_dim(wide, me * thick[2], thick[2] + 2, 0)[:, 1:-1, None],
    )
    sent = source.reshape(CX, CY, devices, NZ // devices).transpose(2, 3, 0, 1)
    held = lax.all_to_all(sent, EVERY, split_axis=0, concat_axis=0, tiled=True)
    held = held.reshape(first_count, second_count, thick[0], CX, CY).transpose(2, 0, 3, 1, 4)
    z_source = held.reshape(thick[0], nx, ny)
    held = lax.all_to_all(source, "by", split_axis=0, concat_axis=1, tiled=True)
    sources = [slab_halo(z_source, 1), slab_halo(turn(z_source), 1), slab_halo(held, 1)]
    matrices = (rows_inverse, columns_inverse, depth_inverse)
    iterate = jnp.zeros((thick[0], nx, ny), jnp.float32)
    for step in range(3 * ITERS // 2):
        at = step % 3
        iterate = phase(
            slab_halo(iterate, 2),
            sources[at],
            diagonals[at],
            inside[at],
            matrices[2 * step % 3],
            matrices[(2 * step + 1) % 3],
        )
        if step + 1 < 3 * ITERS // 2:
            iterate = turn(iterate)
    return lax.all_to_all(iterate, "by", split_axis=1, concat_axis=0, tiled=True)


def local(normals, owners, cells, levels, rows_inverse, columns_inverse, depth_inverse):
    bricks = lax.axis_size(EVERY)
    point_count = cells.shape[0]
    capacity = 2 * point_count // bricks
    chunks = bricks * capacity // 128
    level = jnp.broadcast_to(levels.astype(jnp.float32), (1, 128))
    levels = lax.all_gather(level, EVERY, tiled=True)[:, 0]
    send, rank = pack(owners, cells, normals, bricks, capacity)
    held = lax.all_to_all(send, EVERY, split_axis=0, concat_axis=0, tiled=True)
    field = held.reshape(bricks, 4, capacity).transpose(1, 0, 2).reshape(4 * chunks, 128)
    cell_rows = field[3 * chunks :]
    used = (jnp.max(cell_rows, axis=1) > 0).astype(jnp.int32)
    source, x_face, y_face = splat(field, used)
    source = source.reshape(CX, CY, NZ)
    x_before, x_after = neighbours(x_face, "bx", CY)
    y_before, y_after = neighbours(y_face, "by", CX)
    source = source + jnp.pad(x_before[None], ((0, CX - 1), (0, 0), (0, 0)))
    source = source + jnp.pad(x_after[None], ((CX - 1, 0), (0, 0), (0, 0)))
    source = source + jnp.pad(y_before[:, None], ((0, 0), (0, CY - 1), (0, 0)))
    source = source + jnp.pad(y_after[:, None], ((0, 0), (CY - 1, 0), (0, 0)))
    iterate = relax(source, levels, rows_inverse, columns_inverse, depth_inverse)
    sampled = sample(cell_rows, iterate.reshape(CX * CY, NZ))
    returned = lax.all_to_all(sampled.reshape(bricks, capacity), EVERY, split_axis=0, concat_axis=0, tiled=True)
    implicit = unpack(owners, rank, returned)
    return (iterate, implicit)


def solution(mesh):
    placed = (
        P(None, ("bx", "by")),
        P(("bx", "by"), None),
        P(("bx", "by")),
        P("bx", "by"),
        P(),
        P(),
        P(),
    )
    return jax.shard_map(
        local,
        mesh=mesh,
        in_specs=placed,
        out_specs=(P("bx", "by", None), P(("bx", "by"))),
        check_vma=False,
    )
```

```python
import functools

import jax
import jax.numpy as jnp
from jax import lax
from jax.experimental import pallas as pl
from jax.experimental.pallas import tpu as pltpu
from jax.sharding import PartitionSpec as P

CX = 16
CY = 64
NZ = 256
ITERS = 4
EVERY = ("bx", "by")


screen_base = 1.0


def parts_of(value, count):
    parts = []
    for _ in range(count):
        part = value.astype(jnp.bfloat16)
        parts.append(part)
        value = value - part.astype(jnp.float32)
    return parts


def rows_iota(rows, columns):
    return lax.broadcasted_iota(jnp.int32, (rows, columns), 0)


def flags(condition):
    return jnp.where(condition, 1.0, 0.0)


def whole_arrays(count):
    return [pl.BlockSpec(memory_space=pltpu.VMEM)] * count


def pack_kernel(owner_ref, cell_ref, normal_ref, send_ref, rank_ref, total_ref):
    bricks, capacity = send_ref.shape[0], total_ref.shape[1]
    points = owner_ref.shape[1]
    block = 256
    before = flags(rows_iota(block, block) < lax.broadcasted_iota(jnp.int32, (block, block), 1)).astype(jnp.bfloat16)
    total_ref[...] = jnp.zeros_like(total_ref)

    def step(at, seen):
        here = pl.ds(pl.multiple_of(at * block, block), block)
        named = flags(rows_iota(bricks, block) == owner_ref[:, here])
        inside = jnp.dot(named.astype(jnp.bfloat16), before, preferred_element_type=jnp.float32)
        rank = jnp.sum(named * (inside + seen), axis=0, keepdims=True)
        rank_ref[:, here] = rank
        slot = flags(rows_iota(capacity, block).astype(jnp.float32) == rank).astype(jnp.bfloat16)
        values = []
        for k in range(3):
            values += [part.astype(jnp.float32) for part in parts_of(normal_ref[k : k + 1, here], 3)]
        cell = cell_ref[:, here] + 1
        for shift in (16, 8, 0):
            values.append(((cell >> shift) & 255).astype(jnp.float32))
        rows = jnp.concatenate([(named * value).astype(jnp.bfloat16) for value in values], axis=0)
        total_ref[...] += lax.dot_general(
            rows, slot, (((1,), (1,)), ((), ())), preferred_element_type=jnp.float32
        )
        return seen + jnp.sum(named, axis=1, keepdims=True)

    lax.fori_loop(0, points // block, step, jnp.zeros((bricks, 1), jnp.float32))
    part = lambda i: total_ref[i * bricks : (i + 1) * bricks, :]
    fields = [part(3 * k) + part(3 * k + 1) + part(3 * k + 2) for k in range(3)]
    fields.append(part(9) * 65536.0 + part(10) * 256.0 + part(11))
    row = jnp.concatenate(fields, axis=1)
    for j in range(send_ref.shape[1]):
        send_ref[:, j, :] = row[:, 128 * j : 128 * (j + 1)]


def pack(owners, cells, normals, bricks, capacity):
    points = cells.shape[0]
    return pl.pallas_call(
        pack_kernel,
        out_shape=(
            jax.ShapeDtypeStruct((bricks, 4 * capacity // 128, 128), jnp.float32),
            jax.ShapeDtypeStruct((1, points), jnp.float32),
        ),
        in_specs=whole_arrays(3),
        out_specs=tuple(whole_arrays(2)),
        scratch_shapes=[pltpu.VMEM((12 * bricks, capacity), jnp.float32)],
        compiler_params=pltpu.CompilerParams(vmem_limit_bytes=32 << 20),
        name="pack",
    )(owners.reshape(1, points), cells.reshape(1, points), normals)


def unpack_kernel(owner_ref, rank_ref, held_ref, out_ref):
    bricks, capacity = held_ref.shape
    points = owner_ref.shape[1]
    block = 512
    held = jnp.concatenate([part.astype(jnp.float32).T for part in parts_of(held_ref[...], 3)], axis=1)
    held = held.astype(jnp.bfloat16)
    for at in range(points // block):
        here = slice(at * block, (at + 1) * block)
        named = flags(rows_iota(bricks, block) == owner_ref[:, here]).astype(jnp.bfloat16)
        named = jnp.concatenate([named] * 3, axis=0)
        found = jnp.dot(held, named, preferred_element_type=jnp.float32)
        slot = rows_iota(capacity, block).astype(jnp.float32) == rank_ref[:, here]
        out_ref[:, here] = jnp.sum(jnp.where(slot, found, 0.0), axis=0, keepdims=True)


def unpack(owners, rank, held):
    points = owners.shape[0]
    out = pl.pallas_call(
        unpack_kernel,
        out_shape=jax.ShapeDtypeStruct((1, points), jnp.float32),
        in_specs=whole_arrays(3),
        out_specs=pl.BlockSpec(memory_space=pltpu.VMEM),
        compiler_params=pltpu.CompilerParams(vmem_limit_bytes=32 << 20),
        name="unpack",
    )(owners.reshape(1, points), rank, held)
    return out.reshape(points)


def spread(row):
    return jnp.broadcast_to(row, (16, 128)).astype(jnp.bfloat16)


def times_row(table, row16):
    rows = table.shape[0]
    return (table.reshape(rows // 16, 16, 128) * row16[None]).reshape(rows, 128)


def places(cell_row):
    cell = cell_row.astype(jnp.int32) - 1
    return cell >> 14, (cell >> 8) & (CY - 1), cell & (NZ - 1)


def differenced(rows, first, at):
    index = rows_iota(rows, 128) + first
    return jnp.where(index == at + 1, 0.5, 0.0) - jnp.where(index == at - 1, 0.5, 0.0)


def splat_kernel(used_ref, field_ref, source_ref, x_face_ref, y_face_ref):
    chunks = field_ref.shape[0] // 4
    source_ref[...] = jnp.zeros_like(source_ref)
    x_face_ref[...] = jnp.zeros_like(x_face_ref)
    y_face_ref[...] = jnp.zeros_like(y_face_ref)

    def product(rows, columns):
        return lax.dot_general(rows, columns, (((1,), (1,)), ((), ())), preferred_element_type=jnp.float32)

    def step(at, carry):
        @pl.when(used_ref[at] > 0)
        def _():
            x, y, z = places(field_ref[pl.ds(3 * chunks + at, 1), :])
            y_hot = flags(rows_iota(CY, 128) == y).astype(jnp.bfloat16)
            y_step = differenced(CY, 0, y).astype(jnp.bfloat16)
            z_hot = flags(rows_iota(NZ, 128) == z).astype(jnp.bfloat16)
            z_step = differenced(NZ, 0, z).astype(jnp.bfloat16)
            columns = []
            for k in range(3):
                for part in parts_of(field_ref[pl.ds(k * chunks + at, 1), :], 2):
                    columns.append(times_row(z_step if k == 2 else z_hot, spread(part.astype(jnp.float32))))
            columns = jnp.concatenate(columns, axis=1)
            steps = [spread(jnp.where(x == i - 1, 0.5, 0.0) - jnp.where(x == i + 1, 0.5, 0.0)) for i in range(-1, CX + 1)]
            hots = [spread(flags(x == i)) for i in range(CX)]
            along_x = jnp.concatenate([times_row(y_hot, steps[i + 1]) for i in range(CX)], axis=0)
            along_y = jnp.concatenate([times_row(y_step, hots[i]) for i in range(CX)], axis=0)
            along_z = jnp.concatenate([times_row(y_hot, hots[i]) for i in range(CX)], axis=0)
            rows = jnp.concatenate([along_x, along_x, along_y, along_y, along_z, along_z], axis=1)
            source_ref[...] += product(rows, columns)
            ends = jnp.concatenate([times_row(y_hot, steps[0]), times_row(y_hot, steps[CX + 1])], axis=0)
            x_face_ref[...] += product(jnp.concatenate([ends, ends], axis=1), columns[:, :256])
            x_hot = flags(rows_iota(CX, 128) == x).astype(jnp.bfloat16)
            ends = jnp.concatenate(
                [x_hot * spread(jnp.where(y == 0, -0.5, 0.0)), x_hot * spread(jnp.where(y == CY - 1, 0.5, 0.0))], axis=0
            )
            y_face_ref[...] += product(jnp.concatenate([ends, ends], axis=1), columns[:, 256:512])

        return carry

    lax.fori_loop(0, chunks, step, 0)


def splat(field, used):
    shapes = ((CX * CY, NZ), (2 * CY, NZ), (2 * CX, NZ))
    return pl.pallas_call(
        splat_kernel,
        out_shape=tuple(jax.ShapeDtypeStruct(shape, jnp.float32) for shape in shapes),
        in_specs=[pl.BlockSpec(memory_space=pltpu.SMEM), pl.BlockSpec(memory_space=pltpu.VMEM)],
        out_specs=tuple(whole_arrays(3)),
        compiler_params=pltpu.CompilerParams(vmem_limit_bytes=32 << 20),
        name="splat",
    )(used, field)


def sample_kernel(field_ref, iterate_ref, out_ref, turned_ref):
    chunks = out_ref.shape[0]
    for i in range(CX * CY // 128):
        here = slice(128 * i, 128 * (i + 1))
        block = iterate_ref[here, :].T
        high, low = parts_of(block, 2)
        turned_ref[:NZ, here] = high
        turned_ref[NZ:, here] = low

    def step(at, carry):
        tables, heights = [], []
        for half in range(2):
            x, y, z = places(field_ref[pl.ds(2 * at + half, 1), :])
            y_hot = flags(rows_iota(CY, 128) == y).astype(jnp.bfloat16)
            hots = [spread(flags(x == i)) for i in range(CX)]
            tables.append(jnp.concatenate([times_row(y_hot, hots[i]) for i in range(CX)], axis=0))
            heights.append(z)
        found = jnp.dot(turned_ref[...], jnp.concatenate(tables, axis=1), preferred_element_type=jnp.float32)
        found = found[:NZ] + found[NZ:]
        level = rows_iota(NZ, 256) == jnp.concatenate(heights, axis=1)
        row = jnp.sum(jnp.where(level, found, 0.0), axis=0, keepdims=True)
        out_ref[pl.ds(2 * at, 1), :] = row[:, :128]
        out_ref[pl.ds(2 * at + 1, 1), :] = row[:, 128:]
        return carry

    lax.fori_loop(0, chunks // 2, step, 0)


def sample(cell_rows, iterate):
    return pl.pallas_call(
        sample_kernel,
        out_shape=jax.ShapeDtypeStruct(cell_rows.shape, jnp.float32),
        in_specs=whole_arrays(2),
        out_specs=pl.BlockSpec(memory_space=pltpu.VMEM),
        scratch_shapes=[pltpu.VMEM((2 * NZ, CX * CY), jnp.bfloat16)],
        compiler_params=pltpu.CompilerParams(vmem_limit_bytes=32 << 20),
        name="sample",
    )(cell_rows, iterate)


def neighbours(face, axis, count):
    peers = lax.axis_size(axis)
    up = [(i, i + 1) for i in range(peers - 1)]
    down = [(j, i) for i, j in up]
    return lax.ppermute(face[count:], axis, up), lax.ppermute(face[:count], axis, down)


def parts_in_rows(value):
    high, low = parts_of(value, 2)
    return jnp.concatenate([high, low, high], axis=0)


def wide(matrix):
    high, low = parts_of(matrix, 2)
    return jnp.concatenate([high, high, low], axis=1)


def shifted(value, axis, back):
    length = value.shape[axis]
    moved = pltpu.roll(value, length - 1 if back else 1, axis)
    index = lax.broadcasted_iota(jnp.int32, value.shape, axis)
    return jnp.where(index == (length - 1 if back else 0), 0.0, moved)


def remainder_of(source, before, middle, after, diagonal):
    beside = before + after
    beside = beside + shifted(middle, 0, False) + shifted(middle, 0, True)
    beside = beside + shifted(middle, 1, False) + shifted(middle, 1, True)
    return source - (diagonal * middle - beside)


def pieces(ref, sources, per_source, start, rows, bands, per_band):
    columns = []
    for band in range(bands):
        starts = [i * per_source + band * per_band + start for i in range(sources)]
        columns.append(jnp.concatenate([ref[at : at + rows, :] for at in starts], axis=0))
    return jnp.concatenate(columns, axis=1)


def put(sent_ref, k, planes, targets, per_block, start, value):
    turned = value.T
    per_target = turned.shape[0] // targets
    for j in range(targets):
        for band in range(turned.shape[1] // 128):
            at = j * per_block + start + band * per_target * planes + k
            part = turned[j * per_target : (j + 1) * per_target, band * 128 : (band + 1) * 128]
            sent_ref[pl.ds(at, per_target, stride=planes), :] = part


def brick_planes(ref, first_count, second_count, planes, k):
    bands = []
    lane = lax.broadcasted_iota(jnp.int32, (8, 128), 1)
    for i in range(first_count):
        tiles = []
        for j in range(second_count):
            start = ((i * second_count + j) * planes + k) * 8
            tiles.append(ref[start : start + 8, :])
        turned = [pltpu.roll(tile, 64, 1) for tile in tiles]
        pairs = range(0, second_count, 2)
        bands.append(jnp.concatenate([jnp.where(lane < 64, tiles[j], turned[j + 1]) for j in pairs], axis=1))
        bands.append(jnp.concatenate([jnp.where(lane < 64, turned[j], tiles[j + 1]) for j in pairs], axis=1))
    return jnp.concatenate(bands, axis=0)


def sweep_all(count, step_ref, source_ref, diagonal_ref, matrix_ref, emit):
    matrix = wide(matrix_ref[...])
    for k in range(count):
        diagonal = diagonal_ref[0 if diagonal_ref.shape[0] == 1 else k + 1]
        middle = step_ref[k + 1]
        remainder = remainder_of(source_ref[k + 1], step_ref[k], middle, step_ref[k + 2], diagonal)
        high, low = parts_of(remainder, 2)
        row = jnp.concatenate([high, low, high], axis=1)
        step = lax.dot_general(row, matrix, (((1,), (1,)), ((), ())), preferred_element_type=jnp.float32)
        emit(k, middle + step)


def first_kernel(
    grid, held_ref, before_ref, after_ref, diagonal_ref, first_ref, second_ref, sent_ref, source_ref, step_ref
):
    first_count, second_count, planes, per_target = grid
    for k in range(planes):
        source_ref[k + 1] = brick_planes(held_ref, first_count, second_count, planes, k)
    source_ref[0] = brick_planes(before_ref, first_count, second_count, 1, 0)
    source_ref[planes + 1] = brick_planes(after_ref, first_count, second_count, 1, 0)
    first = wide(first_ref[...])
    for k in range(planes + 2):
        step_ref[k] = jnp.dot(first, parts_in_rows(source_ref[k]), preferred_element_type=jnp.float32)
    devices = first_count * second_count
    block = sent_ref.shape[0] // devices

    def emit(k, value):
        put(sent_ref, k, planes, devices, block, 0, source_ref[k + 1])
        put(sent_ref, k, planes, devices, block, block // 2, value)

    sweep_all(planes, step_ref, source_ref, diagonal_ref, second_ref, emit)


def later_kernel(
    shape, edge_ref, held_ref, before_ref, after_ref, diagonal_ref, first_ref, second_ref, *refs
):
    devices, planes, rows, with_source, last = shape
    if with_source:
        sent_ref, source_ref, iterate_ref, step_ref = refs
    else:
        source_ref, sent_ref, iterate_ref, step_ref = refs
    bands = iterate_ref.shape[2] // 128
    block, edge_block = held_ref.shape[0] // devices, before_ref.shape[0] // devices
    per_band = planes * rows
    edge_band = edge_block // bands
    own = lambda k, start: pieces(held_ref, devices, block, start + k * rows, rows, bands, per_band)
    edge = lambda ref, k: pieces(ref, devices, edge_block, k * rows, rows, bands, edge_band)
    if with_source:
        for k in range(planes):
            source_ref[k + 1] = own(k, 0)
        source_ref[0] = edge(before_ref, 0)
        source_ref[planes + 1] = edge(after_ref, 0)
    for k in range(2):
        iterate_ref[k] = edge(before_ref, k + with_source)
        iterate_ref[planes + 2 + k] = edge(after_ref, k + with_source)
    for k in range(planes):
        iterate_ref[k + 2] = own(k, block // 2 if with_source else 0)
    first = wide(first_ref[...])
    for k in range(planes + 2):
        diagonal = diagonal_ref[0 if diagonal_ref.shape[0] == 1 else k]
        middle = iterate_ref[k + 1]
        remainder = remainder_of(source_ref[k], iterate_ref[k], middle, iterate_ref[k + 2], diagonal)
        step = jnp.dot(first, parts_in_rows(remainder), preferred_element_type=jnp.float32)
        if k == 0:
            step = step * edge_ref[0]
        if k == planes + 1:
            step = step * edge_ref[1]
        step_ref[k] = middle + step

    def emit(k, value):
        if last:
            for j in range(value.shape[0] // CY):
                sent_ref[j, k] = value[j * CY : (j + 1) * CY, :]
        else:
            put(sent_ref, k, planes, devices, sent_ref.shape[0] // devices, 0, value)

    sweep_all(planes, step_ref, source_ref, diagonal_ref, second_ref, emit)


SMEM = pl.BlockSpec(memory_space=pltpu.SMEM)
VMEM = pl.BlockSpec(memory_space=pltpu.VMEM)
LIMIT = pltpu.CompilerParams(vmem_limit_bytes=48 << 20)


def first_phase(grid, held, before, after, diagonal, first, second):
    rows, columns = diagonal.shape[1:]
    first_count, second_count, planes, per_target = grid
    return pl.pallas_call(
        functools.partial(first_kernel, grid),
        out_shape=(
            jax.ShapeDtypeStruct((2 * columns * planes * rows // 128, 128), jnp.float32),
            jax.ShapeDtypeStruct((planes + 2, rows, columns), jnp.float32),
        ),
        in_specs=[VMEM] * 6,
        out_specs=(VMEM, VMEM),
        scratch_shapes=[pltpu.VMEM((planes + 2, rows, columns), jnp.float32)],
        compiler_params=LIMIT,
        name="first_phase",
    )(held, before, after, diagonal, first, second)


def later_phase(devices, planes, rows, edges, held, before, after, diagonal, first, second, source=None, last=False):
    columns = second.shape[1]
    length = devices * rows
    if last:
        sent = (length // CY, planes, CY, columns)
    else:
        sent = (columns * planes * length // 128, 128)
    out = [jax.ShapeDtypeStruct(sent, jnp.float32)]
    operands = [edges, held, before, after, diagonal, first, second]
    if source is None:
        out.append(jax.ShapeDtypeStruct((planes + 2, length, columns), jnp.float32))
    else:
        operands.append(source)
    return pl.pallas_call(
        functools.partial(later_kernel, (devices, planes, rows, source is None, last)),
        out_shape=tuple(out),
        in_specs=[SMEM] + [VMEM] * (len(operands) - 1),
        out_specs=tuple([VMEM] * len(out)),
        scratch_shapes=[
            pltpu.VMEM((planes + 4, length, columns), jnp.float32),
            pltpu.VMEM((planes + 2, length, columns), jnp.float32),
        ],
        compiler_params=LIMIT,
        name="later_phase",
    )(*operands)


def join_kernel(source_ref, x_before_ref, x_after_ref, y_before_ref, y_after_ref, brick_ref, sent_ref):
    for i in range(CX):
        here = slice(i * CY, (i + 1) * CY)
        value = source_ref[here, :]
        if i == 0:
            value = value + x_before_ref[...]
        if i == CX - 1:
            value = value + x_after_ref[...]
        row = rows_iota(CY, NZ)
        value = value + jnp.where(row == 0, y_before_ref[i : i + 1, :], 0.0)
        brick_ref[here, :] = value + jnp.where(row == CY - 1, y_after_ref[i : i + 1, :], 0.0)
    half = CX // 2
    for i in range(half):
        both = [brick_ref[j * CY : (j + 1) * CY, :] for j in (i, i + half)]
        sent_ref[pl.ds(i, NZ, stride=half), :] = jnp.concatenate(both, axis=0).T


def join(source, *faces):
    return pl.pallas_call(
        join_kernel,
        out_shape=(
            jax.ShapeDtypeStruct(source.shape, jnp.float32),
            jax.ShapeDtypeStruct((NZ * CX // 2, 2 * CY), jnp.float32),
        ),
        in_specs=[VMEM] * 5,
        out_specs=(VMEM, VMEM),
        compiler_params=LIMIT,
        name="join",
    )(source, *faces)


def along_slabs(to_next, to_previous):
    devices = lax.axis_size(EVERY)
    up = [(i, i + 1) for i in range(devices - 1)]
    down = [(j, i) for i, j in up]
    return lax.ppermute(to_next, EVERY, up), lax.ppermute(to_previous, EVERY, down)


def exchange(value):
    return lax.all_to_all(value, EVERY, split_axis=0, concat_axis=0, tiled=True)


def x_slab_source(brick):
    second_count = lax.axis_size("by")
    mine = lax.axis_index("by")
    brick = brick.reshape(CX, CY, NZ)
    thick = CX // second_count
    slab = jnp.zeros((thick, second_count * CY, NZ), jnp.float32)
    for turn in range(second_count):
        partner = mine ^ turn
        piece = lax.dynamic_slice_in_dim(brick, partner * thick, thick, 0)
        if turn:
            piece = lax.ppermute(piece, "by", [(i, i ^ turn) for i in range(second_count)])
        slab = lax.dynamic_update_slice_in_dim(slab, piece, partner * CY, 1)
    before, after = along_slabs(slab[-1:], slab[:1])
    return jnp.concatenate([before, slab, after], axis=0)


def relax(brick, sent, levels, rows_inverse, columns_inverse, depth_inverse):
    first_count, second_count = lax.axis_size("bx"), lax.axis_size("by")
    devices = first_count * second_count
    me = lax.axis_index(EVERY)
    nx, ny = first_count * CX, second_count * CY
    thick = (NZ // devices, ny // devices, nx // devices)
    diagonal = 6.0 + screen_base * (1.0 + levels.reshape(first_count, second_count))
    diagonal = jnp.repeat(jnp.repeat(diagonal, CX, 0), CY, 1)
    padded = jnp.pad(diagonal, ((1, 1), (1, 1)), constant_values=1.0)
    diagonals = (
        diagonal[None],
        lax.dynamic_slice_in_dim(padded, me * thick[1], thick[1] + 2, 1).T[:, None, 1:-1],
        lax.dynamic_slice_in_dim(padded, me * thick[2], thick[2] + 2, 0)[:, 1:-1, None],
    )
    edges = jnp.stack([me > 0, me < devices - 1]).astype(jnp.float32)
    matrices = (rows_inverse, columns_inverse, depth_inverse)
    held, slab, diagonals = lax.optimization_barrier((exchange(sent), x_slab_source(brick), diagonals))
    blocks = held.reshape(devices, thick[0], CX // 2, 2 * CY)
    before, after = along_slabs(
        blocks[:, -1].reshape(-1, 2 * CY), blocks[:, 0].reshape(-1, 2 * CY)
    )
    sent, z_source = first_phase(
        (first_count, second_count, thick[0], thick[1]), held, before, after, diagonals[0], matrices[0], matrices[1]
    )
    sources = [z_source, None, slab]
    for step in range(1, 3 * ITERS // 2):
        at = step % 3
        planes, rows = thick[at], thick[(at + 2) % 3]
        held = exchange(sent)
        bands = matrices[(2 * step + 1) % 3].shape[1] // 128
        blocks = held.reshape(devices, -1, bands, planes * rows, 128)
        to_next, to_previous = blocks[:, -1, :, -2 * rows :], blocks[:, -1, :, : 2 * rows]
        if sources[at] is None:
            to_next = jnp.concatenate([blocks[:, 0, :, -rows:], to_next], axis=2)
            to_previous = jnp.concatenate([blocks[:, 0, :, :rows], to_previous], axis=2)
        before, after = along_slabs(to_next.reshape(-1, 128), to_previous.reshape(-1, 128))
        out = later_phase(
            devices,
            planes,
            rows,
            edges,
            held,
            before,
            after,
            diagonals[at],
            matrices[2 * step % 3],
            matrices[(2 * step + 1) % 3],
            source=sources[at],
            last=step + 1 == 3 * ITERS // 2,
        )
        sent = out[0]
        if sources[at] is None:
            sources[at] = out[1]
    sent = sent.reshape(second_count * thick[2], CY, NZ)
    return lax.all_to_all(sent, "by", split_axis=0, concat_axis=0, tiled=True)


def local(normals, owners, cells, levels, rows_inverse, columns_inverse, depth_inverse):
    bricks = lax.axis_size(EVERY)
    point_count = cells.shape[0]
    capacity = 2 * point_count // bricks
    chunks = bricks * capacity // 128
    level = jnp.broadcast_to(levels.astype(jnp.float32)[None], (bricks, 1, 128))
    levels = exchange(level)[:, 0, 0]
    send, rank = pack(owners, cells, normals, bricks, capacity)
    send, levels = lax.optimization_barrier((send, levels))
    held = lax.all_to_all(send, EVERY, split_axis=0, concat_axis=0, tiled=True)
    field = held.reshape(bricks, 4, capacity).transpose(1, 0, 2).reshape(4 * chunks, 128)
    cell_rows = field[3 * chunks :]
    used = (jnp.max(cell_rows, axis=1) > 0).astype(jnp.int32)
    source, x_face, y_face = splat(field, used)
    x_before, x_after = neighbours(x_face, "bx", CY)
    y_before, y_after = neighbours(y_face, "by", CX)
    brick, sent = join(source, x_before, x_after, y_before, y_after)
    iterate = relax(brick, sent, levels, rows_inverse, columns_inverse, depth_inverse)
    sampled = sample(cell_rows, iterate.reshape(CX * CY, NZ))
    returned = lax.all_to_all(sampled.reshape(bricks, capacity), EVERY, split_axis=0, concat_axis=0, tiled=True)
    implicit = unpack(owners, rank, returned)
    return (iterate, implicit)


def solution(mesh):
    placed = (
        P(None, ("bx", "by")),
        P(("bx", "by"), None),
        P(("bx", "by")),
        P("bx", "by"),
        P(),
        P(),
        P(),
    )
    return jax.shard_map(
        local,
        mesh=mesh,
        in_specs=placed,
        out_specs=(P("bx", "by", None), P(("bx", "by"))),
        check_vma=False,
    )
```

```python
import functools

import jax
import jax.numpy as jnp
from jax import lax
from jax.experimental import pallas as pl
from jax.experimental.pallas import tpu as pltpu
from jax.sharding import PartitionSpec as P

CX = 16
CY = 64
NZ = 256
ITERS = 4
EVERY = ("bx", "by")


screen_base = 1.0


def parts_of(value, count):
    parts = []
    for _ in range(count):
        part = value.astype(jnp.bfloat16)
        parts.append(part)
        value = value - part.astype(jnp.float32)
    return parts


def rows_iota(rows, columns):
    return lax.broadcasted_iota(jnp.int32, (rows, columns), 0)


def flags(condition):
    return jnp.where(condition, 1.0, 0.0)


def whole_arrays(count):
    return [pl.BlockSpec(memory_space=pltpu.VMEM)] * count


def pack_kernel(level_ref, owner_ref, cell_ref, normal_ref, send_ref, rank_ref, total_ref):
    bricks, capacity = send_ref.shape[0], total_ref.shape[1]
    points = owner_ref.shape[1]
    block = 256
    before = flags(rows_iota(block, block) < lax.broadcasted_iota(jnp.int32, (block, block), 1)).astype(jnp.bfloat16)
    total_ref[...] = jnp.zeros_like(total_ref)

    def step(at, seen):
        here = pl.ds(pl.multiple_of(at * block, block), block)
        named = flags(rows_iota(bricks, block) == owner_ref[:, here])
        inside = jnp.dot(named.astype(jnp.bfloat16), before, preferred_element_type=jnp.float32)
        rank = jnp.sum(named * (inside + seen), axis=0, keepdims=True)
        rank_ref[:, here] = rank
        slot = flags(rows_iota(capacity, block).astype(jnp.float32) == rank).astype(jnp.bfloat16)
        values = []
        for k in range(3):
            values += [part.astype(jnp.float32) for part in parts_of(normal_ref[k : k + 1, here], 3)]
        cell = cell_ref[:, here] + 1
        for shift in (16, 8, 0):
            values.append(((cell >> shift) & 255).astype(jnp.float32))
        rows = jnp.concatenate([(named * value).astype(jnp.bfloat16) for value in values], axis=0)
        total_ref[...] += lax.dot_general(
            rows, slot, (((1,), (1,)), ((), ())), preferred_element_type=jnp.float32
        )
        return seen + jnp.sum(named, axis=1, keepdims=True)

    lax.fori_loop(0, points // block, step, jnp.zeros((bricks, 1), jnp.float32))
    part = lambda i: total_ref[i * bricks : (i + 1) * bricks, :]
    fields = [part(3 * k) + part(3 * k + 1) + part(3 * k + 2) for k in range(3)]
    fields.append(part(9) * 65536.0 + part(10) * 256.0 + part(11))
    row = jnp.concatenate(fields, axis=1)
    used = row.shape[1] // 128
    for j in range(used):
        send_ref[:, j, :] = row[:, 128 * j : 128 * (j + 1)]
    level = jnp.full((bricks, send_ref.shape[1] - used, 128), level_ref[0, 0])
    send_ref[:, used:, :] = level.astype(jnp.float32)


def pack(owners, cells, normals, levels, bricks, capacity):
    points = cells.shape[0]
    return pl.pallas_call(
        pack_kernel,
        out_shape=(
            jax.ShapeDtypeStruct((bricks, 4 * capacity // 128 // 8 * 8 + 8, 128), jnp.float32),
            jax.ShapeDtypeStruct((1, points), jnp.float32),
        ),
        in_specs=[pl.BlockSpec(memory_space=pltpu.SMEM)] + whole_arrays(3),
        out_specs=tuple(whole_arrays(2)),
        scratch_shapes=[pltpu.VMEM((12 * bricks, capacity), jnp.float32)],
        compiler_params=pltpu.CompilerParams(vmem_limit_bytes=32 << 20),
        name="pack",
    )(levels, owners.reshape(1, points), cells.reshape(1, points), normals)


def unpack_kernel(owner_ref, rank_ref, held_ref, out_ref):
    bricks, capacity = held_ref.shape
    points = owner_ref.shape[1]
    block = 512
    held = jnp.concatenate([part.astype(jnp.float32).T for part in parts_of(held_ref[...], 3)], axis=1)
    held = held.astype(jnp.bfloat16)
    for at in range(points // block):
        here = slice(at * block, (at + 1) * block)
        named = flags(rows_iota(bricks, block) == owner_ref[:, here]).astype(jnp.bfloat16)
        named = jnp.concatenate([named] * 3, axis=0)
        found = jnp.dot(held, named, preferred_element_type=jnp.float32)
        slot = rows_iota(capacity, block).astype(jnp.float32) == rank_ref[:, here]
        out_ref[:, here] = jnp.sum(jnp.where(slot, found, 0.0), axis=0, keepdims=True)


def unpack(owners, rank, held):
    points = owners.shape[0]
    out = pl.pallas_call(
        unpack_kernel,
        out_shape=jax.ShapeDtypeStruct((1, points), jnp.float32),
        in_specs=whole_arrays(3),
        out_specs=pl.BlockSpec(memory_space=pltpu.VMEM),
        compiler_params=pltpu.CompilerParams(vmem_limit_bytes=32 << 20),
        name="unpack",
    )(owners.reshape(1, points), rank, held)
    return out.reshape(points)


def spread(row):
    return jnp.broadcast_to(row, (16, 128)).astype(jnp.bfloat16)


def times_row(table, row16):
    rows = table.shape[0]
    return (table.reshape(rows // 16, 16, 128) * row16[None]).reshape(rows, 128)


def places(cell_row):
    cell = cell_row.astype(jnp.int32) - 1
    return cell >> 14, (cell >> 8) & (CY - 1), cell & (NZ - 1)


def differenced(rows, first, at):
    index = rows_iota(rows, 128) + first
    return jnp.where(index == at + 1, 0.5, 0.0) - jnp.where(index == at - 1, 0.5, 0.0)


def splat_kernel(used_ref, field_ref, source_ref, x_face_ref, y_face_ref):
    chunks = field_ref.shape[0] // 4
    source_ref[...] = jnp.zeros_like(source_ref)
    x_face_ref[...] = jnp.zeros_like(x_face_ref)
    y_face_ref[...] = jnp.zeros_like(y_face_ref)

    def product(rows, columns):
        return lax.dot_general(rows, columns, (((1,), (1,)), ((), ())), preferred_element_type=jnp.float32)

    group = 4

    def tables(at):
        x, y, z = places(field_ref[pl.ds(3 * chunks + at, 1), :])
        y_hot = flags(rows_iota(CY, 128) == y).astype(jnp.bfloat16)
        y_step = differenced(CY, 0, y).astype(jnp.bfloat16)
        z_hot = flags(rows_iota(NZ, 128) == z).astype(jnp.bfloat16)
        z_step = differenced(NZ, 0, z).astype(jnp.bfloat16)
        columns = []
        for k in range(3):
            for part in parts_of(field_ref[pl.ds(k * chunks + at, 1), :], 2):
                columns.append(times_row(z_step if k == 2 else z_hot, spread(part.astype(jnp.float32))))
        steps = [spread(jnp.where(x == i - 1, 0.5, 0.0) - jnp.where(x == i + 1, 0.5, 0.0)) for i in range(-1, CX + 1)]
        hots = [spread(flags(x == i)) for i in range(CX)]
        along_x = jnp.concatenate([times_row(y_hot, steps[i + 1]) for i in range(CX)], axis=0)
        along_y = jnp.concatenate([times_row(y_step, hots[i]) for i in range(CX)], axis=0)
        along_z = jnp.concatenate([times_row(y_hot, hots[i]) for i in range(CX)], axis=0)
        ends_x = jnp.concatenate([times_row(y_hot, steps[0]), times_row(y_hot, steps[CX + 1])], axis=0)
        x_hot = flags(rows_iota(CX, 128) == x).astype(jnp.bfloat16)
        ends_y = jnp.concatenate(
            [x_hot * spread(jnp.where(y == 0, -0.5, 0.0)), x_hot * spread(jnp.where(y == CY - 1, 0.5, 0.0))], axis=0
        )
        return columns, along_x, along_y, along_z, ends_x, ends_y

    def step(at, carry):
        total = used_ref[group * at]
        for g in range(1, group):
            total += used_ref[group * at + g]
        @pl.when(total > 0)
        def _():
            cols, rows, cx, ex, cy, ey = [], [], [], [], [], []
            for g in range(group):
                c, ax, ay, az, e_x, e_y = tables(group * at + g)
                cols += c
                rows += [ax, ax, ay, ay, az, az]
                cx += c[:2]; ex += [e_x, e_x]; cy += c[2:4]; ey += [e_y, e_y]
            cat = lambda v: jnp.concatenate(v, axis=1)
            source_ref[...] += product(cat(rows), cat(cols))
            x_face_ref[...] += product(cat(ex), cat(cx))
            y_face_ref[...] += product(cat(ey), cat(cy))

        return carry

    lax.fori_loop(0, chunks // group, step, 0)


def splat(field, used):
    shapes = ((CX * CY, NZ), (2 * CY, NZ), (2 * CX, NZ))
    return pl.pallas_call(
        splat_kernel,
        out_shape=tuple(jax.ShapeDtypeStruct(shape, jnp.float32) for shape in shapes),
        in_specs=[pl.BlockSpec(memory_space=pltpu.SMEM), pl.BlockSpec(memory_space=pltpu.VMEM)],
        out_specs=tuple(whole_arrays(3)),
        compiler_params=pltpu.CompilerParams(vmem_limit_bytes=32 << 20),
        name="splat",
    )(used, field)


def sample_kernel(field_ref, iterate_ref, out_ref, turned_ref):
    chunks = out_ref.shape[0]
    for i in range(CX * CY // 128):
        here = slice(128 * i, 128 * (i + 1))
        block = iterate_ref[here, :].T
        high, low = parts_of(block, 2)
        turned_ref[:NZ, here] = high
        turned_ref[NZ:, here] = low

    def step(at, carry):
        tables, heights = [], []
        for half in range(2):
            x, y, z = places(field_ref[pl.ds(2 * at + half, 1), :])
            y_hot = flags(rows_iota(CY, 128) == y).astype(jnp.bfloat16)
            hots = [spread(flags(x == i)) for i in range(CX)]
            tables.append(jnp.concatenate([times_row(y_hot, hots[i]) for i in range(CX)], axis=0))
            heights.append(z)
        found = jnp.dot(turned_ref[...], jnp.concatenate(tables, axis=1), preferred_element_type=jnp.float32)
        found = found[:NZ] + found[NZ:]
        level = rows_iota(NZ, 256) == jnp.concatenate(heights, axis=1)
        row = jnp.sum(jnp.where(level, found, 0.0), axis=0, keepdims=True)
        out_ref[pl.ds(2 * at, 1), :] = row[:, :128]
        out_ref[pl.ds(2 * at + 1, 1), :] = row[:, 128:]
        return carry

    lax.fori_loop(0, chunks // 2, step, 0, unroll=4)


def sample(cell_rows, iterate):
    return pl.pallas_call(
        sample_kernel,
        out_shape=jax.ShapeDtypeStruct(cell_rows.shape, jnp.float32),
        in_specs=whole_arrays(2),
        out_specs=pl.BlockSpec(memory_space=pltpu.VMEM),
        scratch_shapes=[pltpu.VMEM((2 * NZ, CX * CY), jnp.bfloat16)],
        compiler_params=pltpu.CompilerParams(vmem_limit_bytes=32 << 20),
        name="sample",
    )(cell_rows, iterate)


def neighbours(face, axis, count):
    peers = lax.axis_size(axis)
    up = [(i, i + 1) for i in range(peers - 1)]
    down = [(j, i) for i, j in up]
    return lax.ppermute(face[count:], axis, up), lax.ppermute(face[:count], axis, down)


def parts_in_rows(value):
    high, low = parts_of(value, 2)
    return jnp.concatenate([high, low, high], axis=0)


def wide(matrix):
    high, low = parts_of(matrix, 2)
    return jnp.concatenate([high, high, low], axis=1)


def shifted(value, axis, back):
    length = value.shape[axis]
    moved = pltpu.roll(value, length - 1 if back else 1, axis)
    index = lax.broadcasted_iota(jnp.int32, value.shape, axis)
    return jnp.where(index == (length - 1 if back else 0), 0.0, moved)


def remainder_of(source, before, middle, after, diagonal):
    beside = before + after
    beside = beside + shifted(middle, 0, False) + shifted(middle, 0, True)
    beside = beside + shifted(middle, 1, False) + shifted(middle, 1, True)
    return source - (diagonal * middle - beside)


def pieces(ref, sources, per_source, start, rows, bands, per_band):
    columns = []
    for band in range(bands):
        starts = [i * per_source + band * per_band + start for i in range(sources)]
        columns.append(jnp.concatenate([ref[at : at + rows, :] for at in starts], axis=0))
    return jnp.concatenate(columns, axis=1)


def put(sent_ref, k, planes, targets, per_block, start, value):
    turned = value.T
    per_target = turned.shape[0] // targets
    for j in range(targets):
        for band in range(turned.shape[1] // 128):
            at = j * per_block + start + band * per_target * planes + k
            part = turned[j * per_target : (j + 1) * per_target, band * 128 : (band + 1) * 128]
            sent_ref[pl.ds(at, per_target, stride=planes), :] = part


def brick_planes(ref, first_count, second_count, planes, k):
    bands = []
    lane = lax.broadcasted_iota(jnp.int32, (8, 128), 1)
    for i in range(first_count):
        tiles = []
        for j in range(second_count):
            start = ((i * second_count + j) * planes + k) * 8
            tiles.append(ref[start : start + 8, :])
        turned = [pltpu.roll(tile, 64, 1) for tile in tiles]
        pairs = range(0, second_count, 2)
        bands.append(jnp.concatenate([jnp.where(lane < 64, tiles[j], turned[j + 1]) for j in pairs], axis=1))
        bands.append(jnp.concatenate([jnp.where(lane < 64, turned[j], tiles[j + 1]) for j in pairs], axis=1))
    return jnp.concatenate(bands, axis=0)


def sweep_all(count, step_ref, source_ref, diagonal_ref, matrix_ref, emit):
    matrix = wide(matrix_ref[...])
    for k in range(count):
        diagonal = diagonal_ref[0 if diagonal_ref.shape[0] == 1 else k + 1]
        middle = step_ref[k + 1]
        remainder = remainder_of(source_ref[k + 1], step_ref[k], middle, step_ref[k + 2], diagonal)
        high, low = parts_of(remainder, 2)
        row = jnp.concatenate([high, low, high], axis=1)
        step = lax.dot_general(row, matrix, (((1,), (1,)), ((), ())), preferred_element_type=jnp.float32)
        emit(k, middle + step)


def first_kernel(
    grid, held_ref, before_ref, after_ref, diagonal_ref, first_ref, second_ref, sent_ref, source_ref, step_ref
):
    first_count, second_count, planes, per_target = grid
    for k in range(planes):
        source_ref[k + 1] = brick_planes(held_ref, first_count, second_count, planes, k)
    source_ref[0] = brick_planes(before_ref, first_count, second_count, 1, 0)
    source_ref[planes + 1] = brick_planes(after_ref, first_count, second_count, 1, 0)
    first = wide(first_ref[...])
    for k in range(planes + 2):
        step_ref[k] = jnp.dot(first, parts_in_rows(source_ref[k]), preferred_element_type=jnp.float32)
    devices = first_count * second_count
    block = sent_ref.shape[0] // devices

    def emit(k, value):
        put(sent_ref, k, planes, devices, block, 0, source_ref[k + 1])
        put(sent_ref, k, planes, devices, block, block // 2, value)

    sweep_all(planes, step_ref, source_ref, diagonal_ref, second_ref, emit)


def later_kernel(
    shape, edge_ref, held_ref, before_ref, after_ref, diagonal_ref, first_ref, second_ref, *refs
):
    devices, planes, rows, with_source, last = shape
    if with_source:
        sent_ref, source_ref, iterate_ref, step_ref = refs
    else:
        source_ref, sent_ref, iterate_ref, step_ref = refs
    bands = iterate_ref.shape[2] // 128
    block, edge_block = held_ref.shape[0] // devices, before_ref.shape[0] // devices
    per_band = planes * rows
    edge_band = edge_block // bands
    own = lambda k, start: pieces(held_ref, devices, block, start + k * rows, rows, bands, per_band)
    edge = lambda ref, k: pieces(ref, devices, edge_block, k * rows, rows, bands, edge_band)
    if with_source:
        for k in range(planes):
            source_ref[k + 1] = own(k, 0)
        source_ref[0] = edge(before_ref, 0)
        source_ref[planes + 1] = edge(after_ref, 0)
    for k in range(2):
        iterate_ref[k] = edge(before_ref, k + with_source)
        iterate_ref[planes + 2 + k] = edge(after_ref, k + with_source)
    for k in range(planes):
        iterate_ref[k + 2] = own(k, block // 2 if with_source else 0)
    first = wide(first_ref[...])
    for k in range(planes + 2):
        diagonal = diagonal_ref[0 if diagonal_ref.shape[0] == 1 else k]
        middle = iterate_ref[k + 1]
        remainder = remainder_of(source_ref[k], iterate_ref[k], middle, iterate_ref[k + 2], diagonal)
        step = jnp.dot(first, parts_in_rows(remainder), preferred_element_type=jnp.float32)
        if k == 0:
            step = step * edge_ref[0]
        if k == planes + 1:
            step = step * edge_ref[1]
        step_ref[k] = middle + step

    def emit(k, value):
        if last:
            for j in range(value.shape[0] // CY):
                sent_ref[j, k] = value[j * CY : (j + 1) * CY, :]
        else:
            put(sent_ref, k, planes, devices, sent_ref.shape[0] // devices, 0, value)

    sweep_all(planes, step_ref, source_ref, diagonal_ref, second_ref, emit)


SMEM = pl.BlockSpec(memory_space=pltpu.SMEM)
VMEM = pl.BlockSpec(memory_space=pltpu.VMEM)
LIMIT = pltpu.CompilerParams(vmem_limit_bytes=48 << 20)


def first_phase(grid, held, before, after, diagonal, first, second):
    rows, columns = diagonal.shape[1:]
    first_count, second_count, planes, per_target = grid
    return pl.pallas_call(
        functools.partial(first_kernel, grid),
        out_shape=(
            jax.ShapeDtypeStruct((2 * columns * planes * rows // 128, 128), jnp.float32),
            jax.ShapeDtypeStruct((planes + 2, rows, columns), jnp.float32),
        ),
        in_specs=[VMEM] * 6,
        out_specs=(VMEM, VMEM),
        scratch_shapes=[pltpu.VMEM((planes + 2, rows, columns), jnp.float32)],
        compiler_params=LIMIT,
        name="first_phase",
    )(held, before, after, diagonal, first, second)


def later_phase(devices, planes, rows, edges, held, before, after, diagonal, first, second, source=None, last=False):
    columns = second.shape[1]
    length = devices * rows
    if last:
        sent = (length // CY, planes, CY, columns)
    else:
        sent = (columns * planes * length // 128, 128)
    out = [jax.ShapeDtypeStruct(sent, jnp.float32)]
    operands = [edges, held, before, after, diagonal, first, second]
    if source is None:
        out.append(jax.ShapeDtypeStruct((planes + 2, length, columns), jnp.float32))
    else:
        operands.append(source)
    return pl.pallas_call(
        functools.partial(later_kernel, (devices, planes, rows, source is None, last)),
        out_shape=tuple(out),
        in_specs=[SMEM] + [VMEM] * (len(operands) - 1),
        out_specs=tuple([VMEM] * len(out)),
        scratch_shapes=[
            pltpu.VMEM((planes + 4, length, columns), jnp.float32),
            pltpu.VMEM((planes + 2, length, columns), jnp.float32),
        ],
        compiler_params=LIMIT,
        name="later_phase",
    )(*operands)


def join_kernel(source_ref, x_before_ref, x_after_ref, y_before_ref, y_after_ref, brick_ref, sent_ref):
    for i in range(CX):
        here = slice(i * CY, (i + 1) * CY)
        value = source_ref[here, :]
        if i == 0:
            value = value + x_before_ref[...]
        if i == CX - 1:
            value = value + x_after_ref[...]
        row = rows_iota(CY, NZ)
        value = value + jnp.where(row == 0, y_before_ref[i : i + 1, :], 0.0)
        brick_ref[here, :] = value + jnp.where(row == CY - 1, y_after_ref[i : i + 1, :], 0.0)
    half = CX // 2
    for i in range(half):
        both = [brick_ref[j * CY : (j + 1) * CY, :] for j in (i, i + half)]
        sent_ref[pl.ds(i, NZ, stride=half), :] = jnp.concatenate(both, axis=0).T


def join(source, *faces):
    return pl.pallas_call(
        join_kernel,
        out_shape=(
            jax.ShapeDtypeStruct(source.shape, jnp.float32),
            jax.ShapeDtypeStruct((NZ * CX // 2, 2 * CY), jnp.float32),
        ),
        in_specs=[VMEM] * 5,
        out_specs=(VMEM, VMEM),
        compiler_params=LIMIT,
        name="join",
    )(source, *faces)


def along_slabs(to_next, to_previous):
    devices = lax.axis_size(EVERY)
    up = [(i, i + 1) for i in range(devices - 1)]
    down = [(j, i) for i, j in up]
    return lax.ppermute(to_next, EVERY, up), lax.ppermute(to_previous, EVERY, down)


def exchange(value):
    return lax.all_to_all(value, EVERY, split_axis=0, concat_axis=0, tiled=True)


def x_slab_source(brick):
    second_count = lax.axis_size("by")
    mine = lax.axis_index("by")
    brick = brick.reshape(CX, CY, NZ)
    thick = CX // second_count
    slab = jnp.zeros((thick, second_count * CY, NZ), jnp.float32)
    for turn in range(second_count):
        partner = mine ^ turn
        piece = lax.dynamic_slice_in_dim(brick, partner * thick, thick, 0)
        if turn:
            piece = lax.ppermute(piece, "by", [(i, i ^ turn) for i in range(second_count)])
        slab = lax.dynamic_update_slice_in_dim(slab, piece, partner * CY, 1)
    before, after = along_slabs(slab[-1:], slab[:1])
    return jnp.concatenate([before, slab, after], axis=0)


def relax(brick, sent, levels, rows_inverse, columns_inverse, depth_inverse):
    first_count, second_count = lax.axis_size("bx"), lax.axis_size("by")
    devices = first_count * second_count
    me = lax.axis_index(EVERY)
    nx, ny = first_count * CX, second_count * CY
    thick = (NZ // devices, ny // devices, nx // devices)
    diagonal = 6.0 + screen_base * (1.0 + levels.reshape(first_count, second_count))
    diagonal = jnp.repeat(jnp.repeat(diagonal, CX, 0), CY, 1)
    padded = jnp.pad(diagonal, ((1, 1), (1, 1)), constant_values=1.0)
    diagonals = (
        diagonal[None],
        lax.dynamic_slice_in_dim(padded, me * thick[1], thick[1] + 2, 1).T[:, None, 1:-1],
        lax.dynamic_slice_in_dim(padded, me * thick[2], thick[2] + 2, 0)[:, 1:-1, None],
    )
    edges = jnp.stack([me > 0, me < devices - 1]).astype(jnp.float32)
    matrices = (rows_inverse, columns_inverse, depth_inverse)
    held, diagonals = lax.optimization_barrier((exchange(sent), diagonals))
    blocks = held.reshape(devices, thick[0], CX // 2, 2 * CY)
    before, after = along_slabs(
        blocks[:, -1].reshape(-1, 2 * CY), blocks[:, 0].reshape(-1, 2 * CY)
    )
    sent, z_source = first_phase(
        (first_count, second_count, thick[0], thick[1]), held, before, after, diagonals[0], matrices[0], matrices[1]
    )
    sources = [z_source, None, None]
    for step in range(1, 3 * ITERS // 2):
        at = step % 3
        planes, rows = thick[at], thick[(at + 2) % 3]
        held = exchange(sent)
        if step == 1:
            held, sources[2] = lax.optimization_barrier((held, x_slab_source(brick)))
        bands = matrices[(2 * step + 1) % 3].shape[1] // 128
        blocks = held.reshape(devices, -1, bands, planes * rows, 128)
        to_next, to_previous = blocks[:, -1, :, -2 * rows :], blocks[:, -1, :, : 2 * rows]
        if sources[at] is None:
            to_next = jnp.concatenate([blocks[:, 0, :, -rows:], to_next], axis=2)
            to_previous = jnp.concatenate([blocks[:, 0, :, :rows], to_previous], axis=2)
        before, after = along_slabs(to_next.reshape(-1, 128), to_previous.reshape(-1, 128))
        out = later_phase(
            devices,
            planes,
            rows,
            edges,
            held,
            before,
            after,
            diagonals[at],
            matrices[2 * step % 3],
            matrices[(2 * step + 1) % 3],
            source=sources[at],
            last=step + 1 == 3 * ITERS // 2,
        )
        sent = out[0]
        if sources[at] is None:
            sources[at] = out[1]
    sent = sent.reshape(second_count * thick[2], CY, NZ)
    return lax.all_to_all(sent, "by", split_axis=0, concat_axis=0, tiled=True)


def local(normals, owners, cells, levels, rows_inverse, columns_inverse, depth_inverse):
    bricks = lax.axis_size(EVERY)
    point_count = cells.shape[0]
    capacity = 2 * point_count // bricks
    chunks = bricks * capacity // 128
    send, rank = pack(owners, cells, normals, levels, bricks, capacity)
    held = exchange(send)
    levels = held[:, 4 * capacity // 128, 0]
    field = held[:, : 4 * capacity // 128].reshape(bricks, 4, capacity).transpose(1, 0, 2).reshape(4 * chunks, 128)
    cell_rows = field[3 * chunks :]
    used = (jnp.max(cell_rows, axis=1) > 0).astype(jnp.int32)
    source, x_face, y_face = splat(field, used)
    x_before, x_after = neighbours(x_face, "bx", CY)
    y_before, y_after = neighbours(y_face, "by", CX)
    brick, sent = join(source, x_before, x_after, y_before, y_after)
    iterate = relax(brick, sent, levels, rows_inverse, columns_inverse, depth_inverse)
    sampled = sample(cell_rows, iterate.reshape(CX * CY, NZ))
    returned = lax.all_to_all(sampled.reshape(bricks, capacity), EVERY, split_axis=0, concat_axis=0, tiled=True)
    implicit = unpack(owners, rank, returned)
    return (iterate, implicit)


def solution(mesh):
    placed = (
        P(None, ("bx", "by")),
        P(("bx", "by"), None),
        P(("bx", "by")),
        P("bx", "by"),
        P(),
        P(),
        P(),
    )
    return jax.shard_map(
        local,
        mesh=mesh,
        in_specs=placed,
        out_specs=(P("bx", "by", None), P(("bx", "by"))),
        check_vma=False,
    )
```

```python
import functools

import jax
import jax.numpy as jnp
from jax import lax
from jax.experimental import pallas as pl
from jax.experimental.pallas import tpu as pltpu
from jax.sharding import PartitionSpec as P

CX = 16
CY = 64
NZ = 256
ITERS = 4
EVERY = ("bx", "by")


screen_base = 1.0


def parts_of(value, count):
    parts = []
    for _ in range(count):
        part = value.astype(jnp.bfloat16)
        parts.append(part)
        value = value - part.astype(jnp.float32)
    return parts


def rows_iota(rows, columns):
    return lax.broadcasted_iota(jnp.int32, (rows, columns), 0)


def flags(condition):
    return jnp.where(condition, 1.0, 0.0)


def whole_arrays(count):
    return [pl.BlockSpec(memory_space=pltpu.VMEM)] * count


def pack_kernel(level_ref, owner_ref, cell_ref, normal_ref, send_ref, rank_ref, total_ref):
    bricks, capacity = send_ref.shape[0], total_ref.shape[1]
    points = owner_ref.shape[1]
    block = 256
    before = flags(rows_iota(block, block) < lax.broadcasted_iota(jnp.int32, (block, block), 1)).astype(jnp.bfloat16)
    total_ref[...] = jnp.zeros_like(total_ref)

    def step(at, seen):
        here = pl.ds(pl.multiple_of(at * block, block), block)
        named = flags(rows_iota(bricks, block) == owner_ref[:, here])
        inside = jnp.dot(named.astype(jnp.bfloat16), before, preferred_element_type=jnp.float32)
        rank = jnp.sum(named * (inside + seen), axis=0, keepdims=True)
        rank_ref[:, here] = rank
        slot = flags(rows_iota(capacity, block).astype(jnp.float32) == rank).astype(jnp.bfloat16)
        values = []
        for k in range(3):
            values += [part.astype(jnp.float32) for part in parts_of(normal_ref[k : k + 1, here], 3)]
        cell = cell_ref[:, here] + 1
        for shift in (16, 8, 0):
            values.append(((cell >> shift) & 255).astype(jnp.float32))
        rows = jnp.concatenate([(named * value).astype(jnp.bfloat16) for value in values], axis=0)
        total_ref[...] += lax.dot_general(
            rows, slot, (((1,), (1,)), ((), ())), preferred_element_type=jnp.float32
        )
        return seen + jnp.sum(named, axis=1, keepdims=True)

    lax.fori_loop(0, points // block, step, jnp.zeros((bricks, 1), jnp.float32))
    part = lambda i: total_ref[i * bricks : (i + 1) * bricks, :]
    fields = [part(3 * k) + part(3 * k + 1) + part(3 * k + 2) for k in range(3)]
    fields.append(part(9) * 65536.0 + part(10) * 256.0 + part(11))
    row = jnp.concatenate(fields, axis=1)
    used = row.shape[1] // 128
    for j in range(used):
        send_ref[:, j, :] = row[:, 128 * j : 128 * (j + 1)]
    level = jnp.full((bricks, send_ref.shape[1] - used, 128), level_ref[0, 0])
    send_ref[:, used:, :] = level.astype(jnp.float32)


def pack(owners, cells, normals, levels, bricks, capacity):
    points = cells.shape[0]
    return pl.pallas_call(
        pack_kernel,
        out_shape=(
            jax.ShapeDtypeStruct((bricks, 4 * capacity // 128 // 8 * 8 + 8, 128), jnp.float32),
            jax.ShapeDtypeStruct((1, points), jnp.float32),
        ),
        in_specs=[pl.BlockSpec(memory_space=pltpu.SMEM)] + whole_arrays(3),
        out_specs=tuple(whole_arrays(2)),
        scratch_shapes=[pltpu.VMEM((12 * bricks, capacity), jnp.float32)],
        compiler_params=pltpu.CompilerParams(vmem_limit_bytes=32 << 20),
        name="pack",
    )(levels, owners.reshape(1, points), cells.reshape(1, points), normals)


def unpack_kernel(owner_ref, rank_ref, held_ref, out_ref):
    bricks, capacity = held_ref.shape
    points = owner_ref.shape[1]
    block = 512
    held = jnp.concatenate([part.astype(jnp.float32).T for part in parts_of(held_ref[...], 3)], axis=1)
    held = held.astype(jnp.bfloat16)
    for at in range(points // block):
        here = slice(at * block, (at + 1) * block)
        named = flags(rows_iota(bricks, block) == owner_ref[:, here]).astype(jnp.bfloat16)
        named = jnp.concatenate([named] * 3, axis=0)
        found = jnp.dot(held, named, preferred_element_type=jnp.float32)
        slot = rows_iota(capacity, block).astype(jnp.float32) == rank_ref[:, here]
        out_ref[:, here] = jnp.sum(jnp.where(slot, found, 0.0), axis=0, keepdims=True)


def unpack(owners, rank, held):
    points = owners.shape[0]
    out = pl.pallas_call(
        unpack_kernel,
        out_shape=jax.ShapeDtypeStruct((1, points), jnp.float32),
        in_specs=whole_arrays(3),
        out_specs=pl.BlockSpec(memory_space=pltpu.VMEM),
        compiler_params=pltpu.CompilerParams(vmem_limit_bytes=32 << 20),
        name="unpack",
    )(owners.reshape(1, points), rank, held)
    return out.reshape(points)


def spread(row):
    return jnp.broadcast_to(row, (16, 128)).astype(jnp.bfloat16)


def times_row(table, row16):
    rows = table.shape[0]
    return (table.reshape(rows // 16, 16, 128) * row16[None]).reshape(rows, 128)


def places(cell_row):
    cell = cell_row.astype(jnp.int32) - 1
    return cell >> 14, (cell >> 8) & (CY - 1), cell & (NZ - 1)


def differenced(rows, first, at):
    index = rows_iota(rows, 128) + first
    return jnp.where(index == at + 1, 0.5, 0.0) - jnp.where(index == at - 1, 0.5, 0.0)


GROUP = 4


def product(rows, columns):
    rows, columns = jnp.concatenate(rows, axis=1), jnp.concatenate(columns, axis=1)
    return lax.dot_general(rows, columns, (((1,), (1,)), ((), ())), preferred_element_type=jnp.float32)


def columns_of(field_ref, chunks, at, k, table):
    parts = parts_of(field_ref[pl.ds(k * chunks + at, 1), :], 2)
    return [times_row(table, spread(part.astype(jnp.float32))) for part in parts]


def each_group(used_ref, field_ref, body):
    chunks = field_ref.shape[0] // 4

    def step(at, carry):
        members = [GROUP * at + g for g in range(GROUP)]
        used = sum([used_ref[member] for member in members])

        @pl.when(used > 0)
        def _():
            body(chunks, members)

        return carry

    lax.fori_loop(0, chunks // GROUP, step, 0)


def face_kernel(used_ref, field_ref, x_face_ref, y_face_ref):
    x_face_ref[...] = jnp.zeros_like(x_face_ref)
    y_face_ref[...] = jnp.zeros_like(y_face_ref)

    def body(chunks, members):
        x_rows, x_columns, y_rows, y_columns = [], [], [], []
        for at in members:
            x, y, z = places(field_ref[pl.ds(3 * chunks + at, 1), :])
            x_hot = flags(rows_iota(CX, 128) == x).astype(jnp.bfloat16)
            y_hot = flags(rows_iota(CY, 128) == y).astype(jnp.bfloat16)
            z_hot = flags(rows_iota(NZ, 128) == z).astype(jnp.bfloat16)
            ends = [jnp.where(x == 0, -0.5, 0.0), jnp.where(x == CX - 1, 0.5, 0.0)]
            x_rows += [jnp.concatenate([times_row(y_hot, spread(end)) for end in ends], axis=0)] * 2
            ends = [jnp.where(y == 0, -0.5, 0.0), jnp.where(y == CY - 1, 0.5, 0.0)]
            y_rows += [jnp.concatenate([x_hot * spread(end) for end in ends], axis=0)] * 2
            x_columns += columns_of(field_ref, chunks, at, 0, z_hot)
            y_columns += columns_of(field_ref, chunks, at, 1, z_hot)
        x_face_ref[...] += product(x_rows, x_columns)
        y_face_ref[...] += product(y_rows, y_columns)

    each_group(used_ref, field_ref, body)


def splat_kernel(used_ref, field_ref, source_ref):
    source_ref[...] = jnp.zeros_like(source_ref)

    def body(chunks, members):
        rows, columns = [], []
        for at in members:
            x, y, z = places(field_ref[pl.ds(3 * chunks + at, 1), :])
            y_hot = flags(rows_iota(CY, 128) == y).astype(jnp.bfloat16)
            y_step = differenced(CY, 0, y).astype(jnp.bfloat16)
            z_hot = flags(rows_iota(NZ, 128) == z).astype(jnp.bfloat16)
            z_step = differenced(NZ, 0, z).astype(jnp.bfloat16)
            for k in range(3):
                columns += columns_of(field_ref, chunks, at, k, z_step if k == 2 else z_hot)
            steps = [spread(jnp.where(x == i - 1, 0.5, 0.0) - jnp.where(x == i + 1, 0.5, 0.0)) for i in range(CX)]
            hots = [spread(flags(x == i)) for i in range(CX)]
            for table, by_x in ((y_hot, steps), (y_step, hots), (y_hot, hots)):
                rows += [jnp.concatenate([times_row(table, row) for row in by_x], axis=0)] * 2
        source_ref[...] += product(rows, columns)

    each_group(used_ref, field_ref, body)


def splat(kernel, field, used, *rows):
    return pl.pallas_call(
        kernel,
        out_shape=tuple(jax.ShapeDtypeStruct((count, NZ), jnp.float32) for count in rows),
        in_specs=[pl.BlockSpec(memory_space=pltpu.SMEM), pl.BlockSpec(memory_space=pltpu.VMEM)],
        out_specs=tuple(whole_arrays(len(rows))),
        compiler_params=pltpu.CompilerParams(vmem_limit_bytes=32 << 20),
        cost_estimate=pl.CostEstimate(flops=2 * 49152 * NZ * sum(rows), bytes_accessed=4 << 20, transcendentals=0),
        name="splat",
    )(used, field)


def sample_kernel(blocks, flip_ref, field_ref, held_ref, out_ref, iterate_ref, turned_ref):
    chunks = out_ref.shape[0]
    for i in range(CX * CY // 128):
        here = slice(128 * i, 128 * (i + 1))
        per_block = CX * CY // 128 // blocks
        place = i // per_block
        place = jnp.where(flip_ref[0] > 0, blocks - 1 - place, place) * per_block + i % per_block
        block = held_ref[pl.ds(pl.multiple_of(place * 128, 128), 128), :]
        iterate_ref[here, :] = block
        block = block.T
        high, low = parts_of(block, 2)
        turned_ref[:NZ, here] = high
        turned_ref[NZ:, here] = low

    def step(at, carry):
        tables, heights = [], []
        for half in range(2):
            x, y, z = places(field_ref[pl.ds(2 * at + half, 1), :])
            y_hot = flags(rows_iota(CY, 128) == y).astype(jnp.bfloat16)
            hots = [spread(flags(x == i)) for i in range(CX)]
            tables.append(jnp.concatenate([times_row(y_hot, hots[i]) for i in range(CX)], axis=0))
            heights.append(z)
        found = jnp.dot(turned_ref[...], jnp.concatenate(tables, axis=1), preferred_element_type=jnp.float32)
        found = found[:NZ] + found[NZ:]
        level = rows_iota(NZ, 256) == jnp.concatenate(heights, axis=1)
        row = jnp.sum(jnp.where(level, found, 0.0), axis=0, keepdims=True)
        out_ref[pl.ds(2 * at, 1), :] = row[:, :128]
        out_ref[pl.ds(2 * at + 1, 1), :] = row[:, 128:]
        return carry

    lax.fori_loop(0, chunks // 2, step, 0, unroll=4)


def sample(cell_rows, held, flip, blocks):
    shapes = (cell_rows.shape, held.shape)
    return pl.pallas_call(
        functools.partial(sample_kernel, blocks),
        out_shape=tuple(jax.ShapeDtypeStruct(shape, jnp.float32) for shape in shapes),
        in_specs=[pl.BlockSpec(memory_space=pltpu.SMEM)] + whole_arrays(2),
        out_specs=tuple(whole_arrays(2)),
        scratch_shapes=[pltpu.VMEM((2 * NZ, CX * CY), jnp.bfloat16)],
        compiler_params=pltpu.CompilerParams(vmem_limit_bytes=32 << 20),
        name="sample",
    )(flip, cell_rows, held)


def neighbours(face, axis, count):
    peers = lax.axis_size(axis)
    up = [(i, i + 1) for i in range(peers - 1)]
    down = [(j, i) for i, j in up]
    return lax.ppermute(face[count:], axis, up), lax.ppermute(face[:count], axis, down)


def parts_in_rows(value):
    high, low = parts_of(value, 2)
    return jnp.concatenate([high, low, high], axis=0)


def wide(matrix):
    high, low = parts_of(matrix, 2)
    return jnp.concatenate([high, high, low], axis=1)


def shifted(value, axis, back):
    length = value.shape[axis]
    moved = pltpu.roll(value, length - 1 if back else 1, axis)
    index = lax.broadcasted_iota(jnp.int32, value.shape, axis)
    return jnp.where(index == (length - 1 if back else 0), 0.0, moved)


def remainder_of(source, before, middle, after, diagonal):
    beside = before + after
    beside = beside + shifted(middle, 0, False) + shifted(middle, 0, True)
    beside = beside + shifted(middle, 1, False) + shifted(middle, 1, True)
    return source - (diagonal * middle - beside)


def pieces(ref, order, per_source, start, rows, bands, per_band):
    columns = []
    for band in range(bands):
        starts = [i * per_source + band * per_band + start for i in order]
        columns.append(jnp.concatenate([ref[at : at + rows, :] for at in starts], axis=0))
    return jnp.concatenate(columns, axis=1)


def put(sent_ref, k, planes, order, per_block, start, value):
    turned = value.T
    per_target = turned.shape[0] // len(order)
    for j, target in enumerate(order):
        for band in range(turned.shape[1] // 128):
            at = target * per_block + start + band * per_target * planes + k
            part = turned[j * per_target : (j + 1) * per_target, band * 128 : (band + 1) * 128]
            sent_ref[pl.ds(at, per_target, stride=planes), :] = part


def brick_planes(ref, first_count, second_count, planes, k):
    bands = []
    lane = lax.broadcasted_iota(jnp.int32, (8, 128), 1)
    for i in range(first_count):
        tiles = []
        for j in range(second_count):
            start = ((i * second_count + j) * planes + k) * 8
            tiles.append(ref[start : start + 8, :])
        turned = [pltpu.roll(tile, 64, 1) for tile in tiles]
        pairs = range(0, second_count, 2)
        bands.append(jnp.concatenate([jnp.where(lane < 64, tiles[j], turned[j + 1]) for j in pairs], axis=1))
        bands.append(jnp.concatenate([jnp.where(lane < 64, turned[j], tiles[j + 1]) for j in pairs], axis=1))
    return jnp.concatenate(bands, axis=0)


def sweep_all(count, step_ref, source_ref, diagonal_ref, matrix_ref, emit):
    matrix = wide(matrix_ref[...])
    for k in range(count):
        diagonal = diagonal_ref[0 if diagonal_ref.shape[0] == 1 else k + 1]
        middle = step_ref[k + 1]
        remainder = remainder_of(source_ref[k + 1], step_ref[k], middle, step_ref[k + 2], diagonal)
        high, low = parts_of(remainder, 2)
        row = jnp.concatenate([high, low, high], axis=1)
        step = lax.dot_general(row, matrix, (((1,), (1,)), ((), ())), preferred_element_type=jnp.float32)
        emit(k, middle + step)


def first_kernel(
    grid, held_ref, diagonal_ref, first_ref, second_ref, sent_ref, source_ref, step_ref
):
    first_count, second_count, planes, per_target = grid
    for k in range(planes + 2):
        source_ref[k] = brick_planes(held_ref, first_count, second_count, planes + 2, k)
    first = wide(first_ref[...])
    for k in range(planes + 2):
        step_ref[k] = jnp.dot(first, parts_in_rows(source_ref[k]), preferred_element_type=jnp.float32)
    order = slab_order(first_count, second_count)
    block = sent_ref.shape[0] // len(order)

    def emit(k, value):
        put(sent_ref, k, planes, order, block, 0, source_ref[k + 1])
        put(sent_ref, k, planes, order, block, block // 2, value)

    sweep_all(planes, step_ref, source_ref, diagonal_ref, second_ref, emit)


def later_kernel(
    shape, edge_ref, held_ref, pair_ref, other_ref, diagonal_ref, first_ref, second_ref, *refs
):
    order, planes, rows, with_source, last = shape
    devices = len(order)
    even = edge_ref[2] > 0
    if with_source:
        sent_ref, source_ref, iterate_ref, step_ref = refs
    else:
        source_ref, sent_ref, iterate_ref, step_ref = refs
    bands = iterate_ref.shape[2] // 128
    block, edge_block = held_ref.shape[0] // devices, pair_ref.shape[0] // devices
    per_band = planes * rows
    edge_band = edge_block // bands
    own = lambda k, start: pieces(held_ref, order, block, start + k * rows, rows, bands, per_band)

    def edge(after, k):
        pair, other = [pieces(ref, order, edge_block, k * rows, rows, bands, edge_band) for ref in (pair_ref, other_ref)]
        return jnp.where(even, pair, other) if after else jnp.where(even, other, pair)

    if with_source:
        for k in range(planes):
            source_ref[k + 1] = own(k, 0)
        source_ref[0] = edge(False, 0)
        source_ref[planes + 1] = edge(True, 0)
    for k in range(2):
        iterate_ref[k] = edge(False, k + with_source)
        iterate_ref[planes + 2 + k] = edge(True, k + with_source)
    for k in range(planes):
        iterate_ref[k + 2] = own(k, block // 2 if with_source else 0)
    first = wide(first_ref[...])
    for k in range(planes + 2):
        diagonal = diagonal_ref[0 if diagonal_ref.shape[0] == 1 else k]
        middle = iterate_ref[k + 1]
        remainder = remainder_of(source_ref[k], iterate_ref[k], middle, iterate_ref[k + 2], diagonal)
        step = jnp.dot(first, parts_in_rows(remainder), preferred_element_type=jnp.float32)
        if k == 0:
            step = step * edge_ref[0]
        if k == planes + 1:
            step = step * edge_ref[1]
        step_ref[k] = middle + step

    def emit(k, value):
        if last:
            for j in range(value.shape[0] // CY):
                sent_ref[j, k] = value[j * CY : (j + 1) * CY, :]
        else:
            put(sent_ref, k, planes, order, sent_ref.shape[0] // devices, 0, value)

    sweep_all(planes, step_ref, source_ref, diagonal_ref, second_ref, emit)


SMEM = pl.BlockSpec(memory_space=pltpu.SMEM)
VMEM = pl.BlockSpec(memory_space=pltpu.VMEM)
LIMIT = pltpu.CompilerParams(vmem_limit_bytes=48 << 20)


def first_phase(grid, held, diagonal, first, second):
    rows, columns = diagonal.shape[1:]
    first_count, second_count, planes, per_target = grid
    return pl.pallas_call(
        functools.partial(first_kernel, grid),
        out_shape=(
            jax.ShapeDtypeStruct((2 * columns * planes * rows // 128, 128), jnp.float32),
            jax.ShapeDtypeStruct((planes + 2, rows, columns), jnp.float32),
        ),
        in_specs=[VMEM] * 4,
        out_specs=(VMEM, VMEM),
        scratch_shapes=[pltpu.VMEM((planes + 2, rows, columns), jnp.float32)],
        compiler_params=LIMIT,
        name="first_phase",
    )(held, diagonal, first, second)


def later_phase(order, planes, rows, edges, held, pair, other, diagonal, first, second, source=None, last=False):
    columns = second.shape[1]
    length = len(order) * rows
    if last:
        sent = (length // CY, planes, CY, columns)
    else:
        sent = (columns * planes * length // 128, 128)
    out = [jax.ShapeDtypeStruct(sent, jnp.float32)]
    operands = [edges, held, pair, other, diagonal, first, second]
    if source is None:
        out.append(jax.ShapeDtypeStruct((planes + 2, length, columns), jnp.float32))
    else:
        operands.append(source)
    return pl.pallas_call(
        functools.partial(later_kernel, (order, planes, rows, source is None, last)),
        out_shape=tuple(out),
        in_specs=[SMEM] + [VMEM] * (len(operands) - 1),
        out_specs=tuple([VMEM] * len(out)),
        scratch_shapes=[
            pltpu.VMEM((planes + 4, length, columns), jnp.float32),
            pltpu.VMEM((planes + 2, length, columns), jnp.float32),
        ],
        compiler_params=LIMIT,
        name="later_phase",
    )(*operands)


def join_kernel(order, source_ref, x_before_ref, x_after_ref, y_before_ref, y_after_ref, brick_ref, sent_ref, turned_ref):
    for i in range(CX):
        here = slice(i * CY, (i + 1) * CY)
        value = source_ref[here, :]
        if i == 0:
            value = value + x_before_ref[...]
        if i == CX - 1:
            value = value + x_after_ref[...]
        row = rows_iota(CY, NZ)
        value = value + jnp.where(row == 0, y_before_ref[i : i + 1, :], 0.0)
        brick_ref[here, :] = value + jnp.where(row == CY - 1, y_after_ref[i : i + 1, :], 0.0)
    half = CX // 2
    planes = sent_ref.shape[1] // half
    turned_ref[:8, :] = jnp.zeros((8, 2 * CY), jnp.float32)
    turned_ref[NZ + 8 :, :] = jnp.zeros((8, 2 * CY), jnp.float32)
    for i in range(half):
        both = [brick_ref[j * CY : (j + 1) * CY, :] for j in (i, i + half)]
        turned_ref[8 : NZ + 8, :] = jnp.concatenate(both, axis=0).T
        for j, target in enumerate(order):
            first = 7 + j * (planes - 2)
            sent_ref[target, pl.ds(i, planes, stride=half), :] = turned_ref[first : first + planes, :]


def join(source, order, *faces):
    return pl.pallas_call(
        functools.partial(join_kernel, order),
        out_shape=(
            jax.ShapeDtypeStruct(source.shape, jnp.float32),
            jax.ShapeDtypeStruct((len(order), (NZ // len(order) + 2) * CX // 2, 2 * CY), jnp.float32),
        ),
        in_specs=[VMEM] * 5,
        out_specs=(VMEM, VMEM),
        scratch_shapes=[pltpu.VMEM((NZ + 16, 2 * CY), jnp.float32)],
        compiler_params=LIMIT,
        name="join",
    )(source, *faces)


def slab_order(first_count, second_count):
    order = []
    for i in range(first_count):
        row = [i * second_count + j for j in range(second_count)]
        order += row if i % 2 == 0 else row[::-1]
    return order


def place_in_row(j):
    return jnp.where(lax.axis_index("bx") % 2 == 0, j, lax.axis_size("by") - 1 - j)


def beside(to_next, to_previous, even):
    order = slab_order(lax.axis_size("bx"), lax.axis_size("by"))
    got = []
    for start, value in ((0, jnp.where(even, to_next, to_previous)), (1, jnp.where(even, to_previous, to_next))):
        pairs = [(order[i], order[i + 1]) for i in range(start, len(order) - 1, 2)]
        got.append(lax.ppermute(value, EVERY, pairs + [(j, i) for i, j in pairs]))
    return got


def exchange(value):
    return lax.all_to_all(value, EVERY, split_axis=0, concat_axis=0, tiled=True)


def x_slab_source(brick, even):
    second_count = lax.axis_size("by")
    mine = lax.axis_index("by")
    brick = brick.reshape(CX, CY, NZ)
    thick = CX // second_count
    slab = jnp.zeros((thick, second_count * CY, NZ), jnp.float32)
    for turn in range(second_count):
        partner = mine ^ turn
        piece = lax.dynamic_slice_in_dim(brick, place_in_row(partner) * thick, thick, 0)
        if turn:
            piece = lax.ppermute(piece, "by", [(i, i ^ turn) for i in range(second_count)])
        slab = lax.dynamic_update_slice_in_dim(slab, piece, partner * CY, 1)
    pair, other = beside(slab[-1:], slab[:1], even)
    return jnp.concatenate([jnp.where(even, other, pair), slab, jnp.where(even, pair, other)], axis=0)


def relax(brick, sent, levels, rows_inverse, columns_inverse, depth_inverse):
    first_count, second_count = lax.axis_size("bx"), lax.axis_size("by")
    devices = first_count * second_count
    order = slab_order(first_count, second_count)
    me = lax.axis_index("bx") * second_count + place_in_row(lax.axis_index("by"))
    even = me % 2 == 0
    nx, ny = first_count * CX, second_count * CY
    thick = (NZ // devices, ny // devices, nx // devices)
    diagonal = 6.0 + screen_base * (1.0 + levels.reshape(first_count, second_count))
    diagonal = jnp.repeat(jnp.repeat(diagonal, CX, 0), CY, 1)
    padded = jnp.pad(diagonal, ((1, 1), (1, 1)), constant_values=1.0)
    diagonals = (
        diagonal[None],
        lax.dynamic_slice_in_dim(padded, me * thick[1], thick[1] + 2, 1).T[:, None, 1:-1],
        lax.dynamic_slice_in_dim(padded, me * thick[2], thick[2] + 2, 0)[:, 1:-1, None],
    )
    edges = jnp.stack([me > 0, me < devices - 1, even]).astype(jnp.float32)
    matrices = (rows_inverse, columns_inverse, depth_inverse)
    held, diagonals = lax.optimization_barrier((exchange(sent), diagonals))
    sent, z_source = first_phase(
        (first_count, second_count, thick[0], thick[1]), held.reshape(-1, 2 * CY), diagonals[0], matrices[0], matrices[1]
    )
    sources = [z_source, None, None]
    for step in range(1, 3 * ITERS // 2):
        at = step % 3
        planes, rows = thick[at], thick[(at + 2) % 3]
        held = exchange(sent)
        if step == 1:
            held, sources[2] = lax.optimization_barrier((held, x_slab_source(brick, even)))
        bands = matrices[(2 * step + 1) % 3].shape[1] // 128
        blocks = held.reshape(devices, -1, bands, planes * rows, 128)
        to_next, to_previous = blocks[:, -1, :, -2 * rows :], blocks[:, -1, :, : 2 * rows]
        if sources[at] is None:
            to_next = jnp.concatenate([blocks[:, 0, :, -rows:], to_next], axis=2)
            to_previous = jnp.concatenate([blocks[:, 0, :, :rows], to_previous], axis=2)
        pair, other = beside(to_next.reshape(-1, 128), to_previous.reshape(-1, 128), even)
        out = later_phase(
            order,
            planes,
            rows,
            edges,
            held,
            pair,
            other,
            diagonals[at],
            matrices[2 * step % 3],
            matrices[(2 * step + 1) % 3],
            source=sources[at],
            last=step + 1 == 3 * ITERS // 2,
        )
        sent = out[0]
        if sources[at] is None:
            sources[at] = out[1]
    sent = sent.reshape(second_count * thick[2], CY, NZ)
    return lax.all_to_all(sent, "by", split_axis=0, concat_axis=0, tiled=True)


def local(normals, owners, cells, levels, rows_inverse, columns_inverse, depth_inverse):
    bricks = lax.axis_size(EVERY)
    point_count = cells.shape[0]
    capacity = 2 * point_count // bricks
    chunks = bricks * capacity // 128
    send, rank = pack(owners, cells, normals, levels, bricks, capacity)
    held = exchange(send)
    levels = held[:, 4 * capacity // 128, 0]
    field = held[:, : 4 * capacity // 128].reshape(bricks, 4, capacity).transpose(1, 0, 2).reshape(4 * chunks, 128)
    cell_rows = field[3 * chunks :]
    used = (jnp.max(cell_rows, axis=1) > 0).astype(jnp.int32)
    x_face, y_face = splat(face_kernel, field, used, 2 * CY, 2 * CX)
    (source,) = splat(splat_kernel, field, used, CX * CY)
    x_before, x_after = neighbours(x_face, "bx", CY)
    y_before, y_after = neighbours(y_face, "by", CX)
    brick, sent = join(source, slab_order(lax.axis_size("bx"), lax.axis_size("by")), x_before, x_after, y_before, y_after)
    held = relax(brick, sent, levels, rows_inverse, columns_inverse, depth_inverse)
    flip = (lax.axis_index("bx") % 2).astype(jnp.int32).reshape(1)
    sampled, iterate = sample(cell_rows, held.reshape(CX * CY, NZ), flip, lax.axis_size("by"))
    returned = lax.all_to_all(sampled.reshape(bricks, capacity), EVERY, split_axis=0, concat_axis=0, tiled=True)
    implicit = unpack(owners, rank, returned)
    return (iterate.reshape(CX, CY, NZ), implicit)


def solution(mesh):
    placed = (
        P(None, ("bx", "by")),
        P(("bx", "by"), None),
        P(("bx", "by")),
        P("bx", "by"),
        P(),
        P(),
        P(),
    )
    return jax.shard_map(
        local,
        mesh=mesh,
        in_specs=placed,
        out_specs=(P("bx", "by", None), P(("bx", "by"))),
        check_vma=False,
    )
```

```python
import functools

import jax
import jax.numpy as jnp
from jax import lax
from jax.experimental import pallas as pl
from jax.experimental.pallas import tpu as pltpu
from jax.sharding import PartitionSpec as P

CX = 16
CY = 64
NZ = 256
ITERS = 4
EVERY = ("bx", "by")


screen_base = 1.0


def parts_of(value, count):
    parts = []
    for _ in range(count):
        part = value.astype(jnp.bfloat16)
        parts.append(part)
        value = value - part.astype(jnp.float32)
    return parts


def rows_iota(rows, columns):
    return lax.broadcasted_iota(jnp.int32, (rows, columns), 0)


def flags(condition):
    return jnp.where(condition, 1.0, 0.0)


def whole_arrays(count):
    return [pl.BlockSpec(memory_space=pltpu.VMEM)] * count


def product(rows, columns):
    rows, columns = jnp.concatenate(rows, axis=1), jnp.concatenate(columns, axis=1)
    return lax.dot_general(rows, columns, (((1,), (1,)), ((), ())), preferred_element_type=jnp.float32)


def pack_kernel(level_ref, owner_ref, cell_ref, normal_ref, send_ref, slot_ref, total_ref):
    bricks, capacity = send_ref.shape[0], total_ref.shape[1]
    points = owner_ref.shape[1]
    block = 256
    earlier = rows_iota(block, block) < lax.broadcasted_iota(jnp.int32, (block, block), 1)
    total_ref[...] = jnp.zeros_like(total_ref)

    def names(at):
        here = pl.ds(pl.multiple_of(at * block, block), block)
        named = flags(rows_iota(bricks, block) == owner_ref[:, here])
        x = cell_ref[:, here] >> 14
        return here, named, x, flags(rows_iota(CX, block) == x)

    def tally(named, x_hot):
        return product([named.astype(jnp.bfloat16)], [x_hot.astype(jnp.bfloat16)])

    def count(at, counts):
        _, named, _, x_hot = names(at)
        return counts + tally(named, x_hot)

    counts = lax.fori_loop(0, points // block, count, jnp.zeros((bricks, CX), jnp.float32), unroll=4)
    per_brick = jnp.sum(counts, axis=1, keepdims=True)

    def step(at, seen):
        here, named, x, x_hot = names(at)
        x_less = flags(rows_iota(CX, block) < x)
        ahead = jnp.dot(
            jnp.concatenate([counts, seen], axis=1).astype(jnp.bfloat16),
            jnp.concatenate([x_less, x_hot], axis=0).astype(jnp.bfloat16),
            preferred_element_type=jnp.float32,
        )
        key = (owner_ref[:, here] * CX + x).astype(jnp.float32)
        column = jnp.broadcast_to(key, (128, block)).T
        same = (jnp.concatenate([column] * (block // 128), axis=1) == key) & earlier
        rank = jnp.sum(named * ahead, axis=0, keepdims=True) + jnp.sum(flags(same), axis=0, keepdims=True)
        used = jnp.sum(named * per_brick, axis=0, keepdims=True)
        place = jnp.floor((rank * capacity + 0.5) / used)
        slot_ref[:, here] = place
        slot = flags(rows_iota(capacity, block).astype(jnp.float32) == place).astype(jnp.bfloat16)
        values = []
        for k in range(3):
            values += [part.astype(jnp.float32) for part in parts_of(normal_ref[k : k + 1, here], 3)]
        cell = cell_ref[:, here] + 1
        for shift in (16, 8, 0):
            values.append(((cell >> shift) & 255).astype(jnp.float32))
        rows = jnp.concatenate([(named * value).astype(jnp.bfloat16) for value in values], axis=0)
        total_ref[...] += product([rows], [slot])
        return seen + tally(named, x_hot)

    lax.fori_loop(0, points // block, step, jnp.zeros((bricks, CX), jnp.float32), unroll=2)
    part = lambda i: total_ref[i * bricks : (i + 1) * bricks, :]
    fields = [part(3 * k) + part(3 * k + 1) + part(3 * k + 2) for k in range(3)]
    fields.append(part(9) * 65536.0 + part(10) * 256.0 + part(11))
    row = jnp.concatenate(fields, axis=1)
    used = row.shape[1] // 128
    for j in range(used):
        send_ref[:, j, :] = row[:, 128 * j : 128 * (j + 1)]
    level = jnp.full((bricks, send_ref.shape[1] - used, 128), level_ref[0, 0])
    send_ref[:, used:, :] = level.astype(jnp.float32)


def pack(owners, cells, normals, levels, bricks, capacity):
    points = cells.shape[0]
    return pl.pallas_call(
        pack_kernel,
        out_shape=(
            jax.ShapeDtypeStruct((bricks, 4 * capacity // 128 // 8 * 8 + 8, 128), jnp.float32),
            jax.ShapeDtypeStruct((1, points), jnp.float32),
        ),
        in_specs=[pl.BlockSpec(memory_space=pltpu.SMEM)] + whole_arrays(3),
        out_specs=tuple(whole_arrays(2)),
        scratch_shapes=[pltpu.VMEM((12 * bricks, capacity), jnp.float32)],
        compiler_params=pltpu.CompilerParams(vmem_limit_bytes=32 << 20),
        name="pack",
    )(levels, owners.reshape(1, points), cells.reshape(1, points), normals)


def unpack_kernel(owner_ref, rank_ref, held_ref, out_ref):
    bricks, capacity = held_ref.shape
    points = owner_ref.shape[1]
    block = 512
    held = jnp.concatenate([part.astype(jnp.float32).T for part in parts_of(held_ref[...], 3)], axis=1)
    held = held.astype(jnp.bfloat16)
    for at in range(points // block):
        here = slice(at * block, (at + 1) * block)
        named = flags(rows_iota(bricks, block) == owner_ref[:, here]).astype(jnp.bfloat16)
        named = jnp.concatenate([named] * 3, axis=0)
        found = jnp.dot(held, named, preferred_element_type=jnp.float32)
        slot = rows_iota(capacity, block).astype(jnp.float32) == rank_ref[:, here]
        out_ref[:, here] = jnp.sum(jnp.where(slot, found, 0.0), axis=0, keepdims=True)


def unpack(owners, rank, held):
    points = owners.shape[0]
    out = pl.pallas_call(
        unpack_kernel,
        out_shape=jax.ShapeDtypeStruct((1, points), jnp.float32),
        in_specs=whole_arrays(3),
        out_specs=pl.BlockSpec(memory_space=pltpu.VMEM),
        compiler_params=pltpu.CompilerParams(vmem_limit_bytes=32 << 20),
        name="unpack",
    )(owners.reshape(1, points), rank, held)
    return out.reshape(points)


def spread(row):
    return jnp.broadcast_to(row, (16, 128)).astype(jnp.bfloat16)


def times_row(table, row16):
    rows = table.shape[0]
    return (table.reshape(rows // 16, 16, 128) * row16[None]).reshape(rows, 128)


def places(cell_row):
    cell = cell_row.astype(jnp.int32) - 1
    return cell >> 14, (cell >> 8) & (CY - 1), cell & (NZ - 1)


GROUP = 4
WINDOW = 6


def units_turned(tile):
    row = rows_iota(8, 128)
    unit = lax.broadcasted_iota(jnp.int32, (8, 128), 1) // 16
    for bit in (4, 2, 1):
        low, high = (row & bit) == 0, (unit & bit) != 0
        from_below = pltpu.roll(pltpu.roll(tile, 8 - bit, 0), 16 * bit, 1)
        from_above = pltpu.roll(pltpu.roll(tile, bit, 0), 128 - 16 * bit, 1)
        tile = jnp.where(low & high, from_below, jnp.where(low | high, tile, from_above))
    return tile


def regroup_kernel(held_ref, field_ref):
    bricks = held_ref.shape[0]
    chunks = field_ref.shape[0] // 4
    halves, blocks = chunks // bricks, bricks // 8
    for k in range(4):
        for half in range(halves):
            for block in range(blocks):
                tile = held_ref[8 * block : 8 * (block + 1), halves * k + half, :]
                here = pl.ds(k * chunks + 8 * half * blocks + block, 8, stride=blocks)
                field_ref[here, :] = units_turned(tile)


def regroup(held, bricks, capacity):
    chunks = bricks * capacity // 128
    if capacity % 128 or bricks % 8:
        field = held[:, : 4 * capacity // 128].reshape(bricks, 4, capacity)
        return field.transpose(1, 0, 2).reshape(4 * chunks, 128)
    return pl.pallas_call(
        regroup_kernel,
        out_shape=jax.ShapeDtypeStruct((4 * chunks, 128), jnp.float32),
        in_specs=whole_arrays(1),
        out_specs=pl.BlockSpec(memory_space=pltpu.VMEM),
        name="regroup",
    )(held)


def splat_kernel(
    bound_ref, even_ref, field_ref, source_ref, x_pair_ref, x_other_ref, y_pair_ref, y_other_ref, sum_ref, column_ref
):
    chunks = field_ref.shape[0] // 4
    points = 128 * GROUP
    sum_ref[...] = jnp.zeros_like(sum_ref)

    def group(at, carry):
        first, last = bound_ref[at, 0], bound_ref[at, 1]
        cells = []
        for member in range(GROUP):
            chunk = GROUP * at + member
            x, y, z = places(field_ref[pl.ds(3 * chunks + chunk, 1), :])
            z_hot = flags(rows_iota(NZ, 128) == z).astype(jnp.bfloat16)
            for k in range(3):
                parts = parts_of(field_ref[pl.ds(k * chunks + chunk, 1), :], 2)
                for j, part in enumerate(parts):
                    here = slice(j * points + 128 * member, j * points + 128 * (member + 1))
                    column_ref[k * NZ : (k + 1) * NZ, here] = times_row(z_hot, spread(part.astype(jnp.float32)))
            cells.append((x, flags(rows_iota(CY, 128) == y).astype(jnp.bfloat16)))

        def window(turn, carry):
            start = first + turn * WINDOW
            rows = []
            for x, y_hot in cells:
                hots = [spread(flags(x == start + i)) for i in range(WINDOW)]
                rows.append(jnp.concatenate([times_row(y_hot, hot) for hot in hots], axis=0))
            here = pl.ds(pl.multiple_of(start * CY, CY), WINDOW * CY)
            sum_ref[here, :] += product(rows * 2, [column_ref[...]])
            return carry

        window(0, 0)
        lax.fori_loop(1, jnp.maximum(last - first, 0) // WINDOW + 1, window, 0)
        return carry

    lax.fori_loop(0, chunks // GROUP, group, 0)
    row = rows_iota(CY, NZ)
    lane = lax.broadcasted_iota(jnp.int32, (CY, NZ), 1)

    def part(i, k):
        return sum_ref[i * CY : (i + 1) * CY, k * NZ : (k + 1) * NZ]

    for i in range(CX):
        y_part, z_part = part(i, 1), part(i, 2)
        value = jnp.where(row == CY - 1, 0.0, pltpu.roll(y_part, CY - 1, 0)) - jnp.where(row == 0, 0.0, pltpu.roll(y_part, 1, 0))
        value += jnp.where(lane == NZ - 1, 0.0, pltpu.roll(z_part, NZ - 1, 1)) - jnp.where(lane == 0, 0.0, pltpu.roll(z_part, 1, 1))
        if i < CX - 1:
            value += part(i + 1, 0)
        if i > 0:
            value -= part(i - 1, 0)
        source_ref[i * CY : (i + 1) * CY, :] = -0.5 * value
    before, after = -0.5 * part(0, 0), 0.5 * part(CX - 1, 0)
    x_pair_ref[...] = jnp.where(even_ref[0] > 0, after, before)
    x_other_ref[...] = jnp.where(even_ref[0] > 0, before, after)
    y_part = slice(NZ, 2 * NZ)
    before = -0.5 * jnp.concatenate([sum_ref[i * CY : i * CY + 1, y_part] for i in range(CX)], axis=0)
    after = 0.5 * jnp.concatenate([sum_ref[(i + 1) * CY - 1 : (i + 1) * CY, y_part] for i in range(CX)], axis=0)
    y_pair_ref[...] = jnp.where(even_ref[1] > 0, after, before)
    y_other_ref[...] = jnp.where(even_ref[1] > 0, before, after)


def splat(field, bounds, even):
    shapes = [(CX * CY, NZ), (CY, NZ), (CY, NZ), (CX, NZ), (CX, NZ)]
    return pl.pallas_call(
        splat_kernel,
        out_shape=tuple(jax.ShapeDtypeStruct(shape, jnp.float32) for shape in shapes),
        in_specs=[pl.BlockSpec(memory_space=pltpu.SMEM)] * 2 + whole_arrays(1),
        out_specs=tuple(whole_arrays(5)),
        scratch_shapes=[
            pltpu.VMEM(((CX + WINDOW) * CY, 3 * NZ), jnp.float32),
            pltpu.VMEM((3 * NZ, 2 * GROUP * 128), jnp.bfloat16),
        ],
        compiler_params=pltpu.CompilerParams(vmem_limit_bytes=32 << 20),
        name="splat",
    )(bounds, even, field)


def sample_kernel(blocks, flip_ref, bound_ref, field_ref, held_ref, out_ref, iterate_ref, turned_ref, sampled_ref):
    chunks = field_ref.shape[0]
    turned_ref[:, CX * CY :] = jnp.zeros((2 * NZ, turned_ref.shape[1] - CX * CY), jnp.bfloat16)
    for i in range(CX * CY // 128):
        here = slice(128 * i, 128 * (i + 1))
        per_block = CX * CY // 128 // blocks
        place = i // per_block
        place = jnp.where(flip_ref[0] > 0, blocks - 1 - place, place) * per_block + i % per_block
        block = held_ref[pl.ds(pl.multiple_of(place * 128, 128), 128), :]
        iterate_ref[here, :] = block
        high, low = parts_of(block.T, 2)
        turned_ref[:NZ, here] = high
        turned_ref[NZ:, here] = low
    width = 8

    def group(at, carry):
        first, last = bound_ref[at, 0] // 2 * 2, bound_ref[at, 1]
        cells = [places(field_ref[pl.ds(GROUP * at + member, 1), :]) for member in range(GROUP)]
        level = rows_iota(NZ, 128 * GROUP) == jnp.concatenate([z for _, _, z in cells], axis=1)

        def window(turn, total):
            start = first + turn * width
            tables = []
            for x, y, _ in cells:
                y_hot = flags(rows_iota(CY, 128) == y).astype(jnp.bfloat16)
                hots = [spread(flags(x == start + i)) for i in range(width)]
                tables.append(jnp.concatenate([times_row(y_hot, hot) for hot in hots], axis=0))
            here = pl.ds(pl.multiple_of(start * CY, 128), width * CY)
            found = jnp.dot(turned_ref[:, here], jnp.concatenate(tables, axis=1), preferred_element_type=jnp.float32)
            found = jnp.where(level, found[:NZ] + found[NZ:], 0.0)
            return total + jnp.sum(found, axis=0, keepdims=True)

        turns = jnp.maximum(last - first, 0) // width + 1
        row = lax.fori_loop(1, turns, window, window(0, jnp.zeros((1, 128 * GROUP), jnp.float32)))
        for member in range(GROUP):
            sampled_ref[pl.ds(GROUP * at + member, 1), :] = row[:, 128 * member : 128 * (member + 1)]
        return carry

    lax.fori_loop(0, chunks // GROUP, group, 0)
    if len(out_ref.shape) == 2:
        out_ref[...] = sampled_ref[...]
        return
    bricks, halves = out_ref.shape[:2]
    for half in range(halves):
        for block in range(bricks // 8):
            tile = sampled_ref[pl.ds(8 * half * (bricks // 8) + block, 8, stride=bricks // 8), :]
            out_ref[8 * block : 8 * (block + 1), half, :] = units_turned(tile)


def sample(cell_rows, bounds, held, flip, blocks, bricks, capacity):
    turned = (bricks, capacity // 128, 128)
    if capacity % 128 or bricks % 8:
        turned = cell_rows.shape
    return pl.pallas_call(
        functools.partial(sample_kernel, blocks),
        out_shape=tuple(jax.ShapeDtypeStruct(shape, jnp.float32) for shape in (turned, held.shape)),
        in_specs=[pl.BlockSpec(memory_space=pltpu.SMEM)] * 2 + whole_arrays(2),
        out_specs=tuple(whole_arrays(2)),
        scratch_shapes=[
            pltpu.VMEM((2 * NZ, CX * CY + 512), jnp.bfloat16),
            pltpu.VMEM(cell_rows.shape, jnp.float32),
        ],
        compiler_params=pltpu.CompilerParams(vmem_limit_bytes=32 << 20),
        name="sample",
    )(flip, bounds, cell_rows, held)


def swaps(pair, other, axis):
    peers = lax.axis_size(axis)
    got = []
    for start, value in ((0, pair), (1, other)):
        pairs = [(i, i + 1) for i in range(start, peers - 1, 2)]
        got.append(lax.ppermute(value, axis, pairs + [(j, i) for i, j in pairs]))
    return got


def parts_in_rows(value):
    high, low = parts_of(value, 2)
    return jnp.concatenate([high, low, high], axis=0)


def wide(matrix):
    high, low = parts_of(matrix, 2)
    return jnp.concatenate([high, high, low], axis=1)


def shifted(value, axis, back):
    length = value.shape[axis]
    moved = pltpu.roll(value, length - 1 if back else 1, axis)
    index = lax.broadcasted_iota(jnp.int32, value.shape, axis)
    return jnp.where(index == (length - 1 if back else 0), 0.0, moved)


def remainder_of(source, before, middle, after, diagonal):
    beside = before + after
    beside = beside + shifted(middle, 0, False) + shifted(middle, 0, True)
    beside = beside + shifted(middle, 1, False) + shifted(middle, 1, True)
    return source - (diagonal * middle - beside)


def pieces(ref, order, per_source, start, rows, bands, per_band):
    columns = []
    for band in range(bands):
        starts = [i * per_source + band * per_band + start for i in order]
        columns.append(jnp.concatenate([ref[at : at + rows, :] for at in starts], axis=0))
    return jnp.concatenate(columns, axis=1)


def put(sent_ref, k, planes, order, per_block, start, value):
    turned = value.T
    per_target = turned.shape[0] // len(order)
    for j, target in enumerate(order):
        for band in range(turned.shape[1] // 128):
            at = target * per_block + start + band * per_target * planes + k
            part = turned[j * per_target : (j + 1) * per_target, band * 128 : (band + 1) * 128]
            sent_ref[pl.ds(at, per_target, stride=planes), :] = part


def brick_planes(ref, first_count, second_count, planes, k):
    bands = []
    lane = lax.broadcasted_iota(jnp.int32, (8, 128), 1)
    for i in range(first_count):
        tiles = []
        for j in range(second_count):
            start = ((i * second_count + j) * planes + k) * 8
            tiles.append(ref[start : start + 8, :])
        turned = [pltpu.roll(tile, 64, 1) for tile in tiles]
        pairs = range(0, second_count, 2)
        bands.append(jnp.concatenate([jnp.where(lane < 64, tiles[j], turned[j + 1]) for j in pairs], axis=1))
        bands.append(jnp.concatenate([jnp.where(lane < 64, turned[j], tiles[j + 1]) for j in pairs], axis=1))
    return jnp.concatenate(bands, axis=0)


def sweep_all(count, step_ref, source_ref, diagonal_ref, matrix_ref, emit):
    matrix = wide(matrix_ref[...])
    for k in range(count):
        diagonal = diagonal_ref[0 if diagonal_ref.shape[0] == 1 else k + 1]
        middle = step_ref[k + 1]
        remainder = remainder_of(source_ref[k + 1], step_ref[k], middle, step_ref[k + 2], diagonal)
        high, low = parts_of(remainder, 2)
        row = jnp.concatenate([high, low, high], axis=1)
        step = lax.dot_general(row, matrix, (((1,), (1,)), ((), ())), preferred_element_type=jnp.float32)
        emit(k, middle + step)


def first_kernel(
    grid, held_ref, diagonal_ref, first_ref, second_ref, sent_ref, source_ref, step_ref
):
    first_count, second_count, planes, per_target = grid
    for k in range(planes + 2):
        source_ref[k] = brick_planes(held_ref, first_count, second_count, planes + 2, k)
    first = wide(first_ref[...])
    for k in range(planes + 2):
        step_ref[k] = jnp.dot(first, parts_in_rows(source_ref[k]), preferred_element_type=jnp.float32)
    order = slab_order(first_count, second_count)
    block = sent_ref.shape[0] // len(order)

    def emit(k, value):
        put(sent_ref, k, planes, order, block, 0, source_ref[k + 1])
        put(sent_ref, k, planes, order, block, block // 2, value)

    sweep_all(planes, step_ref, source_ref, diagonal_ref, second_ref, emit)


def later_kernel(
    shape, edge_ref, held_ref, pair_ref, other_ref, diagonal_ref, first_ref, second_ref, *refs
):
    order, planes, rows, with_source, last = shape
    devices = len(order)
    even = edge_ref[2] > 0
    if with_source:
        sent_ref, source_ref, iterate_ref, step_ref = refs
    else:
        source_ref, sent_ref, iterate_ref, step_ref = refs
    bands = iterate_ref.shape[2] // 128
    block, edge_block = held_ref.shape[0] // devices, pair_ref.shape[0] // devices
    per_band = planes * rows
    edge_band = edge_block // bands
    own = lambda k, start: pieces(held_ref, order, block, start + k * rows, rows, bands, per_band)

    def edge(after, k):
        pair, other = [pieces(ref, order, edge_block, k * rows, rows, bands, edge_band) for ref in (pair_ref, other_ref)]
        return jnp.where(even, pair, other) if after else jnp.where(even, other, pair)

    if with_source:
        for k in range(planes):
            source_ref[k + 1] = own(k, 0)
        source_ref[0] = edge(False, 0)
        source_ref[planes + 1] = edge(True, 0)
    for k in range(2):
        iterate_ref[k] = edge(False, k + with_source)
        iterate_ref[planes + 2 + k] = edge(True, k + with_source)
    for k in range(planes):
        iterate_ref[k + 2] = own(k, block // 2 if with_source else 0)
    first = wide(first_ref[...])
    for k in range(planes + 2):
        diagonal = diagonal_ref[0 if diagonal_ref.shape[0] == 1 else k]
        middle = iterate_ref[k + 1]
        remainder = remainder_of(source_ref[k], iterate_ref[k], middle, iterate_ref[k + 2], diagonal)
        step = jnp.dot(first, parts_in_rows(remainder), preferred_element_type=jnp.float32)
        if k == 0:
            step = step * edge_ref[0]
        if k == planes + 1:
            step = step * edge_ref[1]
        step_ref[k] = middle + step

    def emit(k, value):
        if last:
            for j in range(value.shape[0] // CY):
                sent_ref[j, k] = value[j * CY : (j + 1) * CY, :]
        else:
            put(sent_ref, k, planes, order, sent_ref.shape[0] // devices, 0, value)

    sweep_all(planes, step_ref, source_ref, diagonal_ref, second_ref, emit)


SMEM = pl.BlockSpec(memory_space=pltpu.SMEM)
VMEM = pl.BlockSpec(memory_space=pltpu.VMEM)
LIMIT = pltpu.CompilerParams(vmem_limit_bytes=48 << 20)


def first_phase(grid, held, diagonal, first, second):
    rows, columns = diagonal.shape[1:]
    first_count, second_count, planes, per_target = grid
    return pl.pallas_call(
        functools.partial(first_kernel, grid),
        out_shape=(
            jax.ShapeDtypeStruct((2 * columns * planes * rows // 128, 128), jnp.float32),
            jax.ShapeDtypeStruct((planes + 2, rows, columns), jnp.float32),
        ),
        in_specs=[VMEM] * 4,
        out_specs=(VMEM, VMEM),
        scratch_shapes=[pltpu.VMEM((planes + 2, rows, columns), jnp.float32)],
        compiler_params=LIMIT,
        name="first_phase",
    )(held, diagonal, first, second)


def later_phase(order, planes, rows, edges, held, pair, other, diagonal, first, second, source=None, last=False):
    columns = second.shape[1]
    length = len(order) * rows
    if last:
        sent = (length // CY, planes, CY, columns)
    else:
        sent = (columns * planes * length // 128, 128)
    out = [jax.ShapeDtypeStruct(sent, jnp.float32)]
    operands = [edges, held, pair, other, diagonal, first, second]
    if source is None:
        out.append(jax.ShapeDtypeStruct((planes + 2, length, columns), jnp.float32))
    else:
        operands.append(source)
    return pl.pallas_call(
        functools.partial(later_kernel, (order, planes, rows, source is None, last)),
        out_shape=tuple(out),
        in_specs=[SMEM] + [VMEM] * (len(operands) - 1),
        out_specs=tuple([VMEM] * len(out)),
        scratch_shapes=[
            pltpu.VMEM((planes + 4, length, columns), jnp.float32),
            pltpu.VMEM((planes + 2, length, columns), jnp.float32),
        ],
        compiler_params=LIMIT,
        name="later_phase",
    )(*operands)


def join_kernel(order, even_ref, source_ref, x_pair_ref, x_other_ref, y_pair_ref, y_other_ref, brick_ref, sent_ref, turned_ref):
    x_even, y_even = even_ref[0] > 0, even_ref[1] > 0
    y_before = jnp.where(y_even, y_other_ref[...], y_pair_ref[...])
    y_after = jnp.where(y_even, y_pair_ref[...], y_other_ref[...])
    for i in range(CX):
        here = slice(i * CY, (i + 1) * CY)
        value = source_ref[here, :]
        if i == 0:
            value = value + jnp.where(x_even, x_other_ref[...], x_pair_ref[...])
        if i == CX - 1:
            value = value + jnp.where(x_even, x_pair_ref[...], x_other_ref[...])
        row = rows_iota(CY, NZ)
        value = value + jnp.where(row == 0, y_before[i : i + 1, :], 0.0)
        brick_ref[here, :] = value + jnp.where(row == CY - 1, y_after[i : i + 1, :], 0.0)
    half = CX // 2
    planes = sent_ref.shape[1] // half
    turned_ref[:8, :] = jnp.zeros((8, 2 * CY), jnp.float32)
    turned_ref[NZ + 8 :, :] = jnp.zeros((8, 2 * CY), jnp.float32)
    for i in range(half):
        both = [brick_ref[j * CY : (j + 1) * CY, :] for j in (i, i + half)]
        turned_ref[8 : NZ + 8, :] = jnp.concatenate(both, axis=0).T
        for j, target in enumerate(order):
            first = 7 + j * (planes - 2)
            sent_ref[target, pl.ds(i, planes, stride=half), :] = turned_ref[first : first + planes, :]


def join(source, even, order, *faces):
    return pl.pallas_call(
        functools.partial(join_kernel, order),
        out_shape=(
            jax.ShapeDtypeStruct(source.shape, jnp.float32),
            jax.ShapeDtypeStruct((len(order), (NZ // len(order) + 2) * CX // 2, 2 * CY), jnp.float32),
        ),
        in_specs=[SMEM] + [VMEM] * 5,
        out_specs=(VMEM, VMEM),
        scratch_shapes=[pltpu.VMEM((NZ + 16, 2 * CY), jnp.float32)],
        compiler_params=LIMIT,
        name="join",
    )(even, source, *faces)


def slab_order(first_count, second_count):
    order = []
    for i in range(first_count):
        row = [i * second_count + j for j in range(second_count)]
        order += row if i % 2 == 0 else row[::-1]
    return order


def place_in_row(j):
    return jnp.where(lax.axis_index("bx") % 2 == 0, j, lax.axis_size("by") - 1 - j)


def beside(to_next, to_previous, even):
    order = slab_order(lax.axis_size("bx"), lax.axis_size("by"))
    got = []
    for start, value in ((0, jnp.where(even, to_next, to_previous)), (1, jnp.where(even, to_previous, to_next))):
        pairs = [(order[i], order[i + 1]) for i in range(start, len(order) - 1, 2)]
        got.append(lax.ppermute(value, EVERY, pairs + [(j, i) for i, j in pairs]))
    return got


def exchange(value):
    return lax.all_to_all(value, EVERY, split_axis=0, concat_axis=0, tiled=True)


def x_slab_source(brick, even):
    second_count = lax.axis_size("by")
    mine = lax.axis_index("by")
    brick = brick.reshape(CX, CY, NZ)
    thick = CX // second_count
    slab = jnp.zeros((thick, second_count * CY, NZ), jnp.float32)
    for turn in range(second_count):
        partner = mine ^ turn
        piece = lax.dynamic_slice_in_dim(brick, place_in_row(partner) * thick, thick, 0)
        if turn:
            piece = lax.ppermute(piece, "by", [(i, i ^ turn) for i in range(second_count)])
        slab = lax.dynamic_update_slice_in_dim(slab, piece, partner * CY, 1)
    pair, other = beside(slab[-1:], slab[:1], even)
    return jnp.concatenate([jnp.where(even, other, pair), slab, jnp.where(even, pair, other)], axis=0)


def relax(brick, sent, levels, rows_inverse, columns_inverse, depth_inverse):
    first_count, second_count = lax.axis_size("bx"), lax.axis_size("by")
    devices = first_count * second_count
    order = slab_order(first_count, second_count)
    me = lax.axis_index("bx") * second_count + place_in_row(lax.axis_index("by"))
    even = me % 2 == 0
    nx, ny = first_count * CX, second_count * CY
    thick = (NZ // devices, ny // devices, nx // devices)
    diagonal = 6.0 + screen_base * (1.0 + levels.reshape(first_count, second_count))
    diagonal = jnp.repeat(jnp.repeat(diagonal, CX, 0), CY, 1)
    padded = jnp.pad(diagonal, ((1, 1), (1, 1)), constant_values=1.0)
    diagonals = (
        diagonal[None],
        lax.dynamic_slice_in_dim(padded, me * thick[1], thick[1] + 2, 1).T[:, None, 1:-1],
        lax.dynamic_slice_in_dim(padded, me * thick[2], thick[2] + 2, 0)[:, 1:-1, None],
    )
    edges = jnp.stack([me > 0, me < devices - 1, even]).astype(jnp.float32)
    matrices = (rows_inverse, columns_inverse, depth_inverse)
    held, diagonals = lax.optimization_barrier((exchange(sent), diagonals))
    sent, z_source = first_phase(
        (first_count, second_count, thick[0], thick[1]), held.reshape(-1, 2 * CY), diagonals[0], matrices[0], matrices[1]
    )
    sources = [z_source, None, None]
    for step in range(1, 3 * ITERS // 2):
        at = step % 3
        planes, rows = thick[at], thick[(at + 2) % 3]
        held = exchange(sent)
        if step == 1:
            held, sources[2] = lax.optimization_barrier((held, x_slab_source(brick, even)))
        bands = matrices[(2 * step + 1) % 3].shape[1] // 128
        blocks = held.reshape(devices, -1, bands, planes * rows, 128)
        to_next, to_previous = blocks[:, -1, :, -2 * rows :], blocks[:, -1, :, : 2 * rows]
        if sources[at] is None:
            to_next = jnp.concatenate([blocks[:, 0, :, -rows:], to_next], axis=2)
            to_previous = jnp.concatenate([blocks[:, 0, :, :rows], to_previous], axis=2)
        pair, other = beside(to_next.reshape(-1, 128), to_previous.reshape(-1, 128), even)
        out = later_phase(
            order,
            planes,
            rows,
            edges,
            held,
            pair,
            other,
            diagonals[at],
            matrices[2 * step % 3],
            matrices[(2 * step + 1) % 3],
            source=sources[at],
            last=step + 1 == 3 * ITERS // 2,
        )
        sent = out[0]
        if sources[at] is None:
            sources[at] = out[1]
    sent = sent.reshape(second_count * thick[2], CY, NZ)
    return lax.all_to_all(sent, "by", split_axis=0, concat_axis=0, tiled=True)


def local(normals, owners, cells, levels, rows_inverse, columns_inverse, depth_inverse):
    bricks = lax.axis_size(EVERY)
    point_count = cells.shape[0]
    capacity = 2 * point_count // bricks
    chunks = bricks * capacity // 128
    send, slot = pack(owners, cells, normals, levels, bricks, capacity)
    held = exchange(send)
    levels = held[:, 4 * capacity // 128, 0]
    field = regroup(held, bricks, capacity)
    cell_rows = field[3 * chunks :]
    grouped = cell_rows.reshape(chunks // GROUP, -1)
    x = (grouped.astype(jnp.int32) - 1) >> 14
    bounds = [jnp.min(jnp.where(grouped > 0, x, CX), axis=1), jnp.max(jnp.where(grouped > 0, x, -1), axis=1)]
    bounds = jnp.stack(bounds, axis=1)
    even = jnp.stack([lax.axis_index("bx") % 2 == 0, lax.axis_index("by") % 2 == 0]).astype(jnp.int32)
    source, x_pair, x_other, y_pair, y_other = splat(field, bounds, even)
    faces = swaps(x_pair, x_other, "bx") + swaps(y_pair, y_other, "by")
    brick, sent = join(source, even, slab_order(lax.axis_size("bx"), lax.axis_size("by")), *faces)
    held = relax(brick, sent, levels, rows_inverse, columns_inverse, depth_inverse)
    flip = (lax.axis_index("bx") % 2).astype(jnp.int32).reshape(1)
    held = held.reshape(CX * CY, NZ)
    sampled, iterate = sample(cell_rows, bounds, held, flip, lax.axis_size("by"), bricks, capacity)
    if sampled.ndim == 2:
        sampled = sampled.reshape(bricks, capacity)
    implicit = unpack(owners, slot, exchange(sampled).reshape(bricks, capacity))
    return (iterate.reshape(CX, CY, NZ), implicit)


def solution(mesh):
    placed = (
        P(None, ("bx", "by")),
        P(("bx", "by"), None),
        P(("bx", "by")),
        P("bx", "by"),
        P(),
        P(),
        P(),
    )
    return jax.shard_map(
        local,
        mesh=mesh,
        in_specs=placed,
        out_specs=(P("bx", "by", None), P(("bx", "by"))),
        check_vma=False,
    )
```

```python
import functools

import jax
import jax.numpy as jnp
from jax import lax
from jax.experimental import pallas as pl
from jax.experimental.pallas import tpu as pltpu
from jax.sharding import PartitionSpec as P

CX = 16
CY = 64
NZ = 256
ITERS = 4
EVERY = ("bx", "by")


screen_base = 1.0


def parts_of(value, count):
    parts = []
    for _ in range(count):
        part = value.astype(jnp.bfloat16)
        parts.append(part)
        value = value - part.astype(jnp.float32)
    return parts


def rows_iota(rows, columns):
    return lax.broadcasted_iota(jnp.int32, (rows, columns), 0)


def flags(condition):
    return jnp.where(condition, 1.0, 0.0)


def whole_arrays(count):
    return [pl.BlockSpec(memory_space=pltpu.VMEM)] * count


def product(rows, columns):
    rows, columns = jnp.concatenate(rows, axis=1), jnp.concatenate(columns, axis=1)
    return lax.dot_general(rows, columns, (((1,), (1,)), ((), ())), preferred_element_type=jnp.float32)


def pack_kernel(level_ref, owner_ref, cell_ref, normal_ref, send_ref, slot_ref, total_ref):
    bricks, capacity = send_ref.shape[0], total_ref.shape[1]
    points = owner_ref.shape[1]
    block = 256
    earlier = rows_iota(block, block) < lax.broadcasted_iota(jnp.int32, (block, block), 1)
    total_ref[...] = jnp.zeros_like(total_ref)

    def names(at):
        here = pl.ds(pl.multiple_of(at * block, block), block)
        named = flags(rows_iota(bricks, block) == owner_ref[:, here])
        x = cell_ref[:, here] >> 14
        return here, named, x, flags(rows_iota(CX, block) == x)

    def tally(named, x_hot):
        return product([x_hot.astype(jnp.bfloat16)], [named.astype(jnp.bfloat16)])

    def count(at, counts):
        _, named, _, x_hot = names(at)
        return counts + tally(named, x_hot)

    counts = lax.fori_loop(0, points // block, count, jnp.zeros((CX, bricks), jnp.float32), unroll=4)
    ahead, shift, shifts = jnp.zeros((1, bricks), jnp.float32), jnp.zeros((1, bricks), jnp.float32), []
    for i in range(CX):
        shift = jnp.maximum(shift, float(i * capacity // CX) - ahead)
        shifts.append(shift)
        ahead = ahead + counts[i : i + 1, :]
    shifts = jnp.concatenate(shifts, axis=0)

    def step(at, seen):
        here, named, x, x_hot = names(at)
        x_less = flags(rows_iota(CX, block) < x)
        own = jnp.dot(
            jnp.concatenate([counts, seen, shifts], axis=0).astype(jnp.bfloat16),
            named.astype(jnp.bfloat16),
            preferred_element_type=jnp.float32,
        )
        ahead = jnp.sum(x_less * own[:CX] + x_hot * own[CX : 2 * CX], axis=0, keepdims=True)
        used = jnp.sum(own[:CX], axis=0, keepdims=True)
        moved = jnp.minimum(jnp.sum(x_hot * own[2 * CX :], axis=0, keepdims=True), capacity - used)
        key = (owner_ref[:, here] * CX + x).astype(jnp.float32)
        column = jnp.broadcast_to(key, (128, block)).T
        same = (jnp.concatenate([column] * (block // 128), axis=1) == key) & earlier
        place = ahead + jnp.sum(flags(same), axis=0, keepdims=True) + moved
        slot_ref[:, here] = place
        slot = flags(rows_iota(capacity, block).astype(jnp.float32) == place).astype(jnp.bfloat16)
        values = []
        for k in range(3):
            values += [part.astype(jnp.float32) for part in parts_of(normal_ref[k : k + 1, here], 3)]
        cell = cell_ref[:, here] + 1
        for shift in (16, 8, 0):
            values.append(((cell >> shift) & 255).astype(jnp.float32))
        rows = jnp.concatenate([(named * value).astype(jnp.bfloat16) for value in values], axis=0)
        total_ref[...] += product([rows], [slot])
        return seen + tally(named, x_hot)

    lax.fori_loop(0, points // block, step, jnp.zeros((CX, bricks), jnp.float32), unroll=2)
    part = lambda i: total_ref[i * bricks : (i + 1) * bricks, :]
    fields = [part(3 * k) + part(3 * k + 1) + part(3 * k + 2) for k in range(3)]
    fields.append(part(9) * 65536.0 + part(10) * 256.0 + part(11))
    row = jnp.concatenate(fields, axis=1)
    used = row.shape[1] // 128
    for j in range(used):
        send_ref[:, j, :] = row[:, 128 * j : 128 * (j + 1)]
    level = jnp.full((bricks, send_ref.shape[1] - used, 128), level_ref[0, 0])
    send_ref[:, used:, :] = level.astype(jnp.float32)


def pack(owners, cells, normals, levels, bricks, capacity):
    points = cells.shape[0]
    return pl.pallas_call(
        pack_kernel,
        out_shape=(
            jax.ShapeDtypeStruct((bricks, 4 * capacity // 128 // 8 * 8 + 8, 128), jnp.float32),
            jax.ShapeDtypeStruct((1, points), jnp.float32),
        ),
        in_specs=[pl.BlockSpec(memory_space=pltpu.SMEM)] + whole_arrays(3),
        out_specs=tuple(whole_arrays(2)),
        scratch_shapes=[pltpu.VMEM((12 * bricks, capacity), jnp.float32)],
        compiler_params=pltpu.CompilerParams(vmem_limit_bytes=16 << 20),
        name="pack",
    )(levels, owners.reshape(1, points), cells.reshape(1, points), normals)


def unpack_kernel(owner_ref, rank_ref, held_ref, out_ref):
    bricks, capacity = held_ref.shape
    points = owner_ref.shape[1]
    block = 512
    held = jnp.concatenate([part.astype(jnp.float32).T for part in parts_of(held_ref[...], 3)], axis=1)
    held = held.astype(jnp.bfloat16)
    for at in range(points // block):
        here = slice(at * block, (at + 1) * block)
        named = flags(rows_iota(bricks, block) == owner_ref[:, here]).astype(jnp.bfloat16)
        named = jnp.concatenate([named] * 3, axis=0)
        found = jnp.dot(held, named, preferred_element_type=jnp.float32)
        slot = rows_iota(capacity, block).astype(jnp.float32) == rank_ref[:, here]
        out_ref[:, here] = jnp.sum(jnp.where(slot, found, 0.0), axis=0, keepdims=True)


def unpack(owners, rank, held):
    points = owners.shape[0]
    out = pl.pallas_call(
        unpack_kernel,
        out_shape=jax.ShapeDtypeStruct((1, points), jnp.float32),
        in_specs=whole_arrays(3),
        out_specs=pl.BlockSpec(memory_space=pltpu.VMEM),
        compiler_params=pltpu.CompilerParams(vmem_limit_bytes=16 << 20),
        name="unpack",
    )(owners.reshape(1, points), rank, held)
    return out.reshape(points)


def spread(row):
    return jnp.broadcast_to(row, (16, 128)).astype(jnp.bfloat16)


def times_row(table, row16):
    rows = table.shape[0]
    return (table.reshape(rows // 16, 16, 128) * row16[None]).reshape(rows, 128)


def places(cell_row):
    cell = cell_row.astype(jnp.int32) - 1
    return cell >> 14, (cell >> 8) & (CY - 1), cell & (NZ - 1)


GROUP = 4
WINDOW = 4


def units_turned(tile):
    row = rows_iota(8, 128)
    unit = lax.broadcasted_iota(jnp.int32, (8, 128), 1) // 16
    for bit in (4, 2, 1):
        low, high = (row & bit) == 0, (unit & bit) != 0
        from_below = pltpu.roll(pltpu.roll(tile, 8 - bit, 0), 16 * bit, 1)
        from_above = pltpu.roll(pltpu.roll(tile, bit, 0), 128 - 16 * bit, 1)
        tile = jnp.where(low & high, from_below, jnp.where(low | high, tile, from_above))
    return tile


def grouped(bricks, capacity):
    return capacity % 128 == 0 and bricks % 8 == 0


def regroup(held_ref, field_ref):
    bricks = held_ref.shape[0]
    chunks = field_ref.shape[0] // 4
    halves, blocks = chunks // bricks, bricks // 8
    for k in range(4):
        for half in range(halves):
            for block in range(blocks):
                tile = held_ref[8 * block : 8 * (block + 1), halves * k + half, :]
                here = pl.ds(k * chunks + 8 * half * blocks + block, 8, stride=blocks)
                field_ref[here, :] = units_turned(tile)


def splat_kernel(
    even_ref,
    held_ref,
    source_ref,
    x_pair_ref,
    x_other_ref,
    y_pair_ref,
    y_other_ref,
    cell_ref,
    bound_ref,
    field_ref,
    sum_ref,
    column_ref,
):
    chunks = field_ref.shape[0] // 4
    points = 128 * GROUP
    if len(held_ref.shape) == 3:
        regroup(held_ref, field_ref)
    else:
        field_ref[...] = held_ref[...]
    cell_ref[...] = field_ref[3 * chunks :, :]
    for at in range(chunks // GROUP):
        cell = cell_ref[GROUP * at : GROUP * (at + 1), :]
        x = places(cell)[0].astype(jnp.float32)
        bound_ref[at, 0] = jnp.min(jnp.where(cell > 0, x, float(CX))).astype(jnp.int32)
        bound_ref[at, 1] = jnp.max(jnp.where(cell > 0, x, -1.0)).astype(jnp.int32)
    sum_ref[...] = jnp.zeros_like(sum_ref)

    def group(at, carry):
        first, last = bound_ref[at, 0], bound_ref[at, 1]
        cells = []
        for member in range(GROUP):
            chunk = GROUP * at + member
            x, y, z = places(field_ref[pl.ds(3 * chunks + chunk, 1), :])
            z_hot = flags(rows_iota(NZ, 128) == z).astype(jnp.bfloat16)
            for k in range(3):
                parts = parts_of(field_ref[pl.ds(k * chunks + chunk, 1), :], 2)
                for j, part in enumerate(parts):
                    here = slice(j * points + 128 * member, j * points + 128 * (member + 1))
                    column_ref[k * NZ : (k + 1) * NZ, here] = times_row(z_hot, spread(part.astype(jnp.float32)))
            cells.append((x, flags(rows_iota(CY, 128) == y).astype(jnp.bfloat16)))

        def window(turn, carry):
            start = first + turn * WINDOW
            rows = []
            for x, y_hot in cells:
                hots = [spread(flags(x == start + i)) for i in range(WINDOW)]
                rows.append(jnp.concatenate([times_row(y_hot, hot) for hot in hots], axis=0))
            here = pl.ds(pl.multiple_of(start * CY, CY), WINDOW * CY)
            sum_ref[here, :] += product(rows * 2, [column_ref[...]])
            return carry

        window(0, 0)
        lax.fori_loop(1, jnp.maximum(last - first, 0) // WINDOW + 1, window, 0)
        return carry

    lax.fori_loop(0, chunks // GROUP, group, 0)
    row = rows_iota(CY, NZ)
    lane = lax.broadcasted_iota(jnp.int32, (CY, NZ), 1)

    def part(i, k):
        return sum_ref[i * CY : (i + 1) * CY, k * NZ : (k + 1) * NZ]

    for i in range(CX):
        y_part, z_part = part(i, 1), part(i, 2)
        value = jnp.where(row == CY - 1, 0.0, pltpu.roll(y_part, CY - 1, 0)) - jnp.where(row == 0, 0.0, pltpu.roll(y_part, 1, 0))
        value += jnp.where(lane == NZ - 1, 0.0, pltpu.roll(z_part, NZ - 1, 1)) - jnp.where(lane == 0, 0.0, pltpu.roll(z_part, 1, 1))
        if i < CX - 1:
            value += part(i + 1, 0)
        if i > 0:
            value -= part(i - 1, 0)
        source_ref[i * CY : (i + 1) * CY, :] = -0.5 * value
    before, after = -0.5 * part(0, 0), 0.5 * part(CX - 1, 0)
    x_pair_ref[...] = jnp.where(even_ref[0] > 0, after, before)
    x_other_ref[...] = jnp.where(even_ref[0] > 0, before, after)
    y_part = slice(NZ, 2 * NZ)
    before = -0.5 * jnp.concatenate([sum_ref[i * CY : i * CY + 1, y_part] for i in range(CX)], axis=0)
    after = 0.5 * jnp.concatenate([sum_ref[(i + 1) * CY - 1 : (i + 1) * CY, y_part] for i in range(CX)], axis=0)
    y_pair_ref[...] = jnp.where(even_ref[1] > 0, after, before)
    y_other_ref[...] = jnp.where(even_ref[1] > 0, before, after)


def splat(held, even, chunks):
    shapes = [(CX * CY, NZ), (CY, NZ), (CY, NZ), (CX, NZ), (CX, NZ), (chunks, 128)]
    out = [jax.ShapeDtypeStruct(shape, jnp.float32) for shape in shapes]
    return pl.pallas_call(
        splat_kernel,
        out_shape=tuple(out + [jax.ShapeDtypeStruct((chunks // GROUP, 2), jnp.int32)]),
        in_specs=[pl.BlockSpec(memory_space=pltpu.SMEM)] + whole_arrays(1),
        out_specs=tuple(whole_arrays(6) + [pl.BlockSpec(memory_space=pltpu.SMEM)]),
        scratch_shapes=[
            pltpu.VMEM((4 * chunks, 128), jnp.float32),
            pltpu.VMEM(((CX + WINDOW) * CY, 3 * NZ), jnp.float32),
            pltpu.VMEM((3 * NZ, 2 * GROUP * 128), jnp.bfloat16),
        ],
        compiler_params=pltpu.CompilerParams(vmem_limit_bytes=16 << 20),
        name="splat",
    )(even, held)


def sample_kernel(blocks, flip_ref, bound_ref, field_ref, held_ref, out_ref, iterate_ref, turned_ref, sampled_ref):
    chunks = field_ref.shape[0]
    turned_ref[:, CX * CY :] = jnp.zeros((2 * NZ, turned_ref.shape[1] - CX * CY), jnp.bfloat16)
    for i in range(CX * CY // 128):
        here = slice(128 * i, 128 * (i + 1))
        per_block = CX * CY // 128 // blocks
        place = i // per_block
        place = jnp.where(flip_ref[0] > 0, blocks - 1 - place, place) * per_block + i % per_block
        block = held_ref[pl.ds(pl.multiple_of(place * 128, 128), 128), :]
        iterate_ref[here, :] = block
        high, low = parts_of(block.T, 2)
        turned_ref[:NZ, here] = high
        turned_ref[NZ:, here] = low
    width = 4

    def group(at, carry):
        first, last = bound_ref[at, 0] // 2 * 2, bound_ref[at, 1]
        cells = [places(field_ref[pl.ds(GROUP * at + member, 1), :]) for member in range(GROUP)]
        level = rows_iota(NZ, 128 * GROUP) == jnp.concatenate([z for _, _, z in cells], axis=1)

        def window(turn, total):
            start = first + turn * width
            tables = []
            for x, y, _ in cells:
                y_hot = flags(rows_iota(CY, 128) == y).astype(jnp.bfloat16)
                hots = [spread(flags(x == start + i)) for i in range(width)]
                tables.append(jnp.concatenate([times_row(y_hot, hot) for hot in hots], axis=0))
            here = pl.ds(pl.multiple_of(start * CY, 128), width * CY)
            found = jnp.dot(turned_ref[:, here], jnp.concatenate(tables, axis=1), preferred_element_type=jnp.float32)
            found = jnp.where(level, found[:NZ] + found[NZ:], 0.0)
            return total + jnp.sum(found, axis=0, keepdims=True)

        turns = jnp.maximum(last - first, 0) // width + 1
        row = lax.fori_loop(1, turns, window, window(0, jnp.zeros((1, 128 * GROUP), jnp.float32)))
        for member in range(GROUP):
            sampled_ref[pl.ds(GROUP * at + member, 1), :] = row[:, 128 * member : 128 * (member + 1)]
        return carry

    lax.fori_loop(0, chunks // GROUP, group, 0)
    if len(out_ref.shape) == 2:
        out_ref[...] = sampled_ref[...]
        return
    bricks, halves = out_ref.shape[:2]
    for half in range(halves):
        for block in range(bricks // 8):
            tile = sampled_ref[pl.ds(8 * half * (bricks // 8) + block, 8, stride=bricks // 8), :]
            out_ref[8 * block : 8 * (block + 1), half, :] = units_turned(tile)


def sample(cell_rows, bounds, held, flip, blocks, bricks, capacity):
    turned = (bricks, capacity // 128, 128)
    if not grouped(bricks, capacity):
        turned = cell_rows.shape
    return pl.pallas_call(
        functools.partial(sample_kernel, blocks),
        out_shape=tuple(jax.ShapeDtypeStruct(shape, jnp.float32) for shape in (turned, held.shape)),
        in_specs=[pl.BlockSpec(memory_space=pltpu.SMEM)] * 2 + whole_arrays(2),
        out_specs=tuple(whole_arrays(2)),
        scratch_shapes=[
            pltpu.VMEM((2 * NZ, CX * CY + 256), jnp.bfloat16),
            pltpu.VMEM(cell_rows.shape, jnp.float32),
        ],
        compiler_params=pltpu.CompilerParams(vmem_limit_bytes=16 << 20),
        name="sample",
    )(flip, bounds, cell_rows, held)


def swaps(pair, other, axis):
    peers = lax.axis_size(axis)
    got = []
    for start, value in ((0, pair), (1, other)):
        pairs = [(i, i + 1) for i in range(start, peers - 1, 2)]
        got.append(lax.ppermute(value, axis, pairs + [(j, i) for i, j in pairs]))
    return got


def parts_in_rows(value):
    high, low = parts_of(value, 2)
    return jnp.concatenate([high, low, high], axis=0)


def wide(matrix):
    high, low = parts_of(matrix, 2)
    return jnp.concatenate([high, high, low], axis=1)


def shifted(value, axis, back):
    length = value.shape[axis]
    moved = pltpu.roll(value, length - 1 if back else 1, axis)
    index = lax.broadcasted_iota(jnp.int32, value.shape, axis)
    return jnp.where(index == (length - 1 if back else 0), 0.0, moved)


def remainder_of(source, before, middle, after, diagonal):
    beside = before + after
    beside = beside + shifted(middle, 0, False) + shifted(middle, 0, True)
    beside = beside + shifted(middle, 1, False) + shifted(middle, 1, True)
    return source - (diagonal * middle - beside)


def pieces(ref, order, per_source, start, rows, bands, per_band):
    columns = []
    for band in range(bands):
        starts = [i * per_source + band * per_band + start for i in order]
        columns.append(jnp.concatenate([ref[at : at + rows, :] for at in starts], axis=0))
    return jnp.concatenate(columns, axis=1)


def put(sent_ref, k, planes, order, per_block, runs, value):
    turned = value.T
    per_target = turned.shape[0] // len(order)
    for j, target in enumerate(order):
        for band in range(turned.shape[1] // 128):
            columns = slice(band * 128, (band + 1) * 128)
            start = target * per_block + band * (per_block * 128 // turned.shape[1]) + k
            for place, first, count in runs:
                if count:
                    part = turned[j * per_target + first : j * per_target + first + count, columns]
                    sent_ref[pl.ds(start + place * planes, count, stride=planes), :] = part


def brick_planes(ref, first_count, second_count, planes, k):
    bands = []
    lane = lax.broadcasted_iota(jnp.int32, (8, 128), 1)
    for i in range(first_count):
        tiles = []
        for j in range(second_count):
            start = ((i * second_count + j) * planes + k) * 8
            tiles.append(ref[start : start + 8, :])
        turned = [pltpu.roll(tile, 64, 1) for tile in tiles]
        pairs = range(0, second_count, 2)
        bands.append(jnp.concatenate([jnp.where(lane < 64, tiles[j], turned[j + 1]) for j in pairs], axis=1))
        bands.append(jnp.concatenate([jnp.where(lane < 64, turned[j], tiles[j + 1]) for j in pairs], axis=1))
    return jnp.concatenate(bands, axis=0)


def diagonal_of(ref, k, turned, shape):
    if ref.shape[0] == 1:
        return ref[0]
    if not turned:
        return ref[k]
    column = jnp.broadcast_to(ref[k], (128, shape[0])).T
    return jnp.concatenate([column] * (shape[1] // 128), axis=1)


def fetch(pairs, sem_ref):
    copies = [pltpu.make_async_copy(source, held, sem_ref.at[i]) for i, (source, held) in enumerate(pairs)]
    for copy in copies:
        copy.start()
    return copies


def sweep_all(count, step_ref, source_ref, diagonal_ref, turned, matrix_ref, emit):
    matrix = wide(matrix_ref[...])
    for k in range(count):
        middle = step_ref[k + 1]
        diagonal = diagonal_of(diagonal_ref, k + 1, turned, middle.shape)
        remainder = remainder_of(source_ref[k + 1], step_ref[k], middle, step_ref[k + 2], diagonal)
        high, low = parts_of(remainder, 2)
        row = jnp.concatenate([high, low, high], axis=1)
        step = lax.dot_general(row, matrix, (((1,), (1,)), ((), ())), preferred_element_type=jnp.float32)
        emit(k, middle + step)


def first_kernel(
    grid, held_ref, diagonal_ref, first_any, second_any, sent_ref, source_ref, step_ref, first_ref, second_ref, sem_ref
):
    copies = fetch([(first_any, first_ref), (second_any, second_ref)], sem_ref)
    first_count, second_count, planes, per_target = grid
    for k in range(planes + 2):
        source_ref[k] = brick_planes(held_ref, first_count, second_count, planes + 2, k)
    copies[0].wait()
    first = wide(first_ref[...])
    for k in range(planes + 2):
        step_ref[k] = jnp.dot(first, parts_in_rows(source_ref[k]), preferred_element_type=jnp.float32)
    order = slab_order(first_count, second_count)
    block = sent_ref.shape[0] // len(order)

    def emit(k, value):
        last = sent_ref.shape[0] * 128 // (2 * planes * len(order) * value.shape[0]) - 1
        put(sent_ref, k, planes, order, block, [(0, 0, 1), (last + 2, last, 1), (last + 3, 1, last - 1)], source_ref[k + 1])
        put(sent_ref, k, planes, order, block, [(1, 0, last + 1)], value)

    copies[1].wait()
    sweep_all(planes, step_ref, source_ref, diagonal_ref, False, second_ref, emit)


def later_kernel(
    shape, edge_ref, held_ref, pair_ref, other_ref, diagonal_ref, first_any, second_any, *refs
):
    order, planes, rows, with_source, last, turned = shape
    devices = len(order)
    *refs, first_ref, second_ref, sem_ref = refs
    copies = fetch([(first_any, first_ref), (second_any, second_ref)], sem_ref)
    even = edge_ref[2] > 0
    if with_source:
        sent_ref, source_ref, iterate_ref, step_ref = refs
    else:
        source_ref, sent_ref, iterate_ref, step_ref = refs
    bands = iterate_ref.shape[2] // 128
    block, edge_block = held_ref.shape[0] // devices, pair_ref.shape[0] // devices
    per_band = block // bands
    edge_band = edge_block // bands
    own = lambda place: pieces(held_ref, order, block, place * rows, rows, bands, per_band)

    def edge(after, k):
        pair, other = [pieces(ref, order, edge_block, k * rows, rows, bands, edge_band) for ref in (pair_ref, other_ref)]
        return jnp.where(even, pair, other) if after else jnp.where(even, other, pair)

    if with_source:
        for k in range(planes):
            source_ref[k + 1] = own(0 if k == 0 else planes + 1 if k == planes - 1 else planes + 1 + k)
        source_ref[0] = edge(False, 2)
        source_ref[planes + 1] = edge(True, 0)
    for k in range(2):
        iterate_ref[k] = edge(False, k)
        iterate_ref[planes + 2 + k] = edge(True, k + with_source)
    for k in range(planes):
        iterate_ref[k + 2] = own(k + with_source)
    copies[0].wait()
    first = wide(first_ref[...])
    for k in range(planes + 2):
        middle = iterate_ref[k + 1]
        diagonal = diagonal_of(diagonal_ref, k, turned, middle.shape)
        remainder = remainder_of(source_ref[k], iterate_ref[k], middle, iterate_ref[k + 2], diagonal)
        step = jnp.dot(first, parts_in_rows(remainder), preferred_element_type=jnp.float32)
        if k == 0:
            step = step * edge_ref[0]
        if k == planes + 1:
            step = step * edge_ref[1]
        step_ref[k] = middle + step

    def emit(k, value):
        if last:
            for j in range(value.shape[0] // CY):
                sent_ref[j, k] = value[j * CY : (j + 1) * CY, :]
        else:
            per_target = value.shape[1] // devices
            put(sent_ref, k, planes, order, sent_ref.shape[0] // devices, [(0, 0, per_target)], value)

    copies[1].wait()
    sweep_all(planes, step_ref, source_ref, diagonal_ref, turned, second_ref, emit)


ANY = pl.BlockSpec(memory_space=pl.ANY)
SMEM = pl.BlockSpec(memory_space=pltpu.SMEM)
VMEM = pl.BlockSpec(memory_space=pltpu.VMEM)
LIMIT = pltpu.CompilerParams(vmem_limit_bytes=20 << 20)


def matrix_scratch(first, second):
    return [pltpu.VMEM(matrix.shape, jnp.float32) for matrix in (first, second)] + [pltpu.SemaphoreType.DMA((2,))]


def first_phase(grid, held, diagonal, first, second):
    rows, columns = diagonal.shape[1:]
    first_count, second_count, planes, per_target = grid
    return pl.pallas_call(
        functools.partial(first_kernel, grid),
        out_shape=(
            jax.ShapeDtypeStruct((2 * columns * planes * rows // 128, 128), jnp.float32),
            jax.ShapeDtypeStruct((planes + 2, rows, columns), jnp.float32),
        ),
        in_specs=[VMEM] * 2 + [ANY] * 2,
        out_specs=(VMEM, VMEM),
        scratch_shapes=[pltpu.VMEM((planes + 2, rows, columns), jnp.float32)] + matrix_scratch(first, second),
        compiler_params=LIMIT,
        name="first_phase",
    )(held, diagonal, first, second)


def later_phase(
    order, planes, rows, turned, edges, held, pair, other, diagonal, first, second, source=None, last=False
):
    columns = second.shape[1]
    length = len(order) * rows
    if last:
        sent = (length // CY, planes, CY, columns)
    else:
        sent = (columns * planes * length // 128, 128)
    out = [jax.ShapeDtypeStruct(sent, jnp.float32)]
    operands = [edges, held, pair, other, diagonal, first, second]
    if source is None:
        out.append(jax.ShapeDtypeStruct((planes + 2, length, columns), jnp.float32))
    else:
        operands.append(source)
    return pl.pallas_call(
        functools.partial(later_kernel, (order, planes, rows, source is None, last, turned)),
        out_shape=tuple(out),
        in_specs=[SMEM] + [VMEM] * 4 + [ANY] * 2 + [VMEM] * (len(operands) - 7),
        out_specs=tuple([VMEM] * len(out)),
        scratch_shapes=[
            pltpu.VMEM((planes + 4, length, columns), jnp.float32),
            pltpu.VMEM((planes + 2, length, columns), jnp.float32),
        ]
        + matrix_scratch(first, second),
        compiler_params=LIMIT,
        name="later_phase",
    )(*operands)


def join_kernel(order, even_ref, source_ref, x_pair_ref, x_other_ref, y_pair_ref, y_other_ref, brick_ref, sent_ref, turned_ref):
    x_even, y_even = even_ref[0] > 0, even_ref[1] > 0
    y_before = jnp.where(y_even, y_other_ref[...], y_pair_ref[...])
    y_after = jnp.where(y_even, y_pair_ref[...], y_other_ref[...])
    for i in range(CX):
        here = slice(i * CY, (i + 1) * CY)
        value = source_ref[here, :]
        if i == 0:
            value = value + jnp.where(x_even, x_other_ref[...], x_pair_ref[...])
        if i == CX - 1:
            value = value + jnp.where(x_even, x_pair_ref[...], x_other_ref[...])
        row = rows_iota(CY, NZ)
        value = value + jnp.where(row == 0, y_before[i : i + 1, :], 0.0)
        brick_ref[here, :] = value + jnp.where(row == CY - 1, y_after[i : i + 1, :], 0.0)
    half = CX // 2
    planes = sent_ref.shape[1] // half
    turned_ref[:8, :] = jnp.zeros((8, 2 * CY), jnp.float32)
    turned_ref[NZ + 8 :, :] = jnp.zeros((8, 2 * CY), jnp.float32)
    for i in range(half):
        both = [brick_ref[j * CY : (j + 1) * CY, :] for j in (i, i + half)]
        turned_ref[8 : NZ + 8, :] = jnp.concatenate(both, axis=0).T
        for j, target in enumerate(order):
            first = 7 + j * (planes - 2)
            sent_ref[target, pl.ds(i, planes, stride=half), :] = turned_ref[first : first + planes, :]


def join(source, even, order, *faces):
    return pl.pallas_call(
        functools.partial(join_kernel, order),
        out_shape=(
            jax.ShapeDtypeStruct(source.shape, jnp.float32),
            jax.ShapeDtypeStruct((len(order), (NZ // len(order) + 2) * CX // 2, 2 * CY), jnp.float32),
        ),
        in_specs=[SMEM] + [VMEM] * 5,
        out_specs=(VMEM, VMEM),
        scratch_shapes=[pltpu.VMEM((NZ + 16, 2 * CY), jnp.float32)],
        compiler_params=LIMIT,
        name="join",
    )(even, source, *faces)


def slab_order(first_count, second_count):
    order = []
    for i in range(first_count):
        row = [i * second_count + j for j in range(second_count)]
        order += row if i % 2 == 0 else row[::-1]
    return order


def place_in_row(j):
    return jnp.where(lax.axis_index("bx") % 2 == 0, j, lax.axis_size("by") - 1 - j)


def beside(to_next, to_previous, even):
    order = slab_order(lax.axis_size("bx"), lax.axis_size("by"))
    got = []
    for start, value in ((0, jnp.where(even, to_next, to_previous)), (1, jnp.where(even, to_previous, to_next))):
        pairs = [(order[i], order[i + 1]) for i in range(start, len(order) - 1, 2)]
        got.append(lax.ppermute(value, EVERY, pairs + [(j, i) for i, j in pairs]))
    return got


def exchange(value):
    return lax.all_to_all(value, EVERY, split_axis=0, concat_axis=0, tiled=True)


def x_slab_source(brick, even):
    second_count = lax.axis_size("by")
    mine = lax.axis_index("by")
    brick = brick.reshape(CX, CY, NZ)
    thick = CX // second_count
    slab = jnp.zeros((thick, second_count * CY, NZ), jnp.float32)
    for turn in range(second_count):
        partner = mine ^ turn
        piece = lax.dynamic_slice_in_dim(brick, place_in_row(partner) * thick, thick, 0)
        if turn:
            piece = lax.ppermute(piece, "by", [(i, i ^ turn) for i in range(second_count)])
        slab = lax.dynamic_update_slice_in_dim(slab, piece, partner * CY, 1)
    pair, other = beside(slab[-1:], slab[:1], even)
    return jnp.concatenate([jnp.where(even, other, pair), slab, jnp.where(even, pair, other)], axis=0)


def relax(brick, sent, levels, rows_inverse, columns_inverse, depth_inverse):
    first_count, second_count = lax.axis_size("bx"), lax.axis_size("by")
    devices = first_count * second_count
    order = slab_order(first_count, second_count)
    me = lax.axis_index("bx") * second_count + place_in_row(lax.axis_index("by"))
    even = me % 2 == 0
    nx, ny = first_count * CX, second_count * CY
    thick = (NZ // devices, ny // devices, nx // devices)
    diagonal = 6.0 + screen_base * (1.0 + levels.reshape(first_count, second_count))
    diagonal = jnp.repeat(jnp.repeat(diagonal, CX, 0), CY, 1)
    padded = jnp.pad(diagonal, ((1, 1), (1, 1)), constant_values=1.0)
    diagonals = (
        diagonal[None],
        lax.dynamic_slice_in_dim(padded, me * thick[1], thick[1] + 2, 1).T[:, None, 1:-1],
        lax.dynamic_slice_in_dim(padded, me * thick[2], thick[2] + 2, 0)[:, None, 1:-1],
    )
    edges = jnp.stack([me > 0, me < devices - 1, even]).astype(jnp.float32)
    matrices = (rows_inverse, columns_inverse, depth_inverse)
    held, diagonals = lax.optimization_barrier((exchange(sent), diagonals))
    sent, z_source = first_phase(
        (first_count, second_count, thick[0], thick[1]), held.reshape(-1, 2 * CY), diagonals[0], matrices[0], matrices[1]
    )
    sources = [z_source, None, None]
    for step in range(1, 3 * ITERS // 2):
        at = step % 3
        planes, rows = thick[at], thick[(at + 2) % 3]
        held = exchange(sent)
        if step == 1:
            held, sources[2] = lax.optimization_barrier((held, x_slab_source(brick, even)))
        bands = matrices[(2 * step + 1) % 3].shape[1] // 128
        blocks = held.reshape(devices, bands, -1, 128)
        to_next, to_previous = blocks[:, :, -2 * rows :], blocks[:, :, : 2 * rows]
        if sources[at] is None:
            to_next, to_previous = blocks[:, :, (planes - 1) * rows : (planes + 2) * rows], blocks[:, :, : 3 * rows]
        pair, other = beside(to_next.reshape(-1, 128), to_previous.reshape(-1, 128), even)
        out = later_phase(
            order,
            planes,
            rows,
            at == 2,
            edges,
            held,
            pair,
            other,
            diagonals[at],
            matrices[2 * step % 3],
            matrices[(2 * step + 1) % 3],
            source=sources[at],
            last=step + 1 == 3 * ITERS // 2,
        )
        sent = out[0]
        if sources[at] is None:
            sources[at] = out[1]
    sent = sent.reshape(second_count * thick[2], CY, NZ)
    return lax.all_to_all(sent, "by", split_axis=0, concat_axis=0, tiled=True)


def local(normals, owners, cells, levels, rows_inverse, columns_inverse, depth_inverse):
    bricks = lax.axis_size(EVERY)
    point_count = cells.shape[0]
    capacity = 2 * point_count // bricks
    chunks = bricks * capacity // 128
    send, slot = pack(owners, cells, normals, levels, bricks, capacity)
    held = exchange(send)
    levels = held[:, 4 * capacity // 128, 0]
    if not grouped(bricks, capacity):
        held = held[:, : 4 * capacity // 128].reshape(bricks, 4, capacity)
        held = held.transpose(1, 0, 2).reshape(4 * chunks, 128)
    even = jnp.stack([lax.axis_index("bx") % 2 == 0, lax.axis_index("by") % 2 == 0]).astype(jnp.int32)
    source, x_pair, x_other, y_pair, y_other, cell_rows, bounds = splat(held, even, chunks)
    faces = swaps(x_pair, x_other, "bx") + swaps(y_pair, y_other, "by")
    brick, sent = join(source, even, slab_order(lax.axis_size("bx"), lax.axis_size("by")), *faces)
    held = relax(brick, sent, levels, rows_inverse, columns_inverse, depth_inverse)
    flip = (lax.axis_index("bx") % 2).astype(jnp.int32).reshape(1)
    held = held.reshape(CX * CY, NZ)
    sampled, iterate = sample(cell_rows, bounds, held, flip, lax.axis_size("by"), bricks, capacity)
    if sampled.ndim == 2:
        sampled = sampled.reshape(bricks, capacity)
    implicit = unpack(owners, slot, exchange(sampled).reshape(bricks, capacity))
    return (iterate.reshape(CX, CY, NZ), implicit)


def solution(mesh):
    placed = (
        P(None, ("bx", "by")),
        P(("bx", "by"), None),
        P(("bx", "by")),
        P("bx", "by"),
        P(),
        P(),
        P(),
    )
    return jax.shard_map(
        local,
        mesh=mesh,
        in_specs=placed,
        out_specs=(P("bx", "by", None), P(("bx", "by"))),
        check_vma=False,
    )
```

```python
import functools

import jax
import jax.numpy as jnp
from jax import lax
from jax.experimental import pallas as pl
from jax.experimental.pallas import tpu as pltpu
from jax.sharding import PartitionSpec as P

CX = 16
CY = 64
NZ = 256
ITERS = 4
EVERY = ("bx", "by")


screen_base = 1.0


def parts_of(value, count):
    parts = []
    for _ in range(count):
        part = value.astype(jnp.bfloat16)
        parts.append(part)
        value = value - part.astype(jnp.float32)
    return parts


def rows_iota(rows, columns):
    return lax.broadcasted_iota(jnp.int32, (rows, columns), 0)


def flags(condition):
    return jnp.where(condition, 1.0, 0.0)


def whole_arrays(count):
    return [pl.BlockSpec(memory_space=pltpu.VMEM)] * count


def product(rows, columns):
    rows, columns = jnp.concatenate(rows, axis=1), jnp.concatenate(columns, axis=1)
    return lax.dot_general(rows, columns, (((1,), (1,)), ((), ())), preferred_element_type=jnp.float32)


def pack_kernel(
    level_ref, owner_any, cell_any, normal_any, send_ref, slot_ref, total_ref, owner_ref, cell_ref, normal_ref, sem_ref
):
    bricks, capacity = send_ref.shape[0], total_ref.shape[1]
    points = owner_ref.shape[1]
    block = 256
    copies = fetch([(owner_any, owner_ref), (cell_any, cell_ref), (normal_any, normal_ref)], sem_ref)
    earlier = rows_iota(block, block) < lax.broadcasted_iota(jnp.int32, (block, block), 1)
    total_ref[...] = jnp.zeros_like(total_ref)
    for copy in copies:
        copy.wait()

    def names(at):
        here = pl.ds(pl.multiple_of(at * block, block), block)
        named = flags(rows_iota(bricks, block) == owner_ref[:, here])
        x = cell_ref[:, here] >> 14
        return here, named, x, flags(rows_iota(CX, block) == x)

    def tally(named, x_hot):
        return product([x_hot.astype(jnp.bfloat16)], [named.astype(jnp.bfloat16)])

    def count(at, counts):
        _, named, _, x_hot = names(at)
        return counts + tally(named, x_hot)

    counts = lax.fori_loop(0, points // block, count, jnp.zeros((CX, bricks), jnp.float32), unroll=4)
    ahead, shift, shifts = jnp.zeros((1, bricks), jnp.float32), jnp.zeros((1, bricks), jnp.float32), []
    for i in range(CX):
        shift = jnp.maximum(shift, float(i * capacity // CX) - ahead)
        shifts.append(shift)
        ahead = ahead + counts[i : i + 1, :]
    shifts = jnp.concatenate(shifts, axis=0)

    def step(at, seen):
        here, named, x, x_hot = names(at)
        x_less = flags(rows_iota(CX, block) < x)
        own = jnp.dot(
            jnp.concatenate([counts, seen, shifts], axis=0).astype(jnp.bfloat16),
            named.astype(jnp.bfloat16),
            preferred_element_type=jnp.float32,
        )
        ahead = jnp.sum(x_less * own[:CX] + x_hot * own[CX : 2 * CX], axis=0, keepdims=True)
        used = jnp.sum(own[:CX], axis=0, keepdims=True)
        moved = jnp.minimum(jnp.sum(x_hot * own[2 * CX :], axis=0, keepdims=True), capacity - used)
        key = (owner_ref[:, here] * CX + x).astype(jnp.float32)
        column = jnp.broadcast_to(key, (128, block)).T
        same = (jnp.concatenate([column] * (block // 128), axis=1) == key) & earlier
        place = ahead + jnp.sum(flags(same), axis=0, keepdims=True) + moved
        slot_ref[:, here] = place
        slot = flags(rows_iota(capacity, block).astype(jnp.float32) == place).astype(jnp.bfloat16)
        values = []
        for k in range(3):
            values += [part.astype(jnp.float32) for part in parts_of(normal_ref[k : k + 1, here], 3)]
        cell = cell_ref[:, here] + 1
        for shift in (16, 8, 0):
            values.append(((cell >> shift) & 255).astype(jnp.float32))
        rows = jnp.concatenate([(named * value).astype(jnp.bfloat16) for value in values], axis=0)
        total_ref[...] += product([rows], [slot])
        return seen + tally(named, x_hot)

    lax.fori_loop(0, points // block, step, jnp.zeros((CX, bricks), jnp.float32), unroll=2)
    part = lambda i: total_ref[i * bricks : (i + 1) * bricks, :]
    fields = [part(3 * k) + part(3 * k + 1) + part(3 * k + 2) for k in range(3)]
    fields.append(part(9) * 65536.0 + part(10) * 256.0 + part(11))
    row = jnp.concatenate(fields, axis=1)
    used = row.shape[1] // 128
    for j in range(used):
        send_ref[:, j, :] = row[:, 128 * j : 128 * (j + 1)]
    level = jnp.full((bricks, send_ref.shape[1] - used, 128), level_ref[0, 0])
    send_ref[:, used:, :] = level.astype(jnp.float32)


def pack(owners, cells, normals, levels, bricks, capacity):
    points = cells.shape[0]
    return pl.pallas_call(
        pack_kernel,
        out_shape=(
            jax.ShapeDtypeStruct((bricks, 4 * capacity // 128 // 8 * 8 + 8, 128), jnp.float32),
            jax.ShapeDtypeStruct((1, points), jnp.float32),
        ),
        in_specs=[pl.BlockSpec(memory_space=pltpu.SMEM)] + [pl.BlockSpec(memory_space=pl.ANY)] * 3,
        out_specs=tuple(whole_arrays(2)),
        scratch_shapes=[
            pltpu.VMEM((12 * bricks, capacity), jnp.float32),
            pltpu.VMEM((1, points), jnp.int32),
            pltpu.VMEM((1, points), jnp.int32),
            pltpu.VMEM((3, points), jnp.float32),
            pltpu.SemaphoreType.DMA((3,)),
        ],
        compiler_params=pltpu.CompilerParams(vmem_limit_bytes=16 << 20),
        name="pack",
    )(levels, owners.reshape(1, points), cells.reshape(1, points), normals)


def unpack_kernel(owner_ref, rank_ref, held_ref, out_ref):
    bricks, capacity = held_ref.shape
    points = owner_ref.shape[1]
    block = 512
    held = jnp.concatenate([part.astype(jnp.float32).T for part in parts_of(held_ref[...], 3)], axis=1)
    held = held.astype(jnp.bfloat16)
    for at in range(points // block):
        here = slice(at * block, (at + 1) * block)
        named = flags(rows_iota(bricks, block) == owner_ref[:, here]).astype(jnp.bfloat16)
        named = jnp.concatenate([named] * 3, axis=0)
        found = jnp.dot(held, named, preferred_element_type=jnp.float32)
        slot = rows_iota(capacity, block).astype(jnp.float32) == rank_ref[:, here]
        out_ref[:, here] = jnp.sum(jnp.where(slot, found, 0.0), axis=0, keepdims=True)


def unpack(owners, rank, held):
    points = owners.shape[0]
    out = pl.pallas_call(
        unpack_kernel,
        out_shape=jax.ShapeDtypeStruct((1, points), jnp.float32),
        in_specs=whole_arrays(3),
        out_specs=pl.BlockSpec(memory_space=pltpu.VMEM),
        compiler_params=pltpu.CompilerParams(vmem_limit_bytes=16 << 20),
        name="unpack",
    )(owners.reshape(1, points), rank, held)
    return out.reshape(points)


def spread(row):
    return jnp.broadcast_to(row, (16, 128)).astype(jnp.bfloat16)


def times_row(table, row16):
    rows = table.shape[0]
    return (table.reshape(rows // 16, 16, 128) * row16[None]).reshape(rows, 128)


def places(cell_row):
    cell = cell_row.astype(jnp.int32) - 1
    return cell >> 14, (cell >> 8) & (CY - 1), cell & (NZ - 1)


GROUP = 4
WINDOW = 4


def units_turned(tile):
    row = rows_iota(8, 128)
    unit = lax.broadcasted_iota(jnp.int32, (8, 128), 1) // 16
    for bit in (4, 2, 1):
        low, high = (row & bit) == 0, (unit & bit) != 0
        from_below = pltpu.roll(pltpu.roll(tile, 8 - bit, 0), 16 * bit, 1)
        from_above = pltpu.roll(pltpu.roll(tile, bit, 0), 128 - 16 * bit, 1)
        tile = jnp.where(low & high, from_below, jnp.where(low | high, tile, from_above))
    return tile


def grouped(bricks, capacity):
    return capacity % 128 == 0 and bricks % 8 == 0


def regroup(held_ref, field_ref):
    bricks = held_ref.shape[0]
    chunks = field_ref.shape[0] // 4
    halves, blocks = chunks // bricks, bricks // 8
    for k in range(4):
        for half in range(halves):
            for block in range(blocks):
                tile = held_ref[8 * block : 8 * (block + 1), halves * k + half, :]
                here = pl.ds(k * chunks + 8 * half * blocks + block, 8, stride=blocks)
                field_ref[here, :] = units_turned(tile)


def splat_kernel(
    even_ref,
    held_ref,
    source_ref,
    x_pair_ref,
    x_other_ref,
    y_pair_ref,
    y_other_ref,
    cell_ref,
    bound_ref,
    field_ref,
    sum_ref,
    column_ref,
):
    chunks = field_ref.shape[0] // 4
    points = 128 * GROUP
    if len(held_ref.shape) == 3:
        regroup(held_ref, field_ref)
    else:
        field_ref[...] = held_ref[...]
    cell_ref[...] = field_ref[3 * chunks :, :]
    for at in range(chunks // GROUP):
        cell = cell_ref[GROUP * at : GROUP * (at + 1), :]
        x = places(cell)[0].astype(jnp.float32)
        bound_ref[at, 0] = jnp.min(jnp.where(cell > 0, x, float(CX))).astype(jnp.int32)
        bound_ref[at, 1] = jnp.max(jnp.where(cell > 0, x, -1.0)).astype(jnp.int32)
    sum_ref[...] = jnp.zeros_like(sum_ref)

    def group(at, carry):
        first, last = bound_ref[at, 0], bound_ref[at, 1]
        cells = []
        for member in range(GROUP):
            chunk = GROUP * at + member
            x, y, z = places(field_ref[pl.ds(3 * chunks + chunk, 1), :])
            z_hot = flags(rows_iota(NZ, 128) == z).astype(jnp.bfloat16)
            for k in range(3):
                parts = parts_of(field_ref[pl.ds(k * chunks + chunk, 1), :], 2)
                for j, part in enumerate(parts):
                    here = slice(j * points + 128 * member, j * points + 128 * (member + 1))
                    column_ref[k * NZ : (k + 1) * NZ, here] = times_row(z_hot, spread(part.astype(jnp.float32)))
            cells.append((x, flags(rows_iota(CY, 128) == y).astype(jnp.bfloat16)))

        def window(turn, carry):
            start = first + turn * WINDOW
            rows = []
            for x, y_hot in cells:
                hots = [spread(flags(x == start + i)) for i in range(WINDOW)]
                rows.append(jnp.concatenate([times_row(y_hot, hot) for hot in hots], axis=0))
            here = pl.ds(pl.multiple_of(start * CY, CY), WINDOW * CY)
            sum_ref[here, :] += product(rows * 2, [column_ref[...]])
            return carry

        window(0, 0)
        lax.fori_loop(1, jnp.maximum(last - first, 0) // WINDOW + 1, window, 0)
        return carry

    lax.fori_loop(0, chunks // GROUP, group, 0)
    row = rows_iota(CY, NZ)
    lane = lax.broadcasted_iota(jnp.int32, (CY, NZ), 1)

    def part(i, k):
        return sum_ref[i * CY : (i + 1) * CY, k * NZ : (k + 1) * NZ]

    for i in range(CX):
        y_part, z_part = part(i, 1), part(i, 2)
        value = jnp.where(row == CY - 1, 0.0, pltpu.roll(y_part, CY - 1, 0)) - jnp.where(row == 0, 0.0, pltpu.roll(y_part, 1, 0))
        value += jnp.where(lane == NZ - 1, 0.0, pltpu.roll(z_part, NZ - 1, 1)) - jnp.where(lane == 0, 0.0, pltpu.roll(z_part, 1, 1))
        if i < CX - 1:
            value += part(i + 1, 0)
        if i > 0:
            value -= part(i - 1, 0)
        source_ref[i * CY : (i + 1) * CY, :] = -0.5 * value
    before, after = -0.5 * part(0, 0), 0.5 * part(CX - 1, 0)
    x_pair_ref[...] = jnp.where(even_ref[0] > 0, after, before)
    x_other_ref[...] = jnp.where(even_ref[0] > 0, before, after)
    y_part = slice(NZ, 2 * NZ)
    before = -0.5 * jnp.concatenate([sum_ref[i * CY : i * CY + 1, y_part] for i in range(CX)], axis=0)
    after = 0.5 * jnp.concatenate([sum_ref[(i + 1) * CY - 1 : (i + 1) * CY, y_part] for i in range(CX)], axis=0)
    y_pair_ref[...] = jnp.where(even_ref[1] > 0, after, before)
    y_other_ref[...] = jnp.where(even_ref[1] > 0, before, after)


def splat(held, even, chunks):
    shapes = [(CX * CY, NZ), (CY, NZ), (CY, NZ), (CX, NZ), (CX, NZ), (chunks, 128)]
    out = [jax.ShapeDtypeStruct(shape, jnp.float32) for shape in shapes]
    return pl.pallas_call(
        splat_kernel,
        out_shape=tuple(out + [jax.ShapeDtypeStruct((chunks // GROUP, 2), jnp.int32)]),
        in_specs=[pl.BlockSpec(memory_space=pltpu.SMEM)] + whole_arrays(1),
        out_specs=tuple(whole_arrays(6) + [pl.BlockSpec(memory_space=pltpu.SMEM)]),
        scratch_shapes=[
            pltpu.VMEM((4 * chunks, 128), jnp.float32),
            pltpu.VMEM(((CX + WINDOW) * CY, 3 * NZ), jnp.float32),
            pltpu.VMEM((3 * NZ, 2 * GROUP * 128), jnp.bfloat16),
        ],
        compiler_params=pltpu.CompilerParams(vmem_limit_bytes=16 << 20),
        name="splat",
    )(even, held)


def sample_kernel(blocks, flip_ref, bound_ref, field_ref, held_ref, out_ref, iterate_ref, turned_ref, sampled_ref):
    chunks = field_ref.shape[0]
    turned_ref[:, CX * CY :] = jnp.zeros((2 * NZ, turned_ref.shape[1] - CX * CY), jnp.bfloat16)
    for i in range(CX * CY // 128):
        here = slice(128 * i, 128 * (i + 1))
        per_block = CX * CY // 128 // blocks
        place = i // per_block
        place = jnp.where(flip_ref[0] > 0, blocks - 1 - place, place) * per_block + i % per_block
        block = held_ref[pl.ds(pl.multiple_of(place * 128, 128), 128), :]
        iterate_ref[here, :] = block
        high, low = parts_of(block.T, 2)
        turned_ref[:NZ, here] = high
        turned_ref[NZ:, here] = low
    width = 4

    def group(at, carry):
        first, last = bound_ref[at, 0] // 2 * 2, bound_ref[at, 1]
        cells = [places(field_ref[pl.ds(GROUP * at + member, 1), :]) for member in range(GROUP)]
        level = rows_iota(NZ, 128 * GROUP) == jnp.concatenate([z for _, _, z in cells], axis=1)

        def window(turn, total):
            start = first + turn * width
            tables = []
            for x, y, _ in cells:
                y_hot = flags(rows_iota(CY, 128) == y).astype(jnp.bfloat16)
                hots = [spread(flags(x == start + i)) for i in range(width)]
                tables.append(jnp.concatenate([times_row(y_hot, hot) for hot in hots], axis=0))
            here = pl.ds(pl.multiple_of(start * CY, 128), width * CY)
            found = jnp.dot(turned_ref[:, here], jnp.concatenate(tables, axis=1), preferred_element_type=jnp.float32)
            found = jnp.where(level, found[:NZ] + found[NZ:], 0.0)
            return total + jnp.sum(found, axis=0, keepdims=True)

        turns = jnp.maximum(last - first, 0) // width + 1
        row = lax.fori_loop(1, turns, window, window(0, jnp.zeros((1, 128 * GROUP), jnp.float32)))
        for member in range(GROUP):
            sampled_ref[pl.ds(GROUP * at + member, 1), :] = row[:, 128 * member : 128 * (member + 1)]
        return carry

    lax.fori_loop(0, chunks // GROUP, group, 0)
    if len(out_ref.shape) == 2:
        out_ref[...] = sampled_ref[...]
        return
    bricks, halves = out_ref.shape[:2]
    for half in range(halves):
        for block in range(bricks // 8):
            tile = sampled_ref[pl.ds(8 * half * (bricks // 8) + block, 8, stride=bricks // 8), :]
            out_ref[8 * block : 8 * (block + 1), half, :] = units_turned(tile)


def sample(cell_rows, bounds, held, flip, blocks, bricks, capacity):
    turned = (bricks, capacity // 128, 128)
    if not grouped(bricks, capacity):
        turned = cell_rows.shape
    return pl.pallas_call(
        functools.partial(sample_kernel, blocks),
        out_shape=tuple(jax.ShapeDtypeStruct(shape, jnp.float32) for shape in (turned, held.shape)),
        in_specs=[pl.BlockSpec(memory_space=pltpu.SMEM)] * 2 + whole_arrays(2),
        out_specs=tuple(whole_arrays(2)),
        scratch_shapes=[
            pltpu.VMEM((2 * NZ, CX * CY + 256), jnp.bfloat16),
            pltpu.VMEM(cell_rows.shape, jnp.float32),
        ],
        compiler_params=pltpu.CompilerParams(vmem_limit_bytes=16 << 20),
        name="sample",
    )(flip, bounds, cell_rows, held)


def swaps(pair, other, axis):
    peers = lax.axis_size(axis)
    got = []
    for start, value in ((0, pair), (1, other)):
        pairs = [(i, i + 1) for i in range(start, peers - 1, 2)]
        got.append(lax.ppermute(value, axis, pairs + [(j, i) for i, j in pairs]))
    return got


def parts_in_rows(value):
    high, low = parts_of(value, 2)
    return jnp.concatenate([high, low, high], axis=0)


def wide(matrix):
    high, low = parts_of(matrix, 2)
    return jnp.concatenate([high, high, low], axis=1)


def shifted(value, axis, back):
    length = value.shape[axis]
    moved = pltpu.roll(value, length - 1 if back else 1, axis)
    index = lax.broadcasted_iota(jnp.int32, value.shape, axis)
    return jnp.where(index == (length - 1 if back else 0), 0.0, moved)


def remainder_of(source, before, middle, after, diagonal):
    beside = before + after
    beside = beside + shifted(middle, 0, False) + shifted(middle, 0, True)
    beside = beside + shifted(middle, 1, False) + shifted(middle, 1, True)
    return source - (diagonal * middle - beside)


def pieces(ref, order, per_source, start, rows, bands, per_band):
    columns = []
    for band in range(bands):
        starts = [i * per_source + band * per_band + start for i in order]
        columns.append(jnp.concatenate([ref[at : at + rows, :] for at in starts], axis=0))
    return jnp.concatenate(columns, axis=1)


def put(sent_ref, k, planes, order, per_block, runs, value):
    turned = value.T
    per_target = turned.shape[0] // len(order)
    for j, target in enumerate(order):
        for band in range(turned.shape[1] // 128):
            columns = slice(band * 128, (band + 1) * 128)
            start = target * per_block + band * (per_block * 128 // turned.shape[1]) + k
            for place, first, count in runs:
                if count:
                    part = turned[j * per_target + first : j * per_target + first + count, columns]
                    sent_ref[pl.ds(start + place * planes, count, stride=planes), :] = part


def brick_planes(ref, first_count, second_count, planes, k):
    bands = []
    lane = lax.broadcasted_iota(jnp.int32, (8, 128), 1)
    for i in range(first_count):
        tiles = []
        for j in range(second_count):
            start = ((i * second_count + j) * planes + k) * 8
            tiles.append(ref[start : start + 8, :])
        turned = [pltpu.roll(tile, 64, 1) for tile in tiles]
        pairs = range(0, second_count, 2)
        bands.append(jnp.concatenate([jnp.where(lane < 64, tiles[j], turned[j + 1]) for j in pairs], axis=1))
        bands.append(jnp.concatenate([jnp.where(lane < 64, turned[j], tiles[j + 1]) for j in pairs], axis=1))
    return jnp.concatenate(bands, axis=0)


def diagonals(layout, counts, planes, level_ref, me, shape):
    first_count, second_count = counts

    def row(count, width, at):
        block = lax.broadcasted_iota(jnp.int32, (1, count * width), 1) // width
        value = jnp.zeros((1, count * width), jnp.float32)
        for i in range(count):
            value = jnp.where(block == i, level_ref[at(i)], value)
        return 6.0 + screen_base * (1.0 + value)

    if layout == 0:
        rows = [row(second_count, CY, lambda j: i * second_count + j) for i in range(first_count)]
        whole = jnp.concatenate([jnp.broadcast_to(value, (CX, shape[1])) for value in rows], axis=0)
        return lambda k: whole

    def along_x(k):
        i = jnp.clip(me * planes - 1 + k, 0, first_count * CX - 1) // CX
        column = jnp.broadcast_to(row(second_count, CY, lambda j: i * second_count + j), (128, shape[0])).T
        return jnp.concatenate([column] * (shape[1] // 128), axis=1)

    def along_y(k):
        j = jnp.clip(me * planes - 1 + k, 0, second_count * CY - 1) // CY
        return row(first_count, CX, lambda i: i * second_count + j)

    return along_x if layout == 2 else along_y


def fetch(pairs, sem_ref):
    copies = [pltpu.make_async_copy(source, held, sem_ref.at[i]) for i, (source, held) in enumerate(pairs)]
    for copy in copies:
        copy.start()
    return copies


def sweep_all(count, step_ref, source_ref, diagonal, matrix_ref, emit):
    matrix = wide(matrix_ref[...])
    for k in range(count):
        middle = step_ref[k + 1]
        remainder = remainder_of(source_ref[k + 1], step_ref[k], middle, step_ref[k + 2], diagonal(k + 1))
        high, low = parts_of(remainder, 2)
        row = jnp.concatenate([high, low, high], axis=1)
        step = lax.dot_general(row, matrix, (((1,), (1,)), ((), ())), preferred_element_type=jnp.float32)
        emit(k, middle + step)


def first_kernel(
    grid, level_ref, held_ref, first_any, second_any, sent_ref, source_ref, step_ref, first_ref, second_ref, sem_ref
):
    copies = fetch([(first_any, first_ref), (second_any, second_ref)], sem_ref)
    first_count, second_count, planes, per_target = grid
    for k in range(planes + 2):
        source_ref[k] = brick_planes(held_ref, first_count, second_count, planes + 2, k)
    copies[0].wait()
    first = wide(first_ref[...])
    for k in range(planes + 2):
        step_ref[k] = jnp.dot(first, parts_in_rows(source_ref[k]), preferred_element_type=jnp.float32)
    order = slab_order(first_count, second_count)
    block = sent_ref.shape[0] // len(order)

    def emit(k, value):
        last = sent_ref.shape[0] * 128 // (2 * planes * len(order) * value.shape[0]) - 1
        put(sent_ref, k, planes, order, block, [(0, 0, 1), (last + 2, last, 1), (last + 3, 1, last - 1)], source_ref[k + 1])
        put(sent_ref, k, planes, order, block, [(1, 0, last + 1)], value)

    copies[1].wait()
    diagonal = diagonals(0, grid[:2], planes, level_ref, 0, step_ref.shape[1:])
    sweep_all(planes, step_ref, source_ref, diagonal, second_ref, emit)


def later_kernel(
    shape, edge_ref, level_ref, held_ref, pair_ref, other_ref, first_any, second_any, *refs
):
    order, planes, rows, with_source, last, layout, counts = shape
    devices = len(order)
    *refs, first_ref, second_ref, sem_ref = refs
    copies = fetch([(first_any, first_ref), (second_any, second_ref)], sem_ref)
    even = edge_ref[2] > 0
    if with_source:
        sent_ref, source_ref, iterate_ref, step_ref = refs
    else:
        source_ref, sent_ref, iterate_ref, step_ref = refs
    bands = iterate_ref.shape[2] // 128
    block, edge_block = held_ref.shape[0] // devices, pair_ref.shape[0] // devices
    per_band = block // bands
    edge_band = edge_block // bands
    own = lambda place: pieces(held_ref, order, block, place * rows, rows, bands, per_band)

    def edge(after, k):
        pair, other = [pieces(ref, order, edge_block, k * rows, rows, bands, edge_band) for ref in (pair_ref, other_ref)]
        return jnp.where(even, pair, other) if after else jnp.where(even, other, pair)

    if with_source:
        for k in range(planes):
            source_ref[k + 1] = own(0 if k == 0 else planes + 1 if k == planes - 1 else planes + 1 + k)
        source_ref[0] = edge(False, 2)
        source_ref[planes + 1] = edge(True, 0)
    for k in range(2):
        iterate_ref[k] = edge(False, k)
        iterate_ref[planes + 2 + k] = edge(True, k + with_source)
    for k in range(planes):
        iterate_ref[k + 2] = own(k + with_source)
    diagonal = diagonals(layout, counts, planes, level_ref, edge_ref[3], step_ref.shape[1:])
    copies[0].wait()
    first = wide(first_ref[...])
    for k in range(planes + 2):
        middle = iterate_ref[k + 1]
        remainder = remainder_of(source_ref[k], iterate_ref[k], middle, iterate_ref[k + 2], diagonal(k))
        step = jnp.dot(first, parts_in_rows(remainder), preferred_element_type=jnp.float32)
        if k == 0:
            step = step * edge_ref[0].astype(jnp.float32)
        if k == planes + 1:
            step = step * edge_ref[1].astype(jnp.float32)
        step_ref[k] = middle + step

    def emit(k, value):
        if last:
            for j in range(value.shape[0] // CY):
                sent_ref[j, k] = value[j * CY : (j + 1) * CY, :]
        else:
            per_target = value.shape[1] // devices
            put(sent_ref, k, planes, order, sent_ref.shape[0] // devices, [(0, 0, per_target)], value)

    copies[1].wait()
    sweep_all(planes, step_ref, source_ref, diagonal, second_ref, emit)


ANY = pl.BlockSpec(memory_space=pl.ANY)
SMEM = pl.BlockSpec(memory_space=pltpu.SMEM)
VMEM = pl.BlockSpec(memory_space=pltpu.VMEM)
LIMIT = pltpu.CompilerParams(vmem_limit_bytes=20 << 20)


def matrix_scratch(first, second):
    return [pltpu.VMEM(matrix.shape, jnp.float32) for matrix in (first, second)] + [pltpu.SemaphoreType.DMA((2,))]


def first_phase(grid, levels, held, first, second):
    rows, columns = len(first), len(second)
    first_count, second_count, planes, per_target = grid
    return pl.pallas_call(
        functools.partial(first_kernel, grid),
        out_shape=(
            jax.ShapeDtypeStruct((2 * columns * planes * rows // 128, 128), jnp.float32),
            jax.ShapeDtypeStruct((planes + 2, rows, columns), jnp.float32),
        ),
        in_specs=[SMEM, VMEM] + [ANY] * 2,
        out_specs=(VMEM, VMEM),
        scratch_shapes=[pltpu.VMEM((planes + 2, rows, columns), jnp.float32)] + matrix_scratch(first, second),
        compiler_params=LIMIT,
        name="first_phase",
    )(levels, held, first, second)


def later_phase(
    order, planes, rows, layout, counts, edges, levels, held, pair, other, first, second, source=None, last=False
):
    columns = second.shape[1]
    length = len(order) * rows
    if last:
        sent = (length // CY, planes, CY, columns)
    else:
        sent = (columns * planes * length // 128, 128)
    out = [jax.ShapeDtypeStruct(sent, jnp.float32)]
    operands = [edges, levels, held, pair, other, first, second]
    if source is None:
        out.append(jax.ShapeDtypeStruct((planes + 2, length, columns), jnp.float32))
    else:
        operands.append(source)
    return pl.pallas_call(
        functools.partial(later_kernel, (order, planes, rows, source is None, last, layout, counts)),
        out_shape=tuple(out),
        in_specs=[SMEM] * 2 + [VMEM] * 3 + [ANY] * 2 + [VMEM] * (len(operands) - 7),
        out_specs=tuple([VMEM] * len(out)),
        scratch_shapes=[
            pltpu.VMEM((planes + 4, length, columns), jnp.float32),
            pltpu.VMEM((planes + 2, length, columns), jnp.float32),
        ]
        + matrix_scratch(first, second),
        compiler_params=LIMIT,
        name="later_phase",
    )(*operands)


def join_kernel(order, even_ref, source_ref, x_pair_ref, x_other_ref, y_pair_ref, y_other_ref, brick_ref, sent_ref, turned_ref):
    x_even, y_even = even_ref[0] > 0, even_ref[1] > 0
    y_before = jnp.where(y_even, y_other_ref[...], y_pair_ref[...])
    y_after = jnp.where(y_even, y_pair_ref[...], y_other_ref[...])
    for i in range(CX):
        here = slice(i * CY, (i + 1) * CY)
        value = source_ref[here, :]
        if i == 0:
            value = value + jnp.where(x_even, x_other_ref[...], x_pair_ref[...])
        if i == CX - 1:
            value = value + jnp.where(x_even, x_pair_ref[...], x_other_ref[...])
        row = rows_iota(CY, NZ)
        value = value + jnp.where(row == 0, y_before[i : i + 1, :], 0.0)
        brick_ref[here, :] = value + jnp.where(row == CY - 1, y_after[i : i + 1, :], 0.0)
    half = CX // 2
    planes = sent_ref.shape[1] // half
    turned_ref[:8, :] = jnp.zeros((8, 2 * CY), jnp.float32)
    turned_ref[NZ + 8 :, :] = jnp.zeros((8, 2 * CY), jnp.float32)
    for i in range(half):
        both = [brick_ref[j * CY : (j + 1) * CY, :] for j in (i, i + half)]
        turned_ref[8 : NZ + 8, :] = jnp.concatenate(both, axis=0).T
        for j, target in enumerate(order):
            first = 7 + j * (planes - 2)
            sent_ref[target, pl.ds(i, planes, stride=half), :] = turned_ref[first : first + planes, :]


def join(source, even, order, *faces):
    return pl.pallas_call(
        functools.partial(join_kernel, order),
        out_shape=(
            jax.ShapeDtypeStruct(source.shape, jnp.float32),
            jax.ShapeDtypeStruct((len(order), (NZ // len(order) + 2) * CX // 2, 2 * CY), jnp.float32),
        ),
        in_specs=[SMEM] + [VMEM] * 5,
        out_specs=(VMEM, VMEM),
        scratch_shapes=[pltpu.VMEM((NZ + 16, 2 * CY), jnp.float32)],
        compiler_params=LIMIT,
        name="join",
    )(even, source, *faces)


def slab_order(first_count, second_count):
    order = []
    for i in range(first_count):
        row = [i * second_count + j for j in range(second_count)]
        order += row if i % 2 == 0 else row[::-1]
    return order


def place_in_row(j):
    return jnp.where(lax.axis_index("bx") % 2 == 0, j, lax.axis_size("by") - 1 - j)


def beside(to_next, to_previous, even):
    order = slab_order(lax.axis_size("bx"), lax.axis_size("by"))
    got = []
    for start, value in ((1, jnp.where(even, to_previous, to_next)), (0, jnp.where(even, to_next, to_previous))):
        pairs = [(order[i], order[i + 1]) for i in range(start, len(order) - 1, 2)]
        got.append(lax.ppermute(value, EVERY, pairs + [(j, i) for i, j in pairs]))
    return got[::-1]


def exchange(value):
    return lax.all_to_all(value, EVERY, split_axis=0, concat_axis=0, tiled=True)


def x_slab_source(brick, even):
    second_count = lax.axis_size("by")
    mine = lax.axis_index("by")
    brick = brick.reshape(CX, CY, NZ)
    thick = CX // second_count
    slab = jnp.zeros((thick, second_count * CY, NZ), jnp.float32)
    for turn in range(second_count):
        partner = mine ^ turn
        piece = lax.dynamic_slice_in_dim(brick, place_in_row(partner) * thick, thick, 0)
        if turn:
            piece = lax.ppermute(piece, "by", [(i, i ^ turn) for i in range(second_count)])
        slab = lax.dynamic_update_slice_in_dim(slab, piece, partner * CY, 1)
    pair, other = beside(slab[-1:], slab[:1], even)
    return jnp.concatenate([jnp.where(even, other, pair), slab, jnp.where(even, pair, other)], axis=0)


def relax(brick, sent, levels, rows_inverse, columns_inverse, depth_inverse):
    first_count, second_count = lax.axis_size("bx"), lax.axis_size("by")
    devices = first_count * second_count
    order = slab_order(first_count, second_count)
    me = lax.axis_index("bx") * second_count + place_in_row(lax.axis_index("by"))
    even = me % 2 == 0
    nx, ny = first_count * CX, second_count * CY
    thick = (NZ // devices, ny // devices, nx // devices)
    edges = jnp.stack([me > 0, me < devices - 1, even, me]).astype(jnp.int32)
    matrices = (rows_inverse, columns_inverse, depth_inverse)
    held = exchange(sent)
    sent, z_source = first_phase(
        (first_count, second_count, thick[0], thick[1]), levels, held.reshape(-1, 2 * CY), matrices[0], matrices[1]
    )
    sources = [z_source, None, None]
    for step in range(1, 3 * ITERS // 2):
        at = step % 3
        planes, rows = thick[at], thick[(at + 2) % 3]
        held = exchange(sent)
        if step == 1:
            held, sources[2] = lax.optimization_barrier((held, x_slab_source(brick, even)))
        bands = matrices[(2 * step + 1) % 3].shape[1] // 128
        blocks = held.reshape(devices, bands, -1, 128)
        to_next, to_previous = blocks[:, :, -2 * rows :], blocks[:, :, : 2 * rows]
        if sources[at] is None:
            to_next, to_previous = blocks[:, :, (planes - 1) * rows : (planes + 2) * rows], blocks[:, :, : 3 * rows]
        pair, other = beside(to_next.reshape(-1, 128), to_previous.reshape(-1, 128), even)
        out = later_phase(
            order,
            planes,
            rows,
            at,
            (first_count, second_count),
            edges,
            levels,
            held,
            pair,
            other,
            matrices[2 * step % 3],
            matrices[(2 * step + 1) % 3],
            source=sources[at],
            last=step + 1 == 3 * ITERS // 2,
        )
        sent = out[0]
        if sources[at] is None:
            sources[at] = out[1]
    sent = sent.reshape(second_count * thick[2], CY, NZ)
    return lax.all_to_all(sent, "by", split_axis=0, concat_axis=0, tiled=True)


def local(normals, owners, cells, levels, rows_inverse, columns_inverse, depth_inverse):
    bricks = lax.axis_size(EVERY)
    point_count = cells.shape[0]
    capacity = 2 * point_count // bricks
    chunks = bricks * capacity // 128
    send, slot = pack(owners, cells, normals, levels, bricks, capacity)
    held = exchange(send)
    levels = held[:, 4 * capacity // 128, 0]
    if not grouped(bricks, capacity):
        held = held[:, : 4 * capacity // 128].reshape(bricks, 4, capacity)
        held = held.transpose(1, 0, 2).reshape(4 * chunks, 128)
    even = jnp.stack([lax.axis_index("bx") % 2 == 0, lax.axis_index("by") % 2 == 0]).astype(jnp.int32)
    source, x_pair, x_other, y_pair, y_other, cell_rows, bounds = splat(held, even, chunks)
    faces = swaps(x_pair, x_other, "bx") + swaps(y_pair, y_other, "by")
    brick, sent = join(source, even, slab_order(lax.axis_size("bx"), lax.axis_size("by")), *faces)
    held = relax(brick, sent, levels, rows_inverse, columns_inverse, depth_inverse)
    flip = (lax.axis_index("bx") % 2).astype(jnp.int32).reshape(1)
    held = held.reshape(CX * CY, NZ)
    sampled, iterate = sample(cell_rows, bounds, held, flip, lax.axis_size("by"), bricks, capacity)
    if sampled.ndim == 2:
        sampled = sampled.reshape(bricks, capacity)
    implicit = unpack(owners, slot, exchange(sampled).reshape(bricks, capacity))
    return (iterate.reshape(CX, CY, NZ), implicit)


def solution(mesh):
    placed = (
        P(None, ("bx", "by")),
        P(("bx", "by"), None),
        P(("bx", "by")),
        P("bx", "by"),
        P(),
        P(),
        P(),
    )
    return jax.shard_map(
        local,
        mesh=mesh,
        in_specs=placed,
        out_specs=(P("bx", "by", None), P(("bx", "by"))),
        check_vma=False,
    )
```

```python
import functools

import jax
import jax.numpy as jnp
from jax import lax
from jax.experimental import pallas as pl
from jax.experimental.pallas import tpu as pltpu
from jax.sharding import PartitionSpec as P

CX = 16
CY = 64
NZ = 256
ITERS = 4
EVERY = ("bx", "by")


screen_base = 1.0


def parts_of(value, count):
    parts = []
    for _ in range(count):
        part = value.astype(jnp.bfloat16)
        parts.append(part)
        value = value - part.astype(jnp.float32)
    return parts


def rows_iota(rows, columns):
    return lax.broadcasted_iota(jnp.int32, (rows, columns), 0)


def flags(condition):
    return jnp.where(condition, 1.0, 0.0)


def whole_arrays(count):
    return [pl.BlockSpec(memory_space=pltpu.VMEM)] * count


def product(rows, columns):
    rows, columns = jnp.concatenate(rows, axis=1), jnp.concatenate(columns, axis=1)
    return lax.dot_general(rows, columns, (((1,), (1,)), ((), ())), preferred_element_type=jnp.float32)


def pack_kernel(
    level_ref, owner_any, cell_any, normal_any, send_ref, slot_ref, total_ref, owner_ref, cell_ref, normal_ref, sem_ref
):
    bricks, capacity = send_ref.shape[0], total_ref.shape[1]
    points = owner_ref.shape[1]
    block = 256
    copies = fetch([(owner_any, owner_ref), (cell_any, cell_ref), (normal_any, normal_ref)], sem_ref)
    earlier = rows_iota(block, block) < lax.broadcasted_iota(jnp.int32, (block, block), 1)
    total_ref[...] = jnp.zeros_like(total_ref)
    for copy in copies:
        copy.wait()

    def names(at):
        here = pl.ds(pl.multiple_of(at * block, block), block)
        named = flags(rows_iota(bricks, block) == owner_ref[:, here])
        x = cell_ref[:, here] >> 14
        return here, named, x, flags(rows_iota(CX, block) == x)

    def tally(named, x_hot):
        return product([x_hot.astype(jnp.bfloat16)], [named.astype(jnp.bfloat16)])

    def count(at, counts):
        _, named, _, x_hot = names(at)
        return counts + tally(named, x_hot)

    counts = lax.fori_loop(0, points // block, count, jnp.zeros((CX, bricks), jnp.float32), unroll=4)
    ahead, shift, shifts = jnp.zeros((1, bricks), jnp.float32), jnp.zeros((1, bricks), jnp.float32), []
    for i in range(CX):
        shift = jnp.maximum(shift, float(i * capacity // CX) - ahead)
        shifts.append(shift)
        ahead = ahead + counts[i : i + 1, :]
    shifts = jnp.concatenate(shifts, axis=0)

    def step(at, seen):
        here, named, x, x_hot = names(at)
        x_less = flags(rows_iota(CX, block) < x)
        own = jnp.dot(
            jnp.concatenate([counts, seen, shifts], axis=0).astype(jnp.bfloat16),
            named.astype(jnp.bfloat16),
            preferred_element_type=jnp.float32,
        )
        ahead = jnp.sum(x_less * own[:CX] + x_hot * own[CX : 2 * CX], axis=0, keepdims=True)
        used = jnp.sum(own[:CX], axis=0, keepdims=True)
        moved = jnp.minimum(jnp.sum(x_hot * own[2 * CX :], axis=0, keepdims=True), capacity - used)
        key = (owner_ref[:, here] * CX + x).astype(jnp.float32)
        column = jnp.broadcast_to(key, (128, block)).T
        same = (jnp.concatenate([column] * (block // 128), axis=1) == key) & earlier
        place = ahead + jnp.sum(flags(same), axis=0, keepdims=True) + moved
        slot_ref[:, here] = place
        slot = flags(rows_iota(capacity, block).astype(jnp.float32) == place).astype(jnp.bfloat16)
        values = []
        for k in range(3):
            values += [part.astype(jnp.float32) for part in parts_of(normal_ref[k : k + 1, here], 3)]
        cell = cell_ref[:, here] + 1
        for shift in (16, 8, 0):
            values.append(((cell >> shift) & 255).astype(jnp.float32))
        rows = jnp.concatenate([(named * value).astype(jnp.bfloat16) for value in values], axis=0)
        total_ref[...] += product([rows], [slot])
        return seen + tally(named, x_hot)

    lax.fori_loop(0, points // block, step, jnp.zeros((CX, bricks), jnp.float32), unroll=2)
    part = lambda i: total_ref[i * bricks : (i + 1) * bricks, :]
    fields = [part(3 * k) + part(3 * k + 1) + part(3 * k + 2) for k in range(3)]
    fields.append(part(9) * 65536.0 + part(10) * 256.0 + part(11))
    row = jnp.concatenate(fields, axis=1)
    used = row.shape[1] // 128
    for j in range(used):
        send_ref[:, j, :] = row[:, 128 * j : 128 * (j + 1)]
    level = jnp.full((bricks, send_ref.shape[1] - used, 128), level_ref[0, 0])
    send_ref[:, used:, :] = level.astype(jnp.float32)


def pack(owners, cells, normals, levels, bricks, capacity):
    points = cells.shape[0]
    return pl.pallas_call(
        pack_kernel,
        out_shape=(
            jax.ShapeDtypeStruct((bricks, 4 * capacity // 128 // 8 * 8 + 8, 128), jnp.float32),
            jax.ShapeDtypeStruct((1, points), jnp.float32),
        ),
        in_specs=[pl.BlockSpec(memory_space=pltpu.SMEM)] + [pl.BlockSpec(memory_space=pl.ANY)] * 3,
        out_specs=tuple(whole_arrays(2)),
        scratch_shapes=[
            pltpu.VMEM((12 * bricks, capacity), jnp.float32),
            pltpu.VMEM((1, points), jnp.int32),
            pltpu.VMEM((1, points), jnp.int32),
            pltpu.VMEM((3, points), jnp.float32),
            pltpu.SemaphoreType.DMA((3,)),
        ],
        compiler_params=pltpu.CompilerParams(vmem_limit_bytes=16 << 20),
        name="pack",
    )(levels, owners.reshape(1, points), cells.reshape(1, points), normals)


def unpack_kernel(second_count, owner_ref, rank_ref, held_ref, out_ref):
    bricks = held_ref.shape[0]
    points = owner_ref.shape[1]
    block = 512
    held = held_ref[...]
    if len(held.shape) == 3:
        halves = held.shape[1] // second_count
        rows = []
        for i in range(0, bricks, second_count):
            rows.append(sum([held_ref[i + j] for j in range(second_count)]))
        part = lambda row, half: row[half * second_count : (half + 1) * second_count, :]
        held = jnp.concatenate(
            [jnp.concatenate([part(row, half) for row in rows], axis=0) for half in range(halves)], axis=1
        )
    capacity = held.shape[1]
    held = jnp.concatenate([part.astype(jnp.float32).T for part in parts_of(held, 3)], axis=1)
    held = held.astype(jnp.bfloat16)
    for at in range(points // block):
        here = slice(at * block, (at + 1) * block)
        named = flags(rows_iota(bricks, block) == owner_ref[:, here]).astype(jnp.bfloat16)
        named = jnp.concatenate([named] * 3, axis=0)
        found = jnp.dot(held, named, preferred_element_type=jnp.float32)
        slot = rows_iota(capacity, block).astype(jnp.float32) == rank_ref[:, here]
        out_ref[:, here] = jnp.sum(jnp.where(slot, found, 0.0), axis=0, keepdims=True)


def unpack(owners, rank, held, second_count):
    points = owners.shape[0]
    out = pl.pallas_call(
        functools.partial(unpack_kernel, second_count),
        out_shape=jax.ShapeDtypeStruct((1, points), jnp.float32),
        in_specs=whole_arrays(3),
        out_specs=pl.BlockSpec(memory_space=pltpu.VMEM),
        compiler_params=pltpu.CompilerParams(vmem_limit_bytes=16 << 20),
        name="unpack",
    )(owners.reshape(1, points), rank, held)
    return out.reshape(points)


def spread(row):
    return jnp.broadcast_to(row, (16, 128)).astype(jnp.bfloat16)


def times_row(table, row16):
    rows = table.shape[0]
    return (table.reshape(rows // 16, 16, 128) * row16[None]).reshape(rows, 128)


def places(cell_row):
    cell = cell_row.astype(jnp.int32) - 1
    return cell >> 14, (cell >> 8) & (CY - 1), cell & (NZ - 1)


GROUP = 4
WINDOW = 4


def units_turned(tile):
    row = rows_iota(8, 128)
    unit = lax.broadcasted_iota(jnp.int32, (8, 128), 1) // 16
    for bit in (4, 2, 1):
        low, high = (row & bit) == 0, (unit & bit) != 0
        from_below = pltpu.roll(pltpu.roll(tile, 8 - bit, 0), 16 * bit, 1)
        from_above = pltpu.roll(pltpu.roll(tile, bit, 0), 128 - 16 * bit, 1)
        tile = jnp.where(low & high, from_below, jnp.where(low | high, tile, from_above))
    return tile


def grouped(bricks, capacity):
    return capacity % 128 == 0 and bricks % 8 == 0


def regroup(held_ref, field_ref):
    bricks = held_ref.shape[0]
    chunks = field_ref.shape[0] // 4
    halves, blocks = chunks // bricks, bricks // 8
    for k in range(4):
        for half in range(halves):
            for block in range(blocks):
                tile = held_ref[8 * block : 8 * (block + 1), halves * k + half, :]
                here = pl.ds(k * chunks + 8 * half * blocks + block, 8, stride=blocks)
                field_ref[here, :] = units_turned(tile)


def splat_kernel(
    even_ref,
    held_ref,
    source_ref,
    x_pair_ref,
    x_other_ref,
    y_pair_ref,
    y_other_ref,
    cell_ref,
    bound_ref,
    field_ref,
    sum_ref,
    column_ref,
):
    chunks = field_ref.shape[0] // 4
    points = 128 * GROUP
    if len(held_ref.shape) == 3:
        regroup(held_ref, field_ref)
    else:
        field_ref[...] = held_ref[...]
    cell_ref[:chunks, :] = field_ref[3 * chunks :, :]
    lane = lax.broadcasted_iota(jnp.int32, (8, 128), 1)
    bounds = jnp.zeros((8, 128), jnp.float32)
    for at in range(chunks // GROUP):
        cell = field_ref[3 * chunks + GROUP * at : 3 * chunks + GROUP * (at + 1), :]
        x = places(cell)[0].astype(jnp.float32)
        least, most = jnp.min(jnp.where(cell > 0, x, float(CX))), jnp.max(jnp.where(cell > 0, x, -1.0))
        bound_ref[at, 0], bound_ref[at, 1] = least.astype(jnp.int32), most.astype(jnp.int32)
        bounds = jnp.where(lane == at, jnp.where(rows_iota(8, 128) == 0, least, most), bounds)
    cell_ref[chunks:, :] = bounds
    sum_ref[...] = jnp.zeros_like(sum_ref)

    def group(at, carry):
        first, last = bound_ref[at, 0], bound_ref[at, 1]
        cells = []
        for member in range(GROUP):
            chunk = GROUP * at + member
            x, y, z = places(field_ref[pl.ds(3 * chunks + chunk, 1), :])
            z_hot = flags(rows_iota(NZ, 128) == z).astype(jnp.bfloat16)
            for k in range(3):
                parts = parts_of(field_ref[pl.ds(k * chunks + chunk, 1), :], 2)
                for j, part in enumerate(parts):
                    here = slice(j * points + 128 * member, j * points + 128 * (member + 1))
                    column_ref[k * NZ : (k + 1) * NZ, here] = times_row(z_hot, spread(part.astype(jnp.float32)))
            cells.append((x, flags(rows_iota(CY, 128) == y).astype(jnp.bfloat16)))

        def window(turn, carry):
            start = first + turn * WINDOW
            rows = []
            for x, y_hot in cells:
                hots = [spread(flags(x == start + i)) for i in range(WINDOW)]
                rows.append(jnp.concatenate([times_row(y_hot, hot) for hot in hots], axis=0))
            here = pl.ds(pl.multiple_of(start * CY, CY), WINDOW * CY)
            sum_ref[here, :] += product(rows * 2, [column_ref[...]])
            return carry

        window(0, 0)
        lax.fori_loop(1, jnp.maximum(last - first, 0) // WINDOW + 1, window, 0)
        return carry

    lax.fori_loop(0, chunks // GROUP, group, 0)
    row = rows_iota(CY, NZ)
    lane = lax.broadcasted_iota(jnp.int32, (CY, NZ), 1)

    def part(i, k):
        return sum_ref[i * CY : (i + 1) * CY, k * NZ : (k + 1) * NZ]

    for i in range(CX):
        y_part, z_part = part(i, 1), part(i, 2)
        value = jnp.where(row == CY - 1, 0.0, pltpu.roll(y_part, CY - 1, 0)) - jnp.where(row == 0, 0.0, pltpu.roll(y_part, 1, 0))
        value += jnp.where(lane == NZ - 1, 0.0, pltpu.roll(z_part, NZ - 1, 1)) - jnp.where(lane == 0, 0.0, pltpu.roll(z_part, 1, 1))
        if i < CX - 1:
            value += part(i + 1, 0)
        if i > 0:
            value -= part(i - 1, 0)
        source_ref[i * CY : (i + 1) * CY, :] = -0.5 * value
    before, after = -0.5 * part(0, 0), 0.5 * part(CX - 1, 0)
    x_pair_ref[...] = jnp.where(even_ref[0] > 0, after, before)
    x_other_ref[...] = jnp.where(even_ref[0] > 0, before, after)
    y_part = slice(NZ, 2 * NZ)
    before = -0.5 * jnp.concatenate([sum_ref[i * CY : i * CY + 1, y_part] for i in range(CX)], axis=0)
    after = 0.5 * jnp.concatenate([sum_ref[(i + 1) * CY - 1 : (i + 1) * CY, y_part] for i in range(CX)], axis=0)
    y_pair_ref[...] = jnp.where(even_ref[1] > 0, after, before)
    y_other_ref[...] = jnp.where(even_ref[1] > 0, before, after)


def splat(held, even, chunks):
    shapes = [(CX * CY, NZ), (CY, NZ), (CY, NZ), (CX, NZ), (CX, NZ), (chunks + 8, 128)]
    out = [jax.ShapeDtypeStruct(shape, jnp.float32) for shape in shapes]
    return pl.pallas_call(
        splat_kernel,
        out_shape=tuple(out),
        in_specs=[pl.BlockSpec(memory_space=pltpu.SMEM)] + whole_arrays(1),
        out_specs=tuple(whole_arrays(6)),
        scratch_shapes=[
            pltpu.SMEM((chunks // GROUP, 2), jnp.int32),
            pltpu.VMEM((4 * chunks, 128), jnp.float32),
            pltpu.VMEM(((CX + WINDOW) * CY, 3 * NZ), jnp.float32),
            pltpu.VMEM((3 * NZ, 2 * GROUP * 128), jnp.bfloat16),
        ],
        compiler_params=pltpu.CompilerParams(vmem_limit_bytes=16 << 20),
        name="splat",
    )(even, held)


def sample_kernel(place_ref, bound_ref, cell_ref, slab_ref, out_ref, turned_ref, sampled_ref):
    second_count, thick = slab_ref.shape[:2]
    chunks = sampled_ref.shape[1]
    columns = thick * CY
    start = place_ref[0] * thick
    for j in range(second_count):
        block = jnp.concatenate([slab_ref[j, i] for i in range(thick)], axis=0)
        high, low = parts_of(block.T, 2)
        turned_ref[:NZ, j * columns : (j + 1) * columns] = high
        turned_ref[NZ:, j * columns : (j + 1) * columns] = low
    sampled_ref[...] = jnp.zeros_like(sampled_ref)
    for j in range(second_count):

        def group(at, carry, j=j):
            @pl.when((bound_ref[j, 0, at] < start + thick) & (bound_ref[j, 1, at] >= start))
            def _():
                tables, heights = [], []
                for member in range(GROUP):
                    x, y, z = places(cell_ref[j, pl.ds(GROUP * at + member, 1), :])
                    y_hot = flags(rows_iota(CY, 128) == y).astype(jnp.bfloat16)
                    hots = [spread(flags(x == start + i)) for i in range(thick)]
                    tables.append(jnp.concatenate([times_row(y_hot, hot) for hot in hots], axis=0))
                    heights.append(z)
                level = rows_iota(NZ, 128 * GROUP) == jnp.concatenate(heights, axis=1)
                values = turned_ref[:, j * columns : (j + 1) * columns]
                found = jnp.dot(values, jnp.concatenate(tables, axis=1), preferred_element_type=jnp.float32)
                row = jnp.sum(jnp.where(level, found[:NZ] + found[NZ:], 0.0), axis=0, keepdims=True)
                for member in range(GROUP):
                    here = slice(128 * member, 128 * (member + 1))
                    sampled_ref[j, pl.ds(GROUP * at + member, 1), :] = row[:, here]

            return carry

        lax.fori_loop(0, chunks // GROUP, group, 0)
    if len(out_ref.shape) == 3 and out_ref.shape == sampled_ref.shape:
        out_ref[...] = sampled_ref[...]
        return
    bricks = out_ref.shape[0]
    blocks = bricks // 8
    for j in range(second_count):
        for half in range(chunks // bricks):
            for block in range(blocks):
                tile = sampled_ref[j, pl.ds(8 * half * blocks + block, 8, stride=blocks), :]
                out_ref[8 * block : 8 * (block + 1), half * second_count + j, :] = units_turned(tile)


def sample(place, bounds, cells, slab, chunks, bricks, capacity):
    second_count, thick = slab.shape[:2]
    shape = (second_count, chunks, 128)
    if grouped(bricks, capacity):
        shape = (bricks, second_count * capacity // 128, 128)
    return pl.pallas_call(
        sample_kernel,
        out_shape=jax.ShapeDtypeStruct(shape, jnp.float32),
        in_specs=[pl.BlockSpec(memory_space=pltpu.SMEM)] * 2 + whole_arrays(2),
        out_specs=pl.BlockSpec(memory_space=pltpu.VMEM),
        scratch_shapes=[
            pltpu.VMEM((2 * NZ, second_count * thick * CY), jnp.bfloat16),
            pltpu.VMEM((second_count, chunks, 128), jnp.float32),
        ],
        compiler_params=pltpu.CompilerParams(vmem_limit_bytes=16 << 20),
        cost_estimate=pl.CostEstimate(flops=8 << 30, bytes_accessed=4 << 20, transcendentals=0),
        name="sample",
    )(place, bounds, cells, slab)


def swaps(pair, other, axis):
    peers = lax.axis_size(axis)
    got = []
    for start, value in ((0, pair), (1, other)):
        pairs = [(i, i + 1) for i in range(start, peers - 1, 2)]
        got.append(lax.ppermute(value, axis, pairs + [(j, i) for i, j in pairs]))
    return got


def parts_in_rows(value):
    high, low = parts_of(value, 2)
    return jnp.concatenate([high, low, high], axis=0)


def wide(matrix):
    high, low = parts_of(matrix, 2)
    return jnp.concatenate([high, high, low], axis=1)


def shifted(value, axis, back):
    length = value.shape[axis]
    moved = pltpu.roll(value, length - 1 if back else 1, axis)
    index = lax.broadcasted_iota(jnp.int32, value.shape, axis)
    return jnp.where(index == (length - 1 if back else 0), 0.0, moved)


def remainder_of(source, before, middle, after, diagonal):
    beside = before + after
    beside = beside + shifted(middle, 0, False) + shifted(middle, 0, True)
    beside = beside + shifted(middle, 1, False) + shifted(middle, 1, True)
    return source - (diagonal * middle - beside)


def pieces(ref, order, per_source, start, rows, bands, per_band):
    columns = []
    for band in range(bands):
        starts = [i * per_source + band * per_band + start for i in order]
        columns.append(jnp.concatenate([ref[at : at + rows, :] for at in starts], axis=0))
    return jnp.concatenate(columns, axis=1)


def put(sent_ref, k, planes, order, per_block, runs, value):
    turned = value.T
    per_target = turned.shape[0] // len(order)
    for j, target in enumerate(order):
        for band in range(turned.shape[1] // 128):
            columns = slice(band * 128, (band + 1) * 128)
            start = target * per_block + band * (per_block * 128 // turned.shape[1]) + k
            for place, first, count in runs:
                if count:
                    part = turned[j * per_target + first : j * per_target + first + count, columns]
                    sent_ref[pl.ds(start + place * planes, count, stride=planes), :] = part


def brick_planes(ref, first_count, second_count, planes, k):
    bands = []
    lane = lax.broadcasted_iota(jnp.int32, (8, 128), 1)
    for i in range(first_count):
        tiles = []
        for j in range(second_count):
            start = ((i * second_count + j) * planes + k) * 8
            tiles.append(ref[start : start + 8, :])
        turned = [pltpu.roll(tile, 64, 1) for tile in tiles]
        pairs = range(0, second_count, 2)
        bands.append(jnp.concatenate([jnp.where(lane < 64, tiles[j], turned[j + 1]) for j in pairs], axis=1))
        bands.append(jnp.concatenate([jnp.where(lane < 64, turned[j], tiles[j + 1]) for j in pairs], axis=1))
    return jnp.concatenate(bands, axis=0)


def diagonals(layout, counts, planes, level_ref, me, shape):
    first_count, second_count = counts

    def row(count, width, at):
        block = lax.broadcasted_iota(jnp.int32, (1, count * width), 1) // width
        value = jnp.zeros((1, count * width), jnp.float32)
        for i in range(count):
            value = jnp.where(block == i, level_ref[at(i)], value)
        return 6.0 + screen_base * (1.0 + value)

    if layout == 0:
        rows = [row(second_count, CY, lambda j: i * second_count + j) for i in range(first_count)]
        whole = jnp.concatenate([jnp.broadcast_to(value, (CX, shape[1])) for value in rows], axis=0)
        return lambda k: whole

    def along_x(k):
        i = jnp.clip(me * planes - 1 + k, 0, first_count * CX - 1) // CX
        column = jnp.broadcast_to(row(second_count, CY, lambda j: i * second_count + j), (128, shape[0])).T
        return jnp.concatenate([column] * (shape[1] // 128), axis=1)

    def along_y(k):
        j = jnp.clip(me * planes - 1 + k, 0, second_count * CY - 1) // CY
        return row(first_count, CX, lambda i: i * second_count + j)

    return along_x if layout == 2 else along_y


def fetch(pairs, sem_ref):
    copies = [pltpu.make_async_copy(source, held, sem_ref.at[i]) for i, (source, held) in enumerate(pairs)]
    for copy in copies:
        copy.start()
    return copies


def sweep_all(count, step_ref, source_ref, diagonal, matrix_ref, emit):
    matrix = wide(matrix_ref[...])
    for k in range(count):
        middle = step_ref[k + 1]
        remainder = remainder_of(source_ref[k + 1], step_ref[k], middle, step_ref[k + 2], diagonal(k + 1))
        high, low = parts_of(remainder, 2)
        row = jnp.concatenate([high, low, high], axis=1)
        step = lax.dot_general(row, matrix, (((1,), (1,)), ((), ())), preferred_element_type=jnp.float32)
        emit(k, middle + step)


def first_kernel(
    grid, level_ref, held_ref, first_any, second_any, sent_ref, source_ref, step_ref, first_ref, second_ref, sem_ref
):
    copies = fetch([(first_any, first_ref), (second_any, second_ref)], sem_ref)
    first_count, second_count, planes, per_target = grid
    for k in range(planes + 2):
        source_ref[k] = brick_planes(held_ref, first_count, second_count, planes + 2, k)
    copies[0].wait()
    first = wide(first_ref[...])
    for k in range(planes + 2):
        step_ref[k] = jnp.dot(first, parts_in_rows(source_ref[k]), preferred_element_type=jnp.float32)
    order = slab_order(first_count, second_count)
    block = sent_ref.shape[0] // len(order)

    def emit(k, value):
        last = sent_ref.shape[0] * 128 // (2 * planes * len(order) * value.shape[0]) - 1
        put(sent_ref, k, planes, order, block, [(0, 0, 1), (last + 2, last, 1), (last + 3, 1, last - 1)], source_ref[k + 1])
        put(sent_ref, k, planes, order, block, [(1, 0, last + 1)], value)

    copies[1].wait()
    diagonal = diagonals(0, grid[:2], planes, level_ref, 0, step_ref.shape[1:])
    sweep_all(planes, step_ref, source_ref, diagonal, second_ref, emit)


def later_kernel(
    shape, edge_ref, level_ref, held_ref, pair_ref, other_ref, first_any, second_any, *refs
):
    order, planes, rows, with_source, last, layout, counts = shape
    devices = len(order)
    *refs, first_ref, second_ref, sem_ref = refs
    copies = fetch([(first_any, first_ref), (second_any, second_ref)], sem_ref)
    even = edge_ref[2] > 0
    if with_source:
        sent_ref, source_ref, iterate_ref, step_ref = refs
    else:
        source_ref, sent_ref, iterate_ref, step_ref = refs
    bands = iterate_ref.shape[2] // 128
    block, edge_block = held_ref.shape[0] // devices, pair_ref.shape[0] // devices
    per_band = block // bands
    edge_band = edge_block // bands
    own = lambda place: pieces(held_ref, order, block, place * rows, rows, bands, per_band)

    def edge(after, k):
        pair, other = [pieces(ref, order, edge_block, k * rows, rows, bands, edge_band) for ref in (pair_ref, other_ref)]
        return jnp.where(even, pair, other) if after else jnp.where(even, other, pair)

    if with_source:
        for k in range(planes):
            source_ref[k + 1] = own(0 if k == 0 else planes + 1 if k == planes - 1 else planes + 1 + k)
        source_ref[0] = edge(False, 2)
        source_ref[planes + 1] = edge(True, 0)
    for k in range(2):
        iterate_ref[k] = edge(False, k)
        iterate_ref[planes + 2 + k] = edge(True, k + with_source)
    for k in range(planes):
        iterate_ref[k + 2] = own(k + with_source)
    diagonal = diagonals(layout, counts, planes, level_ref, edge_ref[3], step_ref.shape[1:])
    copies[0].wait()
    first = wide(first_ref[...])
    for k in range(planes + 2):
        middle = iterate_ref[k + 1]
        remainder = remainder_of(source_ref[k], iterate_ref[k], middle, iterate_ref[k + 2], diagonal(k))
        step = jnp.dot(first, parts_in_rows(remainder), preferred_element_type=jnp.float32)
        if k == 0:
            step = step * edge_ref[0].astype(jnp.float32)
        if k == planes + 1:
            step = step * edge_ref[1].astype(jnp.float32)
        step_ref[k] = middle + step

    def emit(k, value):
        if last:
            for j in range(value.shape[0] // CY):
                sent_ref[j, k] = value[j * CY : (j + 1) * CY, :]
        else:
            per_target = value.shape[1] // devices
            put(sent_ref, k, planes, order, sent_ref.shape[0] // devices, [(0, 0, per_target)], value)

    copies[1].wait()
    sweep_all(planes, step_ref, source_ref, diagonal, second_ref, emit)


ANY = pl.BlockSpec(memory_space=pl.ANY)
SMEM = pl.BlockSpec(memory_space=pltpu.SMEM)
VMEM = pl.BlockSpec(memory_space=pltpu.VMEM)
LIMIT = pltpu.CompilerParams(vmem_limit_bytes=20 << 20)


def matrix_scratch(first, second):
    return [pltpu.VMEM(matrix.shape, jnp.float32) for matrix in (first, second)] + [pltpu.SemaphoreType.DMA((2,))]


def first_phase(grid, levels, held, first, second):
    rows, columns = len(first), len(second)
    first_count, second_count, planes, per_target = grid
    return pl.pallas_call(
        functools.partial(first_kernel, grid),
        out_shape=(
            jax.ShapeDtypeStruct((2 * columns * planes * rows // 128, 128), jnp.float32),
            jax.ShapeDtypeStruct((planes + 2, rows, columns), jnp.float32),
        ),
        in_specs=[SMEM, VMEM] + [ANY] * 2,
        out_specs=(VMEM, VMEM),
        scratch_shapes=[pltpu.VMEM((planes + 2, rows, columns), jnp.float32)] + matrix_scratch(first, second),
        compiler_params=LIMIT,
        name="first_phase",
    )(levels, held, first, second)


def later_phase(
    order, planes, rows, layout, counts, edges, levels, held, pair, other, first, second, source=None, last=False
):
    columns = second.shape[1]
    length = len(order) * rows
    if last:
        sent = (length // CY, planes, CY, columns)
    else:
        sent = (columns * planes * length // 128, 128)
    out = [jax.ShapeDtypeStruct(sent, jnp.float32)]
    operands = [edges, levels, held, pair, other, first, second]
    if source is None:
        out.append(jax.ShapeDtypeStruct((planes + 2, length, columns), jnp.float32))
    else:
        operands.append(source)
    return pl.pallas_call(
        functools.partial(later_kernel, (order, planes, rows, source is None, last, layout, counts)),
        out_shape=tuple(out),
        in_specs=[SMEM] * 2 + [VMEM] * 3 + [ANY] * 2 + [VMEM] * (len(operands) - 7),
        out_specs=tuple([VMEM] * len(out)),
        scratch_shapes=[
            pltpu.VMEM((planes + 4, length, columns), jnp.float32),
            pltpu.VMEM((planes + 2, length, columns), jnp.float32),
        ]
        + matrix_scratch(first, second),
        compiler_params=LIMIT,
        name="later_phase",
    )(*operands)


def join_kernel(order, even_ref, source_ref, x_pair_ref, x_other_ref, y_pair_ref, y_other_ref, brick_ref, sent_ref, turned_ref):
    x_even, y_even = even_ref[0] > 0, even_ref[1] > 0
    y_before = jnp.where(y_even, y_other_ref[...], y_pair_ref[...])
    y_after = jnp.where(y_even, y_pair_ref[...], y_other_ref[...])
    for i in range(CX):
        here = slice(i * CY, (i + 1) * CY)
        value = source_ref[here, :]
        if i == 0:
            value = value + jnp.where(x_even, x_other_ref[...], x_pair_ref[...])
        if i == CX - 1:
            value = value + jnp.where(x_even, x_pair_ref[...], x_other_ref[...])
        row = rows_iota(CY, NZ)
        value = value + jnp.where(row == 0, y_before[i : i + 1, :], 0.0)
        brick_ref[here, :] = value + jnp.where(row == CY - 1, y_after[i : i + 1, :], 0.0)
    half = CX // 2
    planes = sent_ref.shape[1] // half
    turned_ref[:8, :] = jnp.zeros((8, 2 * CY), jnp.float32)
    turned_ref[NZ + 8 :, :] = jnp.zeros((8, 2 * CY), jnp.float32)
    for i in range(half):
        both = [brick_ref[j * CY : (j + 1) * CY, :] for j in (i, i + half)]
        turned_ref[8 : NZ + 8, :] = jnp.concatenate(both, axis=0).T
        for j, target in enumerate(order):
            first = 7 + j * (planes - 2)
            sent_ref[target, pl.ds(i, planes, stride=half), :] = turned_ref[first : first + planes, :]


def join(source, even, order, *faces):
    return pl.pallas_call(
        functools.partial(join_kernel, order),
        out_shape=(
            jax.ShapeDtypeStruct(source.shape, jnp.float32),
            jax.ShapeDtypeStruct((len(order), (NZ // len(order) + 2) * CX // 2, 2 * CY), jnp.float32),
        ),
        in_specs=[SMEM] + [VMEM] * 5,
        out_specs=(VMEM, VMEM),
        scratch_shapes=[pltpu.VMEM((NZ + 16, 2 * CY), jnp.float32)],
        compiler_params=LIMIT,
        name="join",
    )(even, source, *faces)


def slab_order(first_count, second_count):
    order = []
    for i in range(first_count):
        row = [i * second_count + j for j in range(second_count)]
        order += row if i % 2 == 0 else row[::-1]
    return order


def place_in_row(j):
    return jnp.where(lax.axis_index("bx") % 2 == 0, j, lax.axis_size("by") - 1 - j)


def beside(to_next, to_previous, even):
    order = slab_order(lax.axis_size("bx"), lax.axis_size("by"))
    got = []
    for start, value in ((1, jnp.where(even, to_previous, to_next)), (0, jnp.where(even, to_next, to_previous))):
        pairs = [(order[i], order[i + 1]) for i in range(start, len(order) - 1, 2)]
        got.append(lax.ppermute(value, EVERY, pairs + [(j, i) for i, j in pairs]))
    return got[::-1]


def exchange(value):
    return lax.all_to_all(value, EVERY, split_axis=0, concat_axis=0, tiled=True)


def of_row(value):
    second_count, mine = lax.axis_size("by"), lax.axis_index("by")
    held = jnp.zeros((second_count,) + value.shape, value.dtype)
    for turn in range(second_count):
        piece = value
        if turn:
            piece = lax.ppermute(value, "by", [(i, i ^ turn) for i in range(second_count)])
        held = lax.dynamic_update_slice_in_dim(held, piece[None], mine ^ turn, 0)
    return held


def x_slab_source(brick, even):
    second_count = lax.axis_size("by")
    mine = lax.axis_index("by")
    brick = brick.reshape(CX, CY, NZ)
    thick = CX // second_count
    slab = jnp.zeros((thick, second_count * CY, NZ), jnp.float32)
    for turn in range(second_count):
        partner = mine ^ turn
        piece = lax.dynamic_slice_in_dim(brick, place_in_row(partner) * thick, thick, 0)
        if turn:
            piece = lax.ppermute(piece, "by", [(i, i ^ turn) for i in range(second_count)])
        slab = lax.dynamic_update_slice_in_dim(slab, piece, partner * CY, 1)
    pair, other = beside(slab[-1:], slab[:1], even)
    return jnp.concatenate([jnp.where(even, other, pair), slab, jnp.where(even, pair, other)], axis=0)


def relax(brick, sent, cells, levels, rows_inverse, columns_inverse, depth_inverse):
    first_count, second_count = lax.axis_size("bx"), lax.axis_size("by")
    devices = first_count * second_count
    order = slab_order(first_count, second_count)
    me = lax.axis_index("bx") * second_count + place_in_row(lax.axis_index("by"))
    even = me % 2 == 0
    nx, ny = first_count * CX, second_count * CY
    thick = (NZ // devices, ny // devices, nx // devices)
    edges = jnp.stack([me > 0, me < devices - 1, even, me]).astype(jnp.int32)
    matrices = (rows_inverse, columns_inverse, depth_inverse)
    held = exchange(sent)
    sent, z_source = first_phase(
        (first_count, second_count, thick[0], thick[1]), levels, held.reshape(-1, 2 * CY), matrices[0], matrices[1]
    )
    sources = [z_source, None, None]
    for step in range(1, 3 * ITERS // 2):
        at = step % 3
        planes, rows = thick[at], thick[(at + 2) % 3]
        held = exchange(sent)
        if step == 1:
            held, sources[2], cells = lax.optimization_barrier((held, x_slab_source(brick, even), of_row(cells)))
        bands = matrices[(2 * step + 1) % 3].shape[1] // 128
        blocks = held.reshape(devices, bands, -1, 128)
        to_next, to_previous = blocks[:, :, -2 * rows :], blocks[:, :, : 2 * rows]
        if sources[at] is None:
            to_next, to_previous = blocks[:, :, (planes - 1) * rows : (planes + 2) * rows], blocks[:, :, : 3 * rows]
        pair, other = beside(to_next.reshape(-1, 128), to_previous.reshape(-1, 128), even)
        out = later_phase(
            order,
            planes,
            rows,
            at,
            (first_count, second_count),
            edges,
            levels,
            held,
            pair,
            other,
            matrices[2 * step % 3],
            matrices[(2 * step + 1) % 3],
            source=sources[at],
            last=step + 1 == 3 * ITERS // 2,
        )
        sent = out[0]
        if sources[at] is None:
            sources[at] = out[1]
    return sent, cells


def local(normals, owners, cells, levels, rows_inverse, columns_inverse, depth_inverse):
    bricks = lax.axis_size(EVERY)
    point_count = cells.shape[0]
    capacity = 2 * point_count // bricks
    chunks = bricks * capacity // 128
    send, slot = pack(owners, cells, normals, levels, bricks, capacity)
    held = exchange(send)
    levels = held[:, 4 * capacity // 128, 0]
    if not grouped(bricks, capacity):
        held = held[:, : 4 * capacity // 128].reshape(bricks, 4, capacity)
        held = held.transpose(1, 0, 2).reshape(4 * chunks, 128)
    even = jnp.stack([lax.axis_index("bx") % 2 == 0, lax.axis_index("by") % 2 == 0]).astype(jnp.int32)
    source, x_pair, x_other, y_pair, y_other, cells = splat(held, even, chunks)
    faces = swaps(x_pair, x_other, "bx") + swaps(y_pair, y_other, "by")
    brick, sent = join(source, even, slab_order(lax.axis_size("bx"), lax.axis_size("by")), *faces)
    slab, cells = relax(brick, sent, cells, levels, rows_inverse, columns_inverse, depth_inverse)
    bounds = cells[:, chunks : chunks + 2, : chunks // GROUP].astype(jnp.int32)
    second_count, thick = slab.shape[:2]
    pieces_of = slab.reshape(second_count * thick, CY, NZ)
    held = lax.all_to_all(pieces_of, "by", split_axis=0, concat_axis=0, tiled=True).reshape(slab.shape)
    place = place_in_row(lax.axis_index("by")).astype(jnp.int32).reshape(1)
    sampled = sample(place, bounds, cells, slab, chunks, bricks, capacity)
    if not grouped(bricks, capacity):
        sampled = sampled.reshape(second_count, bricks, capacity).transpose(1, 0, 2)
    sampled, held = lax.optimization_barrier((sampled, held))
    returned = exchange(sampled)
    iterate = jnp.where(lax.axis_index("bx") % 2 == 0, held, held[::-1]).reshape(CX, CY, NZ)
    if not grouped(bricks, capacity):
        returned = jnp.sum(returned.reshape(-1, second_count, second_count, capacity), axis=1).reshape(bricks, capacity)
    implicit = unpack(owners, slot, returned, second_count)
    return (iterate, implicit)


def solution(mesh):
    placed = (
        P(None, ("bx", "by")),
        P(("bx", "by"), None),
        P(("bx", "by")),
        P("bx", "by"),
        P(),
        P(),
        P(),
    )
    return jax.shard_map(
        local,
        mesh=mesh,
        in_specs=placed,
        out_specs=(P("bx", "by", None), P(("bx", "by"))),
        check_vma=False,
    )
```

```python
import functools

import jax
import jax.numpy as jnp
from jax import lax
from jax.experimental import pallas as pl
from jax.experimental.pallas import tpu as pltpu
from jax.sharding import PartitionSpec as P

CX = 16
CY = 64
NZ = 256
ITERS = 4
EVERY = ("bx", "by")


screen_base = 1.0


def parts_of(value, count):
    parts = []
    for _ in range(count):
        part = value.astype(jnp.bfloat16)
        parts.append(part)
        value = value - part.astype(jnp.float32)
    return parts


def rows_iota(rows, columns):
    return lax.broadcasted_iota(jnp.int32, (rows, columns), 0)


def flags(condition):
    return jnp.where(condition, 1.0, 0.0)


def whole_arrays(count):
    return [pl.BlockSpec(memory_space=pltpu.VMEM)] * count


def product(rows, columns):
    rows, columns = jnp.concatenate(rows, axis=1), jnp.concatenate(columns, axis=1)
    return lax.dot_general(rows, columns, (((1,), (1,)), ((), ())), preferred_element_type=jnp.float32)


def pack_kernel(
    level_ref, owner_any, cell_any, normal_any, send_ref, slot_ref, total_ref, owner_ref, cell_ref, normal_ref, sem_ref
):
    bricks, capacity = send_ref.shape[0], total_ref.shape[1]
    points = owner_ref.shape[1]
    block = 256
    copies = fetch([(owner_any, owner_ref), (cell_any, cell_ref), (normal_any, normal_ref)], sem_ref)
    earlier = rows_iota(block, block) < lax.broadcasted_iota(jnp.int32, (block, block), 1)
    total_ref[...] = jnp.zeros_like(total_ref)
    for copy in copies:
        copy.wait()

    def names(at):
        here = pl.ds(pl.multiple_of(at * block, block), block)
        named = flags(rows_iota(bricks, block) == owner_ref[:, here])
        x = cell_ref[:, here] >> 14
        return here, named, x, flags(rows_iota(CX, block) == x)

    def tally(named, x_hot):
        return product([x_hot.astype(jnp.bfloat16)], [named.astype(jnp.bfloat16)])

    def count(at, counts):
        _, named, _, x_hot = names(at)
        return counts + tally(named, x_hot)

    counts = lax.fori_loop(0, points // block, count, jnp.zeros((CX, bricks), jnp.float32), unroll=4)
    ahead, shift, shifts = jnp.zeros((1, bricks), jnp.float32), jnp.zeros((1, bricks), jnp.float32), []
    for i in range(CX):
        shift = jnp.maximum(shift, float(i * capacity // CX) - ahead)
        shifts.append(shift)
        ahead = ahead + counts[i : i + 1, :]
    shifts = jnp.concatenate(shifts, axis=0)

    def step(at, seen):
        here, named, x, x_hot = names(at)
        x_less = flags(rows_iota(CX, block) < x)
        own = jnp.dot(
            jnp.concatenate([counts, seen, shifts], axis=0).astype(jnp.bfloat16),
            named.astype(jnp.bfloat16),
            preferred_element_type=jnp.float32,
        )
        ahead = jnp.sum(x_less * own[:CX] + x_hot * own[CX : 2 * CX], axis=0, keepdims=True)
        used = jnp.sum(own[:CX], axis=0, keepdims=True)
        moved = jnp.minimum(jnp.sum(x_hot * own[2 * CX :], axis=0, keepdims=True), capacity - used)
        key = (owner_ref[:, here] * CX + x).astype(jnp.float32)
        column = jnp.broadcast_to(key, (128, block)).T
        same = (jnp.concatenate([column] * (block // 128), axis=1) == key) & earlier
        place = ahead + jnp.sum(flags(same), axis=0, keepdims=True) + moved
        slot_ref[:, here] = place
        slot = flags(rows_iota(capacity, block).astype(jnp.float32) == place).astype(jnp.bfloat16)
        values = []
        for k in range(3):
            values += [part.astype(jnp.float32) for part in parts_of(normal_ref[k : k + 1, here], 3)]
        cell = cell_ref[:, here] + 1
        for shift in (16, 8, 0):
            values.append(((cell >> shift) & 255).astype(jnp.float32))
        rows = jnp.concatenate([(named * value).astype(jnp.bfloat16) for value in values], axis=0)
        total_ref[...] += product([rows], [slot])
        return seen + tally(named, x_hot)

    lax.fori_loop(0, points // block, step, jnp.zeros((CX, bricks), jnp.float32), unroll=2)
    part = lambda i: total_ref[i * bricks : (i + 1) * bricks, :]
    fields = [part(3 * k) + part(3 * k + 1) + part(3 * k + 2) for k in range(3)]
    fields.append(part(9) * 65536.0 + part(10) * 256.0 + part(11))
    row = jnp.concatenate(fields, axis=1)
    used = row.shape[1] // 128
    for j in range(used):
        send_ref[:, j, :] = row[:, 128 * j : 128 * (j + 1)]
    level = jnp.full((bricks, send_ref.shape[1] - used, 128), level_ref[0, 0])
    send_ref[:, used:, :] = level.astype(jnp.float32)


def pack(owners, cells, normals, levels, bricks, capacity):
    points = cells.shape[0]
    return pl.pallas_call(
        pack_kernel,
        out_shape=(
            jax.ShapeDtypeStruct((bricks, 4 * capacity // 128 // 8 * 8 + 8, 128), jnp.float32),
            jax.ShapeDtypeStruct((1, points), jnp.float32),
        ),
        in_specs=[pl.BlockSpec(memory_space=pltpu.SMEM)] + [pl.BlockSpec(memory_space=pl.ANY)] * 3,
        out_specs=tuple(whole_arrays(2)),
        scratch_shapes=[
            pltpu.VMEM((12 * bricks, capacity), jnp.float32),
            pltpu.VMEM((1, points), jnp.int32),
            pltpu.VMEM((1, points), jnp.int32),
            pltpu.VMEM((3, points), jnp.float32),
            pltpu.SemaphoreType.DMA((3,)),
        ],
        compiler_params=pltpu.CompilerParams(vmem_limit_bytes=16 << 20),
        name="pack",
    )(levels, owners.reshape(1, points), cells.reshape(1, points), normals)


def unpack_kernel(second_count, owner_ref, rank_ref, held_ref, out_ref):
    bricks = held_ref.shape[0]
    points = owner_ref.shape[1]
    block = 512
    held = held_ref[...]
    if len(held.shape) == 3:
        halves = held.shape[1] // second_count
        rows = []
        for i in range(0, bricks, second_count):
            rows.append(sum([held_ref[i + j] for j in range(second_count)]))
        part = lambda row, half: row[half * second_count : (half + 1) * second_count, :]
        held = jnp.concatenate(
            [jnp.concatenate([part(row, half) for row in rows], axis=0) for half in range(halves)], axis=1
        )
    capacity = held.shape[1]
    held = jnp.concatenate([part.astype(jnp.float32).T for part in parts_of(held, 3)], axis=1)
    held = held.astype(jnp.bfloat16)
    for at in range(points // block):
        here = slice(at * block, (at + 1) * block)
        named = flags(rows_iota(bricks, block) == owner_ref[:, here]).astype(jnp.bfloat16)
        named = jnp.concatenate([named] * 3, axis=0)
        found = jnp.dot(held, named, preferred_element_type=jnp.float32)
        slot = rows_iota(capacity, block).astype(jnp.float32) == rank_ref[:, here]
        out_ref[:, here] = jnp.sum(jnp.where(slot, found, 0.0), axis=0, keepdims=True)


def unpack(owners, rank, held, second_count):
    points = owners.shape[0]
    out = pl.pallas_call(
        functools.partial(unpack_kernel, second_count),
        out_shape=jax.ShapeDtypeStruct((1, points), jnp.float32),
        in_specs=whole_arrays(3),
        out_specs=pl.BlockSpec(memory_space=pltpu.VMEM),
        compiler_params=pltpu.CompilerParams(vmem_limit_bytes=16 << 20),
        name="unpack",
    )(owners.reshape(1, points), rank, held)
    return out.reshape(points)


def spread(row):
    return jnp.broadcast_to(row, (16, 128)).astype(jnp.bfloat16)


def times_row(table, row16):
    rows = table.shape[0]
    return (table.reshape(rows // 16, 16, 128) * row16[None]).reshape(rows, 128)


def places(cell_row):
    cell = cell_row.astype(jnp.int32) - 1
    return cell >> 14, (cell >> 8) & (CY - 1), cell & (NZ - 1)


GROUP = 4
WINDOW = 4


def units_turned(tile):
    row = rows_iota(8, 128)
    unit = lax.broadcasted_iota(jnp.int32, (8, 128), 1) // 16
    for bit in (4, 2, 1):
        low, high = (row & bit) == 0, (unit & bit) != 0
        from_below = pltpu.roll(pltpu.roll(tile, 8 - bit, 0), 16 * bit, 1)
        from_above = pltpu.roll(pltpu.roll(tile, bit, 0), 128 - 16 * bit, 1)
        tile = jnp.where(low & high, from_below, jnp.where(low | high, tile, from_above))
    return tile


def grouped(bricks, capacity):
    return capacity % 128 == 0 and bricks % 8 == 0


def regroup(held_ref, field_ref):
    bricks = held_ref.shape[0]
    chunks = field_ref.shape[0] // 4
    halves, blocks = chunks // bricks, bricks // 8
    for k in range(4):
        for half in range(halves):
            for block in range(blocks):
                tile = held_ref[8 * block : 8 * (block + 1), halves * k + half, :]
                here = pl.ds(k * chunks + 8 * half * blocks + block, 8, stride=blocks)
                field_ref[here, :] = units_turned(tile)


def splat_kernel(
    even_ref,
    held_ref,
    source_ref,
    x_pair_ref,
    x_other_ref,
    y_pair_ref,
    y_other_ref,
    cell_ref,
    bound_ref,
    field_ref,
    sum_ref,
    column_ref,
):
    chunks = field_ref.shape[0] // 4
    points = 128 * GROUP
    if len(held_ref.shape) == 3:
        regroup(held_ref, field_ref)
    else:
        field_ref[...] = held_ref[...]
    cell_ref[:chunks, :] = field_ref[3 * chunks :, :]
    lane = lax.broadcasted_iota(jnp.int32, (8, 128), 1)
    bounds = jnp.zeros((8, 128), jnp.float32)
    for at in range(chunks // GROUP):
        cell = field_ref[3 * chunks + GROUP * at : 3 * chunks + GROUP * (at + 1), :]
        x = places(cell)[0].astype(jnp.float32)
        least, most = jnp.min(jnp.where(cell > 0, x, float(CX))), jnp.max(jnp.where(cell > 0, x, -1.0))
        bound_ref[at, 0], bound_ref[at, 1] = least.astype(jnp.int32), most.astype(jnp.int32)
        bounds = jnp.where(lane == at, jnp.where(rows_iota(8, 128) == 0, least, most), bounds)
    cell_ref[chunks:, :] = bounds
    sum_ref[...] = jnp.zeros_like(sum_ref)

    def group(at, carry):
        first, last = bound_ref[at, 0], bound_ref[at, 1]
        cells = []
        for member in range(GROUP):
            chunk = GROUP * at + member
            x, y, z = places(field_ref[pl.ds(3 * chunks + chunk, 1), :])
            z_hot = flags(rows_iota(NZ, 128) == z).astype(jnp.bfloat16)
            for k in range(3):
                parts = parts_of(field_ref[pl.ds(k * chunks + chunk, 1), :], 2)
                for j, part in enumerate(parts):
                    here = slice(j * points + 128 * member, j * points + 128 * (member + 1))
                    column_ref[k * NZ : (k + 1) * NZ, here] = times_row(z_hot, spread(part.astype(jnp.float32)))
            cells.append((x, flags(rows_iota(CY, 128) == y).astype(jnp.bfloat16)))

        def window(turn, carry):
            start = first + turn * WINDOW
            rows = []
            for x, y_hot in cells:
                hots = [spread(flags(x == start + i)) for i in range(WINDOW)]
                rows.append(jnp.concatenate([times_row(y_hot, hot) for hot in hots], axis=0))
            here = pl.ds(pl.multiple_of(start * CY, CY), WINDOW * CY)
            sum_ref[here, :] += product(rows * 2, [column_ref[...]])
            return carry

        window(0, 0)
        lax.fori_loop(1, jnp.maximum(last - first, 0) // WINDOW + 1, window, 0)
        return carry

    lax.fori_loop(0, chunks // GROUP, group, 0)
    row = rows_iota(CY, NZ)
    lane = lax.broadcasted_iota(jnp.int32, (CY, NZ), 1)

    def part(i, k):
        return sum_ref[i * CY : (i + 1) * CY, k * NZ : (k + 1) * NZ]

    for i in range(CX):
        y_part, z_part = part(i, 1), part(i, 2)
        value = jnp.where(row == CY - 1, 0.0, pltpu.roll(y_part, CY - 1, 0)) - jnp.where(row == 0, 0.0, pltpu.roll(y_part, 1, 0))
        value += jnp.where(lane == NZ - 1, 0.0, pltpu.roll(z_part, NZ - 1, 1)) - jnp.where(lane == 0, 0.0, pltpu.roll(z_part, 1, 1))
        if i < CX - 1:
            value += part(i + 1, 0)
        if i > 0:
            value -= part(i - 1, 0)
        source_ref[i * CY : (i + 1) * CY, :] = -0.5 * value
    before, after = -0.5 * part(0, 0), 0.5 * part(CX - 1, 0)
    x_pair_ref[...] = jnp.where(even_ref[0] > 0, after, before)
    x_other_ref[...] = jnp.where(even_ref[0] > 0, before, after)
    y_part = slice(NZ, 2 * NZ)
    before = -0.5 * jnp.concatenate([sum_ref[i * CY : i * CY + 1, y_part] for i in range(CX)], axis=0)
    after = 0.5 * jnp.concatenate([sum_ref[(i + 1) * CY - 1 : (i + 1) * CY, y_part] for i in range(CX)], axis=0)
    y_pair_ref[...] = jnp.where(even_ref[1] > 0, after, before)
    y_other_ref[...] = jnp.where(even_ref[1] > 0, before, after)


def splat(held, even, chunks):
    shapes = [(CX * CY, NZ), (CY, NZ), (CY, NZ), (CX, NZ), (CX, NZ), (chunks + 8, 128)]
    out = [jax.ShapeDtypeStruct(shape, jnp.float32) for shape in shapes]
    return pl.pallas_call(
        splat_kernel,
        out_shape=tuple(out),
        in_specs=[pl.BlockSpec(memory_space=pltpu.SMEM)] + whole_arrays(1),
        out_specs=tuple(whole_arrays(6)),
        scratch_shapes=[
            pltpu.SMEM((chunks // GROUP, 2), jnp.int32),
            pltpu.VMEM((4 * chunks, 128), jnp.float32),
            pltpu.VMEM(((CX + WINDOW) * CY, 3 * NZ), jnp.float32),
            pltpu.VMEM((3 * NZ, 2 * GROUP * 128), jnp.bfloat16),
        ],
        compiler_params=pltpu.CompilerParams(vmem_limit_bytes=16 << 20),
        name="splat",
    )(even, held)


def sample_kernel(place_ref, bound_ref, cell_ref, slab_ref, out_ref, turned_ref, sampled_ref):
    second_count, thick = slab_ref.shape[:2]
    chunks = sampled_ref.shape[1]
    columns = thick * CY
    start = place_ref[0] * thick
    for j in range(second_count):
        block = jnp.concatenate([slab_ref[j, i] for i in range(thick)], axis=0)
        high, low = parts_of(block.T, 2)
        turned_ref[:NZ, j * columns : (j + 1) * columns] = high
        turned_ref[NZ:, j * columns : (j + 1) * columns] = low
    sampled_ref[...] = jnp.zeros_like(sampled_ref)
    for j in range(second_count):

        def group(at, carry, j=j):
            @pl.when((bound_ref[j, 0, at] < start + thick) & (bound_ref[j, 1, at] >= start))
            def _():
                tables, heights = [], []
                for member in range(GROUP):
                    x, y, z = places(cell_ref[j, pl.ds(GROUP * at + member, 1), :])
                    y_hot = flags(rows_iota(CY, 128) == y).astype(jnp.bfloat16)
                    hots = [spread(flags(x == start + i)) for i in range(thick)]
                    tables.append(jnp.concatenate([times_row(y_hot, hot) for hot in hots], axis=0))
                    heights.append(z)
                level = rows_iota(NZ, 128 * GROUP) == jnp.concatenate(heights, axis=1)
                values = turned_ref[:, j * columns : (j + 1) * columns]
                found = jnp.dot(values, jnp.concatenate(tables, axis=1), preferred_element_type=jnp.float32)
                row = jnp.sum(jnp.where(level, found[:NZ] + found[NZ:], 0.0), axis=0, keepdims=True)
                for member in range(GROUP):
                    here = slice(128 * member, 128 * (member + 1))
                    sampled_ref[j, pl.ds(GROUP * at + member, 1), :] = row[:, here]

            return carry

        lax.fori_loop(0, chunks // GROUP, group, 0)
    if len(out_ref.shape) == 3 and out_ref.shape == sampled_ref.shape:
        out_ref[...] = sampled_ref[...]
        return
    bricks = out_ref.shape[0]
    blocks = bricks // 8
    for j in range(second_count):
        for half in range(chunks // bricks):
            for block in range(blocks):
                tile = sampled_ref[j, pl.ds(8 * half * blocks + block, 8, stride=blocks), :]
                out_ref[8 * block : 8 * (block + 1), half * second_count + j, :] = units_turned(tile)


def sample(place, bounds, cells, slab, chunks, bricks, capacity):
    second_count, thick = slab.shape[:2]
    shape = (second_count, chunks, 128)
    if grouped(bricks, capacity):
        shape = (bricks, second_count * capacity // 128, 128)
    return pl.pallas_call(
        sample_kernel,
        out_shape=jax.ShapeDtypeStruct(shape, jnp.float32),
        in_specs=[pl.BlockSpec(memory_space=pltpu.SMEM)] * 2 + whole_arrays(2),
        out_specs=pl.BlockSpec(memory_space=pltpu.VMEM),
        scratch_shapes=[
            pltpu.VMEM((2 * NZ, second_count * thick * CY), jnp.bfloat16),
            pltpu.VMEM((second_count, chunks, 128), jnp.float32),
        ],
        compiler_params=pltpu.CompilerParams(vmem_limit_bytes=16 << 20),
        cost_estimate=pl.CostEstimate(flops=8 << 30, bytes_accessed=4 << 20, transcendentals=0),
        name="sample",
    )(place, bounds, cells, slab)


def swaps(pair, other, axis):
    peers = lax.axis_size(axis)
    got = []
    for start, value in ((0, pair), (1, other)):
        pairs = [(i, i + 1) for i in range(start, peers - 1, 2)]
        got.append(lax.ppermute(value, axis, pairs + [(j, i) for i, j in pairs]))
    return got


def parts_in_rows(value):
    high, low = parts_of(value, 2)
    return jnp.concatenate([high, low, high], axis=0)


def wide(matrix):
    high, low = parts_of(matrix, 2)
    return jnp.concatenate([high, high, low], axis=1)


def shifted(value, axis, back):
    length = value.shape[axis]
    moved = pltpu.roll(value, length - 1 if back else 1, axis)
    index = lax.broadcasted_iota(jnp.int32, value.shape, axis)
    return jnp.where(index == (length - 1 if back else 0), 0.0, moved)


def remainder_of(source, before, middle, after, diagonal):
    beside = before + after
    beside = beside + shifted(middle, 0, False) + shifted(middle, 0, True)
    beside = beside + shifted(middle, 1, False) + shifted(middle, 1, True)
    return source - (diagonal * middle - beside)


def pieces(ref, order, per_source, start, rows, bands, per_band):
    columns = []
    for band in range(bands):
        starts = [i * per_source + band * per_band + start for i in order]
        columns.append(jnp.concatenate([ref[at : at + rows, :] for at in starts], axis=0))
    return jnp.concatenate(columns, axis=1)


def put(sent_ref, k, planes, order, per_block, runs, value):
    turned = value.T
    per_target = turned.shape[0] // len(order)
    for j, target in enumerate(order):
        for band in range(turned.shape[1] // 128):
            columns = slice(band * 128, (band + 1) * 128)
            start = target * per_block + band * (per_block * 128 // turned.shape[1]) + k
            for place, first, count in runs:
                if count:
                    part = turned[j * per_target + first : j * per_target + first + count, columns]
                    sent_ref[pl.ds(start + place * planes, count, stride=planes), :] = part


def brick_planes(ref, first_count, second_count, planes, k):
    bands = []
    lane = lax.broadcasted_iota(jnp.int32, (8, 128), 1)
    for i in range(first_count):
        tiles = []
        for j in range(second_count):
            start = ((i * second_count + j) * planes + k) * 8
            tiles.append(ref[start : start + 8, :])
        turned = [pltpu.roll(tile, 64, 1) for tile in tiles]
        pairs = range(0, second_count, 2)
        bands.append(jnp.concatenate([jnp.where(lane < 64, tiles[j], turned[j + 1]) for j in pairs], axis=1))
        bands.append(jnp.concatenate([jnp.where(lane < 64, turned[j], tiles[j + 1]) for j in pairs], axis=1))
    return jnp.concatenate(bands, axis=0)


def diagonals(layout, counts, planes, level_ref, me, shape):
    first_count, second_count = counts

    def row(count, width, at):
        block = lax.broadcasted_iota(jnp.int32, (1, count * width), 1) // width
        value = jnp.zeros((1, count * width), jnp.float32)
        for i in range(count):
            value = jnp.where(block == i, level_ref[at(i)], value)
        return 6.0 + screen_base * (1.0 + value)

    if layout == 0:
        rows = [row(second_count, CY, lambda j: i * second_count + j) for i in range(first_count)]
        whole = jnp.concatenate([jnp.broadcast_to(value, (CX, shape[1])) for value in rows], axis=0)
        return lambda k: whole

    def along_x(k):
        i = jnp.clip(me * planes - 1 + k, 0, first_count * CX - 1) // CX
        values = [6.0 + screen_base * (1.0 + level_ref[i * second_count + j]) for j in range(second_count)]
        return jnp.concatenate([jnp.full((CY, shape[1]), value) for value in values], axis=0)

    def along_y(k):
        j = jnp.clip(me * planes - 1 + k, 0, second_count * CY - 1) // CY
        return row(first_count, CX, lambda i: i * second_count + j)

    return along_x if layout == 2 else along_y


def fetch(pairs, sem_ref):
    copies = [pltpu.make_async_copy(source, held, sem_ref.at[i]) for i, (source, held) in enumerate(pairs)]
    for copy in copies:
        copy.start()
    return copies


def sweep_all(count, step_ref, source_ref, diagonal, matrix_ref, emit):
    matrix = wide(matrix_ref[...])
    for k in range(count):
        middle = step_ref[k + 1]
        remainder = remainder_of(source_ref[k + 1], step_ref[k], middle, step_ref[k + 2], diagonal(k + 1))
        high, low = parts_of(remainder, 2)
        row = jnp.concatenate([high, low, high], axis=1)
        step = lax.dot_general(row, matrix, (((1,), (1,)), ((), ())), preferred_element_type=jnp.float32)
        emit(k, middle + step)


def first_kernel(
    grid, level_ref, held_ref, first_any, second_any, sent_ref, source_ref, step_ref, first_ref, second_ref, sem_ref
):
    copies = fetch([(first_any, first_ref), (second_any, second_ref)], sem_ref)
    first_count, second_count, planes, per_target = grid
    for k in range(planes + 2):
        source_ref[k] = brick_planes(held_ref, first_count, second_count, planes + 2, k)
    copies[0].wait()
    first = wide(first_ref[...])
    for k in range(planes + 2):
        step_ref[k] = jnp.dot(first, parts_in_rows(source_ref[k]), preferred_element_type=jnp.float32)
    order = slab_order(first_count, second_count)
    block = sent_ref.shape[0] // len(order)

    def emit(k, value):
        last = sent_ref.shape[0] * 128 // (2 * planes * len(order) * value.shape[0]) - 1
        put(sent_ref, k, planes, order, block, [(0, 0, 1), (last + 2, last, 1), (last + 3, 1, last - 1)], source_ref[k + 1])
        put(sent_ref, k, planes, order, block, [(1, 0, last + 1)], value)

    copies[1].wait()
    diagonal = diagonals(0, grid[:2], planes, level_ref, 0, step_ref.shape[1:])
    sweep_all(planes, step_ref, source_ref, diagonal, second_ref, emit)


def later_kernel(
    shape, edge_ref, level_ref, held_ref, pair_ref, other_ref, first_any, second_any, *refs
):
    order, planes, rows, with_source, last, layout, counts = shape
    devices = len(order)
    *refs, first_ref, second_ref, sem_ref = refs
    copies = fetch([(first_any, first_ref), (second_any, second_ref)], sem_ref)
    even = edge_ref[2] > 0
    if with_source:
        sent_ref, source_ref, iterate_ref, step_ref = refs
    else:
        source_ref, sent_ref, iterate_ref, step_ref = refs
    bands = iterate_ref.shape[2] // 128
    block, edge_block = held_ref.shape[0] // devices, pair_ref.shape[0] // devices
    per_band = block // bands
    edge_band = edge_block // bands
    own = lambda place: pieces(held_ref, order, block, place * rows, rows, bands, per_band)

    def edge(after, k):
        pair, other = [pieces(ref, order, edge_block, k * rows, rows, bands, edge_band) for ref in (pair_ref, other_ref)]
        return jnp.where(even, pair, other) if after else jnp.where(even, other, pair)

    if with_source:
        for k in range(planes):
            source_ref[k + 1] = own(0 if k == 0 else planes + 1 if k == planes - 1 else planes + 1 + k)
        source_ref[0] = edge(False, 2)
        source_ref[planes + 1] = edge(True, 0)
    for k in range(2):
        iterate_ref[k] = edge(False, k)
        iterate_ref[planes + 2 + k] = edge(True, k + with_source)
    for k in range(planes):
        iterate_ref[k + 2] = own(k + with_source)
    diagonal = diagonals(layout, counts, planes, level_ref, edge_ref[3], step_ref.shape[1:])
    copies[0].wait()
    first = wide(first_ref[...])
    for k in range(planes + 2):
        middle = iterate_ref[k + 1]
        remainder = remainder_of(source_ref[k], iterate_ref[k], middle, iterate_ref[k + 2], diagonal(k))
        step = jnp.dot(first, parts_in_rows(remainder), preferred_element_type=jnp.float32)
        if k == 0:
            step = step * edge_ref[0].astype(jnp.float32)
        if k == planes + 1:
            step = step * edge_ref[1].astype(jnp.float32)
        step_ref[k] = middle + step

    def emit(k, value):
        if last:
            for j in range(value.shape[0] // CY):
                sent_ref[j, k] = value[j * CY : (j + 1) * CY, :]
        else:
            per_target = value.shape[1] // devices
            put(sent_ref, k, planes, order, sent_ref.shape[0] // devices, [(0, 0, per_target)], value)

    copies[1].wait()
    sweep_all(planes, step_ref, source_ref, diagonal, second_ref, emit)


ANY = pl.BlockSpec(memory_space=pl.ANY)
SMEM = pl.BlockSpec(memory_space=pltpu.SMEM)
VMEM = pl.BlockSpec(memory_space=pltpu.VMEM)
LIMIT = pltpu.CompilerParams(vmem_limit_bytes=20 << 20)


def matrix_scratch(first, second):
    return [pltpu.VMEM(matrix.shape, jnp.float32) for matrix in (first, second)] + [pltpu.SemaphoreType.DMA((2,))]


def first_phase(grid, levels, held, first, second):
    rows, columns = len(first), len(second)
    first_count, second_count, planes, per_target = grid
    return pl.pallas_call(
        functools.partial(first_kernel, grid),
        out_shape=(
            jax.ShapeDtypeStruct((2 * columns * planes * rows // 128, 128), jnp.float32),
            jax.ShapeDtypeStruct((planes + 2, rows, columns), jnp.float32),
        ),
        in_specs=[SMEM, VMEM] + [ANY] * 2,
        out_specs=(VMEM, VMEM),
        scratch_shapes=[pltpu.VMEM((planes + 2, rows, columns), jnp.float32)] + matrix_scratch(first, second),
        compiler_params=LIMIT,
        name="first_phase",
    )(levels, held, first, second)


def later_phase(
    order, planes, rows, layout, counts, edges, levels, held, pair, other, first, second, source=None, last=False
):
    columns = second.shape[1]
    length = len(order) * rows
    if last:
        sent = (length // CY, planes, CY, columns)
    else:
        sent = (columns * planes * length // 128, 128)
    out = [jax.ShapeDtypeStruct(sent, jnp.float32)]
    operands = [edges, levels, held, pair, other, first, second]
    if source is None:
        out.append(jax.ShapeDtypeStruct((planes + 2, length, columns), jnp.float32))
    else:
        operands.append(source)
    return pl.pallas_call(
        functools.partial(later_kernel, (order, planes, rows, source is None, last, layout, counts)),
        out_shape=tuple(out),
        in_specs=[SMEM] * 2 + [VMEM] * 3 + [ANY] * 2 + [VMEM] * (len(operands) - 7),
        out_specs=tuple([VMEM] * len(out)),
        scratch_shapes=[
            pltpu.VMEM((planes + 4, length, columns), jnp.float32),
            pltpu.VMEM((planes + 2, length, columns), jnp.float32),
        ]
        + matrix_scratch(first, second),
        compiler_params=LIMIT,
        name="later_phase",
    )(*operands)


def join_kernel(order, even_ref, source_ref, x_pair_ref, x_other_ref, y_pair_ref, y_other_ref, brick_ref, sent_ref, turned_ref):
    x_even, y_even = even_ref[0] > 0, even_ref[1] > 0
    y_before = jnp.where(y_even, y_other_ref[...], y_pair_ref[...])
    y_after = jnp.where(y_even, y_pair_ref[...], y_other_ref[...])
    for i in range(CX):
        here = slice(i * CY, (i + 1) * CY)
        value = source_ref[here, :]
        if i == 0:
            value = value + jnp.where(x_even, x_other_ref[...], x_pair_ref[...])
        if i == CX - 1:
            value = value + jnp.where(x_even, x_pair_ref[...], x_other_ref[...])
        row = rows_iota(CY, NZ)
        value = value + jnp.where(row == 0, y_before[i : i + 1, :], 0.0)
        brick_ref[here, :] = value + jnp.where(row == CY - 1, y_after[i : i + 1, :], 0.0)
    half = CX // 2
    planes = sent_ref.shape[1] // half
    turned_ref[:8, :] = jnp.zeros((8, 2 * CY), jnp.float32)
    turned_ref[NZ + 8 :, :] = jnp.zeros((8, 2 * CY), jnp.float32)
    for i in range(half):
        both = [brick_ref[j * CY : (j + 1) * CY, :] for j in (i, i + half)]
        turned_ref[8 : NZ + 8, :] = jnp.concatenate(both, axis=0).T
        for j, target in enumerate(order):
            first = 7 + j * (planes - 2)
            sent_ref[target, pl.ds(i, planes, stride=half), :] = turned_ref[first : first + planes, :]


def join(source, even, order, *faces):
    return pl.pallas_call(
        functools.partial(join_kernel, order),
        out_shape=(
            jax.ShapeDtypeStruct(source.shape, jnp.float32),
            jax.ShapeDtypeStruct((len(order), (NZ // len(order) + 2) * CX // 2, 2 * CY), jnp.float32),
        ),
        in_specs=[SMEM] + [VMEM] * 5,
        out_specs=(VMEM, VMEM),
        scratch_shapes=[pltpu.VMEM((NZ + 16, 2 * CY), jnp.float32)],
        compiler_params=LIMIT,
        name="join",
    )(even, source, *faces)


def slab_order(first_count, second_count):
    order = []
    for i in range(first_count):
        row = [i * second_count + j for j in range(second_count)]
        order += row if i % 2 == 0 else row[::-1]
    return order


def place_in_row(j):
    return jnp.where(lax.axis_index("bx") % 2 == 0, j, lax.axis_size("by") - 1 - j)


def beside(to_next, to_previous, even):
    order = slab_order(lax.axis_size("bx"), lax.axis_size("by"))
    got = []
    for start, value in ((1, jnp.where(even, to_previous, to_next)), (0, jnp.where(even, to_next, to_previous))):
        pairs = [(order[i], order[i + 1]) for i in range(start, len(order) - 1, 2)]
        got.append(lax.ppermute(value, EVERY, pairs + [(j, i) for i, j in pairs]))
    return got[::-1]


def exchange(value):
    return lax.all_to_all(value, EVERY, split_axis=0, concat_axis=0, tiled=True)


def of_row(value):
    second_count, mine = lax.axis_size("by"), lax.axis_index("by")
    held = jnp.zeros((second_count,) + value.shape, value.dtype)
    for turn in range(second_count):
        piece = value
        if turn:
            piece = lax.ppermute(value, "by", [(i, i ^ turn) for i in range(second_count)])
        held = lax.dynamic_update_slice_in_dim(held, piece[None], mine ^ turn, 0)
    return held


def x_slab_source(brick, even):
    second_count = lax.axis_size("by")
    mine = lax.axis_index("by")
    brick = brick.reshape(CX, CY, NZ)
    thick = CX // second_count
    slab = jnp.zeros((thick, second_count * CY, NZ), jnp.float32)
    for turn in range(second_count):
        partner = mine ^ turn
        piece = lax.dynamic_slice_in_dim(brick, place_in_row(partner) * thick, thick, 0)
        if turn:
            piece = lax.ppermute(piece, "by", [(i, i ^ turn) for i in range(second_count)])
        slab = lax.dynamic_update_slice_in_dim(slab, piece, partner * CY, 1)
    pair, other = beside(slab[-1:], slab[:1], even)
    return jnp.concatenate([jnp.where(even, other, pair), slab, jnp.where(even, pair, other)], axis=0)


def relax(brick, sent, cells, levels, rows_inverse, columns_inverse, depth_inverse):
    first_count, second_count = lax.axis_size("bx"), lax.axis_size("by")
    devices = first_count * second_count
    order = slab_order(first_count, second_count)
    me = lax.axis_index("bx") * second_count + place_in_row(lax.axis_index("by"))
    even = me % 2 == 0
    nx, ny = first_count * CX, second_count * CY
    thick = (NZ // devices, ny // devices, nx // devices)
    edges = jnp.stack([me > 0, me < devices - 1, even, me]).astype(jnp.int32)
    matrices = (rows_inverse, columns_inverse, depth_inverse)
    held = exchange(sent)
    sent, z_source = first_phase(
        (first_count, second_count, thick[0], thick[1]), levels, held.reshape(-1, 2 * CY), matrices[0], matrices[1]
    )
    sources = [z_source, None, None]
    for step in range(1, 3 * ITERS // 2):
        at = step % 3
        planes, rows = thick[at], thick[(at + 2) % 3]
        held = exchange(sent)
        if step == 1:
            held, sources[2], cells = lax.optimization_barrier((held, x_slab_source(brick, even), of_row(cells)))
        bands = matrices[(2 * step + 1) % 3].shape[1] // 128
        blocks = held.reshape(devices, bands, -1, 128)
        to_next, to_previous = blocks[:, :, -2 * rows :], blocks[:, :, : 2 * rows]
        if sources[at] is None:
            to_next, to_previous = blocks[:, :, (planes - 1) * rows : (planes + 2) * rows], blocks[:, :, : 3 * rows]
        pair, other = beside(to_next.reshape(-1, 128), to_previous.reshape(-1, 128), even)
        out = later_phase(
            order,
            planes,
            rows,
            at,
            (first_count, second_count),
            edges,
            levels,
            held,
            pair,
            other,
            matrices[2 * step % 3],
            matrices[(2 * step + 1) % 3],
            source=sources[at],
            last=step + 1 == 3 * ITERS // 2,
        )
        sent = out[0]
        if sources[at] is None:
            sources[at] = out[1]
    return sent, cells


def local(normals, owners, cells, levels, rows_inverse, columns_inverse, depth_inverse):
    bricks = lax.axis_size(EVERY)
    point_count = cells.shape[0]
    capacity = 2 * point_count // bricks
    chunks = bricks * capacity // 128
    send, slot = pack(owners, cells, normals, levels, bricks, capacity)
    held = exchange(send)
    levels = held[:, 4 * capacity // 128, 0]
    if not grouped(bricks, capacity):
        held = held[:, : 4 * capacity // 128].reshape(bricks, 4, capacity)
        held = held.transpose(1, 0, 2).reshape(4 * chunks, 128)
    even = jnp.stack([lax.axis_index("bx") % 2 == 0, lax.axis_index("by") % 2 == 0]).astype(jnp.int32)
    source, x_pair, x_other, y_pair, y_other, cells = splat(held, even, chunks)
    faces = swaps(x_pair, x_other, "bx") + swaps(y_pair, y_other, "by")
    brick, sent = join(source, even, slab_order(lax.axis_size("bx"), lax.axis_size("by")), *faces)
    slab, cells = relax(brick, sent, cells, levels, rows_inverse, columns_inverse, depth_inverse)
    bounds = cells[:, chunks : chunks + 2, : chunks // GROUP].astype(jnp.int32)
    second_count, thick = slab.shape[:2]
    pieces_of = slab.reshape(second_count * thick, CY, NZ)
    held = lax.all_to_all(pieces_of, "by", split_axis=0, concat_axis=0, tiled=True).reshape(slab.shape)
    place = place_in_row(lax.axis_index("by")).astype(jnp.int32).reshape(1)
    sampled = sample(place, bounds, cells, slab, chunks, bricks, capacity)
    if not grouped(bricks, capacity):
        sampled = sampled.reshape(second_count, bricks, capacity).transpose(1, 0, 2)
    sampled, held = lax.optimization_barrier((sampled, held))
    returned = exchange(sampled)
    iterate = jnp.where(lax.axis_index("bx") % 2 == 0, held, held[::-1]).reshape(CX, CY, NZ)
    if not grouped(bricks, capacity):
        returned = jnp.sum(returned.reshape(-1, second_count, second_count, capacity), axis=1).reshape(bricks, capacity)
    implicit = unpack(owners, slot, returned, second_count)
    return (iterate, implicit)


def solution(mesh):
    placed = (
        P(None, ("bx", "by")),
        P(("bx", "by"), None),
        P(("bx", "by")),
        P("bx", "by"),
        P(),
        P(),
        P(),
    )
    return jax.shard_map(
        local,
        mesh=mesh,
        in_specs=placed,
        out_specs=(P("bx", "by", None), P(("bx", "by"))),
        check_vma=False,
    )
```
